32 devices in a mesh: section: 2 (over core), wide: 16 (over z, y, x).
Axes of the slice: x: 2, y: 2, z: 4, core: 2. Of those that a mesh axis runs over, the one named last changes fastest.
Arguments:
- fields: bfloat16 [8, 1024, 512], P(None, 'wide'), may hold values from -6 to 6
- pixel_mask: int32 [8, 1024, 128], P(None, 'wide'), may hold values from 0 to 1
- channel_counts: int32 [8, 8], replicated, may hold values from 1 to 4, as said below
- kernels: bfloat16 [2, 1600], P('section'), may hold values from -0.625 to 0.625
- enc_bias: float32 [16], replicated, may hold values from -3 to 3
- dec_bias: float32 [4], replicated, may hold values from -3 to 3
- cotangent: bfloat16 [8, 1024, 512], P(None, 'wide'), may hold values from -6 to 6
- run_mean: float32 [16], replicated, may hold values from -4 to 4
- run_cov: float32 [16, 16], replicated, may hold values from -4 to 4
Outputs:
- pixels_out: bfloat16 [2, 8, 1024, 512], P('section', None, 'wide')
- kernel_grads: float32 [2, 1600], P('section')
- enc_bias_grad: float32 [16], replicated
- dec_bias_grad: float32 [4], replicated
- new_mean: float32 [16], replicated
- new_cov: float32 [16, 16], replicated
The draws below stay inside these ranges and needn't reach their ends.
Inputs may be any that keep to these rules, and one draw needn't show every extreme that they name: `channel_counts`: each is 1, 2 or 4; within a micro-batch the counts never fall from one field to the next.
All inputs are finite; a program needn't handle non-finite values.
Results may differ from the reference program's by a relative error of at most 0.0058.
Values may be sent and summed in bfloat16 or wider, within the bound.
No kernel may reach another device: no remote copies, remote signals or barrier semaphores. Data moves between devices by JAX's collectives and lax.ppermute only.
A program may use at most 192 MiB of HBM per device.

```python
import jax
import jax.numpy as jnp
from jax import lax

CIN = 4
CCODE = 16
KS = 5
HW = 128
MICRO = 8
ROWS = 1024
FIELDS_MB = 8
N_SECTION = 2


def draw_fields(key, part):
    key = jax.random.fold_in(key, 11)
    place = jnp.arange(MICRO, dtype=jnp.float32)
    level = 1.0 + place % 2.0 + place / (MICRO - 1)
    values = jax.random.normal(key, (MICRO, ROWS, CIN * HW), jnp.float32) * level[:, None, None]
    return jnp.clip(values, -6.0, 6.0).astype(jnp.bfloat16)


def draw_pixel_mask(key, part):
    key = jax.random.fold_in(key, 23)
    ticket = jax.random.randint(key, (MICRO, ROWS, HW), 0, 4 * ROWS)
    limit = ROWS + 2 * jnp.arange(ROWS, dtype=jnp.int32)
    return (ticket < limit[None, :, None]).astype(jnp.int32)


def draw_channel_counts(key, part):
    key = jax.random.fold_in(key, 37)
    key_level, key_low, key_step = jax.random.split(key, 3)
    level = jax.random.randint(key_level, (MICRO, FIELDS_MB), 0, 3)
    low_micro = jax.random.randint(key_low, (), 0, MICRO)
    high_micro = (low_micro + jax.random.randint(key_step, (), 1, MICRO)) % MICRO
    level = level.at[low_micro, 0].set(0).at[high_micro, FIELDS_MB - 1].set(2)
    level = jnp.sort(level, axis=1)
    return jnp.where(level == 0, 1, jnp.where(level == 1, 2, 4)).astype(jnp.int32)


def block_levels(key, extent, cuts, least, top_value):
    def one(dim, parts):
        heights = jax.random.uniform(jax.random.fold_in(jax.random.fold_in(key, 6), dim), (parts,), jnp.float32, least / len(cuts), top_value / len(cuts))
        return jnp.repeat(jnp.exp(heights), extent[dim] // parts).reshape((-1,) + (1,) * (len(extent) - dim - 1))

    loudness = one(*cuts[0])
    for cut in cuts[1:]:
        loudness = loudness * one(*cut)
    return loudness


def gaussian(rng, shape, width, most, pieces=(), kind=jnp.bfloat16):
    values = jax.random.normal(rng, shape, jnp.float32) * width
    if len(pieces) > 0:
        values = block_levels(rng, shape, pieces, -0.22, 0.18) * values
    return jnp.clip(values, min=-most, max=most).astype(kind)


def setup_inputs(seed: int = 0) -> dict:
    key_list = jax.random.split(jax.random.key(seed), 10)
    fields = draw_fields(jax.random.fold_in(key_list[9], 71), 0)
    pixel_mask = draw_pixel_mask(jax.random.fold_in(key_list[9], 71), 0)
    channel_counts = draw_channel_counts(jax.random.fold_in(key_list[9], 71), 0)
    kernels = gaussian(key_list[3], (N_SECTION, CCODE * CIN * KS * KS), (CIN * KS * KS) ** -0.5, 0.625, ((0, 2),))
    enc_bias = gaussian(key_list[4], (CCODE,), 0.5, 3.0, (), jnp.float32)
    dec_bias = gaussian(key_list[5], (CIN,), 0.5, 3.0, (), jnp.float32)
    cotangent = gaussian(key_list[6], (MICRO, ROWS, CIN * HW), 1.0, 6.0, ((1, 16),))
    run_mean = gaussian(key_list[7], (CCODE,), 1.0, 4.0, (), jnp.float32)
    run_cov = gaussian(key_list[8], (CCODE, CCODE), 1.0, 4.0, (), jnp.float32)
    return dict(fields=fields, pixel_mask=pixel_mask, channel_counts=channel_counts, kernels=kernels, enc_bias=enc_bias, dec_bias=dec_bias, cotangent=cotangent, run_mean=run_mean, run_cov=run_cov)


decay_rate = 0.9
whiten_weight = 0.25

@jax.custom_vjp
def low(v):
    return lax.optimization_barrier(v.astype(jnp.bfloat16)).astype(jnp.float32)

@jax.custom_vjp
def low_back(v):
    return v

def low_keep(v):
    return (low(v), None)

def low_pass(kept, grad):
    return (grad,)

def back_keep(v):
    return (v, None)

def back_low(kept, grad):
    return (low(grad),)
low.defvjp(low_keep, low_pass)
low_back.defvjp(back_keep, back_low)

def reference(fields, pixel_mask, channel_counts, kernels, enc_bias, dec_bias, cotangent, run_mean, run_cov):
    field_total = MICRO * FIELDS_MB

    def to_grid(array, depth):
        return array.reshape(MICRO, FIELDS_MB, HW, depth, HW).transpose(0, 1, 3, 2, 4).reshape(field_total, depth, HW, HW)

    def from_grid(array, depth):
        return array.reshape(MICRO, FIELDS_MB, depth, HW, HW).transpose(0, 1, 3, 2, 4).reshape(MICRO, FIELDS_MB * HW, depth * HW)
    pixel_valid = pixel_mask.astype(jnp.float32).reshape(field_total, HW, HW)
    chan_valid = (jnp.arange(CIN)[None, :] < channel_counts.reshape(field_total)[:, None]).astype(jnp.float32)
    input_mask = chan_valid[:, :, None, None] * pixel_valid[:, None, :, :]
    code_mask = pixel_valid[:, ::2, ::2]
    count = jnp.sum(code_mask)

    def forward(inputs, kernel_pair, enc_b, dec_b):
        kernel_stack = kernel_pair.reshape(2, CCODE, CIN, KS, KS)
        preact = lax.conv_general_dilated(inputs * input_mask, kernel_stack[0], (2, 2), ((2, 2), (2, 2)), dimension_numbers=('NCHW', 'OIHW', 'NCHW'), precision=lax.Precision.HIGHEST) + enc_b[None, :, None, None]
        preact = low_back(preact)
        codes = low(jax.nn.elu(preact))
        weighted = codes * code_mask[:, None, :, :]
        mean = lax.optimization_barrier(jnp.sum(weighted, axis=(0, 2, 3))) / count
        second = jnp.einsum('nchw,ndhw->cd', weighted, codes, precision=lax.Precision.HIGHEST) / count
        cov = second - jnp.outer(mean, mean)
        offset = cov - jnp.eye(CCODE, dtype=jnp.float32)
        penalty = 0.5 * whiten_weight * count * (jnp.sum(offset * offset) + jnp.sum(mean * mean))
        sent = low_back(codes)
        flipped = kernel_stack[1][:, :, ::-1, ::-1]
        rawact = lax.conv_general_dilated(sent, flipped, (1, 1), ((2, 3), (2, 3)), lhs_dilation=(2, 2), dimension_numbers=('NCHW', 'IOHW', 'NCHW'), precision=lax.Precision.HIGHEST) + dec_b[None, :, None, None]
        rawact = low_back(rawact)
        recon = jax.nn.elu(rawact) * input_mask
        return ((recon, penalty), (mean, cov))
    inputs = to_grid(fields.astype(jnp.float32), CIN)
    outputs, pullback, stats = jax.vjp(forward, inputs, kernels.astype(jnp.float32), enc_bias, dec_bias, has_aux=True)
    grads = pullback((to_grid(cotangent.astype(jnp.float32), CIN), jnp.ones((), jnp.float32)))
    pixels_out = jnp.stack([from_grid(grads[0], CIN), from_grid(outputs[0], CIN)]).astype(jnp.bfloat16)
    mean, cov = stats
    new_mean = decay_rate * run_mean + (1.0 - decay_rate) * mean
    new_cov = decay_rate * run_cov + (1.0 - decay_rate) * cov
    return (pixels_out, grads[1], grads[2], grads[3], new_mean, new_cov)
```

```python
import jax
import jax.numpy as jnp
from jax import lax
from jax.experimental import pallas as pl
from jax.experimental.pallas import tpu as pltpu
from jax.sharding import PartitionSpec as P

CIN = 4
CCODE = 16
KS = 5
HW = 128

UW = 16
NB = 5
HALO = 8
NK = CCODE * CIN * KS * KS

decay_rate = 0.9
whiten_weight = 0.25

F32 = jnp.float32
BF16 = jnp.bfloat16


def iota(shape, dim):
    return lax.broadcasted_iota(jnp.int32, shape, dim)


def hot(mask):
    return jnp.where(mask, 1.0, 0.0).astype(BF16)


def dot(a, b, dims=((1,), (0,))):
    return lax.dot_general(a, b, (dims, ((), ())), preferred_element_type=F32)


def fold(x, steps):
    for step in steps:
        x = x + pltpu.roll(x, step, 1)
    return x


def split(x):
    high = x.astype(BF16)
    rest = x - high.astype(F32)
    mid = rest.astype(BF16)
    return high, mid, (rest - mid.astype(F32)).astype(BF16)


class Sizes:
    def __init__(self, fields, sections):
        self.micro, self.band, self.span = fields
        self.sections = sections
        self.mb = self.micro // sections
        self.jf = self.band // 2 + HALO // 2
        self.rows = self.jf * self.mb
        self.own = self.mb * self.band
        self.halo = self.mb * HALO
        self.shift = self.mb.bit_length() - 1
        self.frame = NB * self.rows


def tap_target(n):
    o = (n * 5243) >> 19
    t = n - 100 * o
    c = (t * 1311) >> 15
    t = t - 25 * c
    k = (t * 205) >> 10
    l = t - 5 * k
    return (3 * k + (l >> 1)) * 8 + 2 * c + (l & 1), o


def tap_onehot():
    target, _ = tap_target(iota((1, NK), 1))
    return hot(iota((128, NK), 0) == target)


def gather_rows(z, odd):
    row = iota((2 * z.rows, 1), 0)
    parity = (row >= z.rows).astype(jnp.int32)
    q = row - parity * z.rows
    j = (q >> z.shift) - odd * (HALO // 2)
    m = q & (z.mb - 1)
    r = 2 * j + parity
    halo = z.own + m * HALO
    target = jnp.where(
        r < 0, halo + r + HALO, jnp.where(r >= z.band, halo + r - z.band, m * z.band + r)
    )
    return hot(iota((2 * z.rows, z.own + z.halo), 1) == target)


def scatter_rows(z, odd):
    row = iota((z.own, 1), 0)
    band_shift = z.band.bit_length() - 1
    m = row >> band_shift
    r = row & (z.band - 1)
    target = (r & 1) * z.rows + ((r >> 1) + odd * (HALO // 2)) * z.mb + m
    return hot(iota((z.own, 2 * z.rows), 1) == target)


def pixel_target(lane, inner):
    u_local = (lane >> 3) & (UW - 1)
    u = (lane >> 7) * (UW - 2) + u_local - 1
    valid = (u >= 0) & (u < HW // 2)
    if inner:
        valid = valid & (u_local >= 1) & (u_local <= UW - 2)
    return 2 * u + (lane & 1), (lane >> 1) & 3, valid


def window_columns():
    col, c, valid = pixel_target(iota((1, NB * 128), 1), False)
    target = jnp.where(valid, c * HW + col, -1)
    return hot(iota((CIN * HW, NB * 128), 0) == target)


def unwindow_columns():
    col, c, valid = pixel_target(iota((NB * 128, 1), 0), True)
    target = jnp.where(valid, c * HW + col, -1)
    return hot(iota((NB * 128, CIN * HW), 1) == target)


def window_mask_columns():
    col, _, valid = pixel_target(iota((1, NB * 128), 1), False)
    return hot(iota((HW, NB * 128), 0) == jnp.where(valid, col, -1))


def code_mask_columns():
    lane = iota((1, NB * 256), 1)
    u_local = (lane >> 4) & (UW - 1)
    u = (lane >> 8) * (UW - 2) + u_local - 1
    valid = (u_local >= 1) & (u_local <= UW - 2) & (u < HW // 2)
    return hot(iota((HW, NB * 256), 0) == jnp.where(valid, 2 * u, -1))


def own_rows(z, odd):
    j = (iota((z.rows, 1), 0) >> z.shift) - odd * (HALO // 2)
    return (j >= 0) & (j < z.band // 2)


def mend_coarse(blocks):
    last = HW // 2 - (NB - 1) * (UW - 2)
    rows = blocks[0].shape[0]
    lane = iota((rows, 128), 1)
    halves = [(x[:, :128], x[:, 128:]) for x in blocks]
    done = []
    for b, (low, high) in enumerate(halves):
        before = pltpu.roll(halves[b - 1][1], 32, 1) if b else 0.0
        new_low = jnp.where(lane < 16, before, low)
        if b + 1 < NB:
            after = pltpu.roll(halves[b + 1][0], 96, 1)
            new_high = jnp.where(lane >= 112, after, high)
        else:
            new_high = jnp.where(lane < (last + 1) * 16 - 128, high, 0.0)
        done.append((new_low, new_high))
    return done


def mend_fine(halves):
    rows = halves[0][0].shape[0]
    lane = iota((rows, 128), 1)
    done = []
    for b in range(NB):
        pair = []
        for h in range(2):
            x = halves[b][h]
            before = pltpu.roll(halves[b - 1][h], 16, 1) if b else 0.0
            after = pltpu.roll(halves[b + 1][h], 112, 1) if b + 1 < NB else 0.0
            x = jnp.where(lane < 8, before, x)
            pair.append(jnp.where(lane >= 120, after, x))
        done.append(tuple(pair))
    return done


def put_frame(z, sh, halves):
    zeros = jnp.zeros((NB, 8, 256), F32)
    sh[:, 0:8, :] = zeros
    sh[:, 8 + z.rows : 16 + z.rows, :] = zeros
    for b, (low, high) in enumerate(halves):
        sh[b, 8 : 8 + z.rows, 0:128] = low
        sh[b, 8 : 8 + z.rows, 128:256] = high


def fine_taps(z, sh, b):
    up = sh[b, 8 - z.mb : 8 - z.mb + z.rows, :]
    here = sh[b, 8 : 8 + z.rows, :]
    down = sh[b, 8 + z.mb : 8 + z.mb + z.rows, 0:128]
    return jnp.concatenate([up, here, down], axis=1).astype(BF16)


def coarse_taps(z, sh, b):
    down = sh[b, 8 + z.mb : 8 + z.mb + z.rows, :]
    here = sh[b, 8 : 8 + z.rows, :]
    up = sh[b, 8 - z.mb : 8 - z.mb + z.rows, :]
    return [x.astype(BF16) for x in (down, here, up)]


def spread(z, sh, weights):
    taps = [coarse_taps(z, sh, b) for b in range(NB)]
    down, here, up = (jnp.concatenate([t[i] for t in taps], axis=0) for i in range(3))
    nt = ((1,), (1,))
    out = dot(down, weights[0:256], nt) + dot(here, weights[256:512], nt)
    extra = dot(up, weights[512:640], nt)
    return out[:, :128] + extra, out[:, 128:]


def pick_taps(grads):
    lane = iota((CCODE, 128), 1)
    place = lane >> 3
    kept = jnp.zeros((CCODE, 128), F32)
    for k in range(KS):
        for shift in (-1, 0, 1):
            total = jnp.zeros((CCODE, 128), F32)
            for u in range(1, UW - 1):
                part = grads[u * 16 : u * 16 + 16, k * 128 : k * 128 + 128]
                total = jnp.where(place == u + shift, part, total)
            total = fold(total, (64, 32, 16, 8))
            kept = jnp.where(place == 3 * k + shift + 1, total, kept)
    return kept


def to_pixels(z, odd, low, high):
    rows = z.rows
    flat = [
        jnp.concatenate([h[b * rows : b * rows + rows].astype(BF16) for b in range(NB)], axis=1)
        for h in (low, high)
    ]
    native = dot(jnp.concatenate(flat, axis=0), unwindow_columns()).astype(BF16)
    return dot(scatter_rows(z, odd), native).astype(BF16)


def build_weights(kernel_pair, out_ref):
    row = iota((2 * CCODE, NK), 0)
    _, o = tap_target(iota((1, NK), 1))
    values = jnp.where(row < CCODE, kernel_pair[0], kernel_pair[1])
    spreaded = jnp.where((row & (CCODE - 1)) == o, values, 0.0).astype(BF16)
    taps = dot(tap_onehot(), spreaded, ((1,), (1,))).astype(BF16)
    lane = iota((2 * CCODE, 512), 1)
    repeat = hot(iota((2 * CCODE, 512), 0) == ((lane >> 8) * CCODE + (lane & 15)))
    wide_taps = dot(taps, repeat)
    row_u = iota((128, 256), 0) >> 3
    lane_u = iota((128, 256), 1) >> 4
    for which in range(2):
        for k in range(KS):
            total = jnp.zeros((128, 256), F32)
            for shift in (-1, 0, 1):
                q = 3 * k + shift + 1
                piece = wide_taps[8 * q : 8 * q + 8, 256 * which : 256 * which + 256]
                piece = jnp.broadcast_to(piece[None], (16, 8, 256)).reshape(128, 256)
                total = jnp.where(row_u == lane_u + shift, piece, total)
            out_ref[which, k * 128 : k * 128 + 128, :] = total.astype(BF16)


def encode_kernel(
    z, fields, mask, halo, kernel_own, kernel_other, enc_bias, counts,
    taps_out, code_out, slope_out, inmask_out, codemask_out, weights_out, pay_out,
    field_buf, mask_buf, sh, sems,
):
    section = lax.axis_index("section")
    wide = lax.axis_index("wide")
    odd = lax.rem(wide, 2)
    first = section * z.mb
    field_copy = pltpu.make_async_copy(fields.at[pl.ds(first, z.mb)], field_buf, sems.at[0])
    mask_copy = pltpu.make_async_copy(mask.at[pl.ds(first, z.mb)], mask_buf, sems.at[1])
    field_copy.start()
    mask_copy.start()
    mine, other = kernel_own[...].astype(F32), kernel_other[...].astype(F32)
    leads = section == 0
    build_weights(
        (jnp.where(leads, mine, other), jnp.where(leads, other, mine)), weights_out
    )
    gather = gather_rows(z, odd)
    rows = z.rows
    mask_copy.wait()
    pixel_mask = jnp.concatenate(
        [
            mask_buf[...].astype(F32).astype(BF16).reshape(z.own, HW),
            halo[:, 2 * z.span : 2 * z.span + HW],
        ],
        axis=0,
    )
    framed_mask = dot(gather, pixel_mask).astype(BF16)
    in_mask = dot(framed_mask, window_mask_columns())
    code_mask = dot(framed_mask[0:rows], code_mask_columns())
    field_now = wide * z.band // HW
    micro = iota((rows, 128), 0) & (z.mb - 1)
    count = jnp.zeros((rows, 128), jnp.int32)
    for m in range(z.mb):
        count = jnp.where(micro == m, counts[first + m, field_now], count)
    channel_ok = ((iota((rows, 128), 1) >> 1) & 3) < count
    field_copy.wait()
    pixels = jnp.concatenate(
        [field_buf[...].reshape(z.own, z.span), halo[:, 0 : z.span]], axis=0
    )
    windowed = dot(dot(gather, pixels).astype(BF16), window_columns())
    halves = []
    for b in range(NB):
        pair = []
        for h in range(2):
            rs, cs = slice(h * rows, h * rows + rows), slice(b * 128, b * 128 + 128)
            allowed = jnp.where(channel_ok, in_mask[rs, cs], 0.0)
            inmask_out[b, :, h * 128 : h * 128 + 128] = allowed.astype(BF16)
            pair.append(windowed[rs, cs] * allowed)
        halves.append(pair)
    put_frame(z, sh, halves)
    for b in range(NB):
        taps_out[b] = fine_taps(z, sh, b)
    lane = iota((1, 256), 1) & 15
    bias = jnp.zeros((1, 256), F32)
    for o in range(CCODE):
        bias = jnp.where(lane == o, enc_bias[o], bias)
    pre = dot(taps_out[...].reshape(z.frame, KS * 128), weights_out[0]) + bias
    slope = jnp.exp(jnp.minimum(pre, 0.0))
    code = jnp.where(pre > 0, pre, slope - 1.0).astype(BF16).astype(F32)
    slope_out[...] = slope.reshape(NB, rows, 256)
    mine_rows = own_rows(z, odd)
    first_sum = jnp.zeros((1, 256), F32)
    count_sum = jnp.zeros((1, 256), F32)
    blocks, weighted = [], []
    for b in range(NB):
        here = code[b * rows : b * rows + rows]
        allowed = code_mask[:, b * 256 : b * 256 + 256]
        codemask_out[b] = allowed.astype(BF16)
        allowed = jnp.where(mine_rows, allowed, 0.0)
        first_sum = first_sum + jnp.sum(here * allowed, axis=0, keepdims=True)
        count_sum = count_sum + jnp.sum(allowed, axis=0, keepdims=True)
        blocks.append(here)
        weighted.append((here * allowed).astype(BF16))
    second = dot(jnp.concatenate(weighted, axis=0), code.astype(BF16), ((0,), (0,)))
    for b, (low, high) in enumerate(mend_coarse(blocks)):
        code_out[b, :, 0:128] = low.astype(BF16)
        code_out[b, :, 128:256] = high.astype(BF16)
    lane_u = iota((16, 256), 1) >> 4
    total = jnp.zeros((16, 256), F32)
    for u in range(1, UW - 1):
        total = jnp.where(lane_u == u, second[u * 16 : u * 16 + 16], total)
    total = fold(total[:, :128] + total[:, 128:], (64, 32, 16))
    diagonal = (iota((8, 128), 1) >> 4) == iota((8, 128), 0)
    pay = [
        jnp.sum(jnp.where(diagonal, total[h * 8 : h * 8 + 8], 0.0), axis=0, keepdims=True)
        for h in range(2)
    ]
    for s in (first_sum, count_sum):
        pay.append(fold(jnp.broadcast_to(s[:, :128] + s[:, 128:], (8, 128)), (64, 32, 16))[0:1])
    pay = jnp.concatenate(pay, axis=0)
    for i in range(pay_out.shape[0]):
        pay_out[i] = pay


def decode_kernel(
    z, cotangent, halo, code, in_mask, weights, dec_bias,
    recon_out, sent_out, pay_out,
    cot_buf, sh, sems,
):
    section = lax.axis_index("section")
    odd = lax.rem(lax.axis_index("wide"), 2)
    rows = z.rows
    copy = pltpu.make_async_copy(
        cotangent.at[pl.ds(section * z.mb, z.mb)], cot_buf, sems.at[0]
    )
    copy.start()
    put_frame(
        z, sh, [(code[b, :, 0:128].astype(F32), code[b, :, 128:256].astype(F32)) for b in range(NB)]
    )
    raws = spread(z, sh, weights[1])
    lane_c = (iota((1, 128), 1) >> 1) & 3
    bias = jnp.zeros((1, 128), F32)
    for c in range(CIN):
        bias = jnp.where(lane_c == c, dec_bias[c], bias)
    copy.wait()
    pixels = jnp.concatenate(
        [cot_buf[...].reshape(z.own, z.span), halo[:, z.span : 2 * z.span]], axis=0
    )
    windowed = dot(dot(gather_rows(z, odd), pixels).astype(BF16), window_columns())
    mine_rows = own_rows(z, odd)
    u_local = (iota((1, 128), 1) >> 3) & (UW - 1)
    inner = mine_rows & (u_local >= 1) & (u_local <= UW - 2)
    recons, grads = [], []
    bias_sum = jnp.zeros((1, 128), F32)
    for h in range(2):
        raw = raws[h] + bias
        slope = jnp.exp(jnp.minimum(raw, 0.0))
        recon = jnp.where(raw > 0, raw, slope - 1.0)
        pieces = []
        for b in range(NB):
            allowed = in_mask[b, :, h * 128 : h * 128 + 128].astype(F32)
            cot = windowed[h * rows : h * rows + rows, b * 128 : b * 128 + 128]
            rs = slice(b * rows, b * rows + rows)
            pieces.append((recon[rs] * allowed).astype(BF16))
            grad = (cot * allowed * slope[rs]).astype(BF16).astype(F32)
            bias_sum = bias_sum + jnp.sum(jnp.where(inner, grad, 0.0), axis=0, keepdims=True)
            grads.append(grad)
        recons.append(jnp.concatenate(pieces, axis=0))
    recon_out[...] = to_pixels(z, odd, *recons).reshape(z.mb, z.band, z.span)
    put_frame(z, sh, mend_fine([(grads[b], grads[NB + b]) for b in range(NB)]))
    taps = jnp.concatenate([fine_taps(z, sh, b) for b in range(NB)], axis=0)
    sent_out[...] = dot(taps, weights[1]).astype(BF16).reshape(NB, rows, 256)
    mine = jnp.concatenate(
        [jnp.where(mine_rows, code[b].astype(F32), 0.0).astype(BF16) for b in range(NB)], axis=0
    )
    pay = pick_taps(dot(mine, taps, ((0,), (0,))))
    bias_sum = fold(jnp.broadcast_to(bias_sum, (16, 128)), (64, 32, 16, 8))
    lane = iota((16, 128), 1)
    keep = (lane < 8) & ((lane >> 1) == iota((16, 128), 0))
    column = jnp.sum(jnp.where(keep, bias_sum, 0.0), axis=1, keepdims=True)
    pay_out[...] = jnp.where(lane == 121, column, pay)


def whiten_kernel(
    z, stats, code, slope, sent, code_mask, taps, decode_pay, run_mean, run_cov,
    grad_out, keep_out, send_out, mean_out, cov_out,
):
    section = lax.axis_index("section")
    odd = lax.rem(lax.axis_index("wide"), 2)
    rows = z.rows
    pay = jnp.sum(stats[...], axis=0)
    count = pay[3:4]
    mean = pay[2:3] / count
    diagonal = (iota((8, 128), 1) >> 4) == iota((8, 128), 0)
    second = jnp.concatenate(
        [
            fold(jnp.where(diagonal, jnp.broadcast_to(pay[h : h + 1], (8, 128)), 0.0), (64, 32, 16))
            for h in range(2)
        ],
        axis=0,
    )
    lane = iota((16, 128), 1)
    row = iota((16, 128), 0)
    wide_mean = jnp.broadcast_to(mean, (16, 128))
    mean_column = jnp.sum(jnp.where(lane == row, wide_mean, 0.0), axis=1, keepdims=True)
    cov = second / jnp.broadcast_to(count, (16, 128)) - mean_column * wide_mean
    mean_out[...] = decay_rate * run_mean[...] + (1.0 - decay_rate) * mean[:, 0:CCODE]
    cov_out[...] = decay_rate * run_cov[...] + (1.0 - decay_rate) * cov[:, 0:CCODE]
    offset = cov - jnp.where((lane & 15) == row, 1.0, 0.0)
    pulled = jnp.sum(offset * mean_column, axis=0, keepdims=True)
    linear = whiten_weight * mean - 2.0 * whiten_weight * pulled
    linear = jnp.concatenate([linear, linear], axis=1)
    offset = 2.0 * whiten_weight * jnp.concatenate([offset, offset], axis=1)
    same = (iota((256, 256), 0) >> 4) == (iota((256, 256), 1) >> 4)
    matrix = jnp.broadcast_to(offset[None], (16, 16, 256)).reshape(256, 256)
    high, mid, _ = split(jnp.where(same, matrix, 0.0))
    flat = code[...].reshape(z.frame, 256)
    turned = dot(flat, high) + dot(flat, mid) + linear
    mine_rows = own_rows(z, odd)
    lane_u = iota((1, 256), 1) >> 4
    inner = mine_rows & (lane_u >= 1) & (lane_u <= UW - 2)
    last = HW // 2 - (NB - 1) * (UW - 2)
    blocks, mine = [], []
    bias_sum = jnp.zeros((1, 256), F32)
    for b in range(NB):
        pull = code_mask[b].astype(F32) * turned[b * rows : b * rows + rows]
        grad = ((sent[b].astype(F32) + pull) * slope[b]).astype(BF16).astype(F32)
        kept = jnp.where(inner & (lane_u <= last) if b == NB - 1 else inner, grad, 0.0)
        bias_sum = bias_sum + jnp.sum(kept, axis=0, keepdims=True)
        blocks.append(grad)
        mine.append(kept.astype(BF16))
    for b, (low, high) in enumerate(mend_coarse(blocks)):
        grad_out[b, :, 0:128] = low.astype(BF16)
        grad_out[b, :, 128:256] = high.astype(BF16)
    products = dot(
        jnp.concatenate(mine, axis=0), taps[...].reshape(z.frame, KS * 128), ((0,), (0,))
    )
    encode_pay = pick_taps(products)
    bias_sum = fold(
        jnp.broadcast_to(bias_sum[:, :128] + bias_sum[:, 128:], (16, 128)), (64, 32, 16)
    )
    column = jnp.sum(jnp.where(lane == row, bias_sum, 0.0), axis=1, keepdims=True)
    encode_pay = jnp.where(lane == 120, column, encode_pay)
    decoded = decode_pay[...]
    encode_pay = jnp.where(lane == 121, decoded, encode_pay)
    decoded = jnp.where(lane == 120, column, decoded)
    leads = section == 0
    keep_out[...] = jnp.where(leads, encode_pay, decoded)
    send_out[...] = jnp.where(leads, decoded, encode_pay)


def spread_kernel(z, grad, in_mask, weights, pixels_out, sh):
    odd = lax.rem(lax.axis_index("wide"), 2)
    rows = z.rows
    put_frame(
        z, sh, [(grad[b, :, 0:128].astype(F32), grad[b, :, 128:256].astype(F32)) for b in range(NB)]
    )
    raws = spread(z, sh, weights[0])
    outs = []
    for h in range(2):
        pieces = [
            raws[h][b * rows : b * rows + rows] * in_mask[b, :, h * 128 : h * 128 + 128].astype(F32)
            for b in range(NB)
        ]
        outs.append(jnp.concatenate(pieces, axis=0).astype(BF16))
    pixels_out[...] = to_pixels(z, odd, *outs).reshape(z.mb, z.band, z.span)


def finish_kernel(z, parts, kernel_out, enc_out, dec_out):
    total = jnp.sum(parts[...], axis=0)
    lane = iota((16, 128), 1)
    row = iota((16, 128), 0)
    for slot, out in ((120, enc_out), (121, dec_out)):
        column = jnp.sum(jnp.where(lane == slot, total, 0.0), axis=1, keepdims=True)
        flat = jnp.sum(jnp.where(lane == row, column, 0.0), axis=0, keepdims=True)
        out[...] = flat[:, 0 : out.shape[1]]
    onehot = tap_onehot()
    chosen = sum(dot(x, onehot) for x in split(total))
    _, o = tap_target(iota((1, NK), 1))
    kernel_out[...] = jnp.sum(
        jnp.where(iota((16, NK), 0) == o, chosen, 0.0), axis=0, keepdims=True
    )


VMEM = pl.BlockSpec(memory_space=pltpu.VMEM)
SMEM = pl.BlockSpec(memory_space=pltpu.SMEM)
ANY = pl.BlockSpec(memory_space=pl.ANY)
PARAMS = pltpu.CompilerParams(vmem_limit_bytes=48 * 1024 * 1024)


def shards(sections, wides):
    def run(
        fields, pixel_mask, channel_counts, kernels, enc_bias, dec_bias, cotangent, run_mean, run_cov
    ):
        z = Sizes(fields.shape, sections)
        assert 2 * z.band == HW and z.span == CIN * HW and z.mb == 4
        section = lax.axis_index("section")
        wide = lax.axis_index("wide")
        odd = lax.rem(wide, 2)
        swap = [(i, i ^ 1) for i in range(sections)]
        pair = [(i, i ^ 1) for i in range(wides)]
        start = jnp.where(odd == 0, z.band - HALO, 0)

        def edge(x):
            piece = lax.dynamic_slice(
                x, (section * z.mb, start, 0), (z.mb, HALO, x.shape[2])
            )
            return piece.reshape(z.halo, x.shape[2]).astype(BF16)

        halo = jnp.concatenate([edge(fields), edge(cotangent), edge(pixel_mask)], axis=1)
        halo = lax.ppermute(halo, "wide", pair)
        kernel_other = lax.ppermute(kernels, "section", swap)

        def shape(*dims, dtype=BF16):
            return jax.ShapeDtypeStruct(dims, dtype)

        frame = (NB, z.rows, 256)
        peers = sections * wides
        taps, code, slope, in_mask, code_mask, weights, pay = pl.pallas_call(
            lambda *refs: encode_kernel(z, *refs),
            out_shape=(
                shape(NB, z.rows, KS * 128), shape(*frame), shape(*frame, dtype=F32),
                shape(*frame), shape(*frame), shape(2, KS * 128, 256),
                shape(peers, 4, 128, dtype=F32),
            ),
            in_specs=[ANY, ANY, VMEM, VMEM, VMEM, SMEM, SMEM],
            out_specs=[VMEM] * 7,
            scratch_shapes=[
                pltpu.VMEM((z.mb, z.band, z.span), BF16),
                pltpu.VMEM((z.mb, z.band, HW), jnp.int32),
                pltpu.VMEM((NB, z.rows + 16, 256), F32),
                pltpu.SemaphoreType.DMA((2,)),
            ],
            compiler_params=PARAMS,
            name="encode",
        )(fields, pixel_mask, halo, kernels, kernel_other, enc_bias, channel_counts)
        stats = lax.all_to_all(pay, ("section", "wide"), 0, 0)
        recon, sent, decode_pay = pl.pallas_call(
            lambda *refs: decode_kernel(z, *refs),
            out_shape=(
                shape(z.mb, z.band, z.span), shape(*frame), shape(CCODE, 128, dtype=F32),
            ),
            in_specs=[ANY, VMEM, VMEM, VMEM, VMEM, SMEM],
            out_specs=[VMEM] * 3,
            scratch_shapes=[
                pltpu.VMEM((z.mb, z.band, z.span), BF16),
                pltpu.VMEM((NB, z.rows + 16, 256), F32),
                pltpu.SemaphoreType.DMA((1,)),
            ],
            compiler_params=PARAMS,
            cost_estimate=pl.CostEstimate(
                flops=4_000_000_000, bytes_accessed=4_000_000, transcendentals=0
            ),
            name="decode",
        )(cotangent, halo, code, in_mask, weights, dec_bias)
        grad, keep, send, new_mean, new_cov = pl.pallas_call(
            lambda *refs: whiten_kernel(z, *refs),
            out_shape=(
                shape(*frame), shape(CCODE, 128, dtype=F32), shape(CCODE, 128, dtype=F32),
                shape(1, CCODE, dtype=F32), shape(CCODE, CCODE, dtype=F32),
            ),
            in_specs=[VMEM] * 9,
            out_specs=[VMEM] * 5,
            compiler_params=PARAMS,
            name="whiten",
        )(stats, code, slope, sent, code_mask, taps, decode_pay, run_mean.reshape(1, CCODE), run_cov)
        total = keep + lax.ppermute(send, "section", swap)
        parts = lax.all_to_all(
            jnp.broadcast_to(total[None], (wides, CCODE, 128)), "wide", 0, 0
        )
        pixels = pl.pallas_call(
            lambda *refs: spread_kernel(z, *refs),
            out_shape=shape(z.mb, z.band, z.span),
            in_specs=[VMEM] * 3,
            out_specs=VMEM,
            scratch_shapes=[pltpu.VMEM((NB, z.rows + 16, 256), F32)],
            compiler_params=PARAMS,
            cost_estimate=pl.CostEstimate(
                flops=4_000_000_000, bytes_accessed=4_000_000, transcendentals=0
            ),
            name="spread",
        )(grad, in_mask, weights)
        arrived = lax.ppermute(jnp.where(section == 0, recon, pixels), "section", swap)
        pixels_out = jnp.where(
            section == 0,
            jnp.concatenate([pixels, arrived], axis=0),
            jnp.concatenate([arrived, recon], axis=0),
        )[None]
        kernel_grads, enc_grad, dec_grad = pl.pallas_call(
            lambda *refs: finish_kernel(z, *refs),
            out_shape=(
                shape(1, NK, dtype=F32), shape(1, CCODE, dtype=F32), shape(1, CIN, dtype=F32),
            ),
            in_specs=[VMEM],
            out_specs=[VMEM] * 3,
            compiler_params=PARAMS,
            name="finish",
        )(parts)
        return (
            pixels_out,
            kernel_grads,
            enc_grad.reshape(CCODE),
            dec_grad.reshape(CIN),
            new_mean.reshape(CCODE),
            new_cov,
        )

    return run


def solution(mesh):
    in_specs = (
        P(None, "wide", None),
        P(None, "wide", None),
        P(),
        P("section", None),
        P(),
        P(),
        P(None, "wide", None),
        P(),
        P(),
    )
    out_specs = (P("section", None, "wide", None), P("section", None), P(), P(), P(), P())
    run = shards(mesh.shape["section"], mesh.shape["wide"])
    return jax.shard_map(run, mesh=mesh, in_specs=in_specs, out_specs=out_specs, check_vma=False)
```

```python
import jax
import jax.numpy as jnp
from jax import lax
from jax.experimental import pallas as pl
from jax.experimental.pallas import tpu as pltpu
from jax.sharding import PartitionSpec as P

CIN = 4
CCODE = 16
KS = 5
HW = 128

UW = 16
NB = 5
HALO = 8
NK = CCODE * CIN * KS * KS

decay_rate = 0.9
whiten_weight = 0.25

F32 = jnp.float32
BF16 = jnp.bfloat16


def iota(shape, dim):
    return lax.broadcasted_iota(jnp.int32, shape, dim)


def hot(mask):
    return jnp.where(mask, 1.0, 0.0).astype(BF16)


def dot(a, b, dims=((1,), (0,))):
    return lax.dot_general(a, b, (dims, ((), ())), preferred_element_type=F32)


def fold(x, steps):
    for step in steps:
        x = x + pltpu.roll(x, step, 1)
    return x


def split(x):
    high = x.astype(BF16)
    rest = x - high.astype(F32)
    mid = rest.astype(BF16)
    return high, mid, (rest - mid.astype(F32)).astype(BF16)


class Sizes:
    def __init__(self, fields, sections):
        self.micro, self.band, self.span = fields
        self.sections = sections
        self.mb = self.micro // sections
        self.jf = self.band // 2 + HALO // 2
        self.rows = self.jf * self.mb
        self.own = self.mb * self.band
        self.halo = self.mb * HALO
        self.shift = self.mb.bit_length() - 1
        self.frame = NB * self.rows


def tap_target(n):
    o = (n * 5243) >> 19
    t = n - 100 * o
    c = (t * 1311) >> 15
    t = t - 25 * c
    k = (t * 205) >> 10
    l = t - 5 * k
    return (3 * k + (l >> 1)) * 8 + 2 * c + (l & 1), o


def tap_onehot():
    target, _ = tap_target(iota((1, NK), 1))
    return hot(iota((128, NK), 0) == target)


def row_target(z, row):
    half = z.own // 2
    parity = (row >= half).astype(jnp.int32)
    q = row - parity * half
    return (q & (z.mb - 1)) * z.band + 2 * (q >> z.shift) + parity


def gather_rows(z):
    return hot(iota((z.own, z.own), 1) == row_target(z, iota((z.own, 1), 0)))


def scatter_rows(z):
    return hot(iota((z.own, z.own), 0) == row_target(z, iota((1, z.own), 1)))


def gather_halo(z):
    row = iota((z.halo, 1), 0)
    half = z.halo // 2
    parity = (row >= half).astype(jnp.int32)
    q = row - parity * half
    target = (q & (z.mb - 1)) * HALO + 2 * (q >> z.shift) + parity
    return hot(iota((z.halo, z.halo), 1) == target)


def pixel_target(lane, inner):
    u_local = (lane >> 3) & (UW - 1)
    u = (lane >> 7) * (UW - 2) + u_local - 1
    valid = (u >= 0) & (u < HW // 2)
    if inner:
        valid = valid & (u_local >= 1) & (u_local <= UW - 2)
    return 2 * u + (lane & 1), (lane >> 1) & 3, valid


def window_columns():
    col, c, valid = pixel_target(iota((1, NB * 128), 1), False)
    target = jnp.where(valid, c * HW + col, -1)
    return hot(iota((CIN * HW, NB * 128), 0) == target)


def unwindow_columns():
    col, c, valid = pixel_target(iota((NB * 128, 1), 0), True)
    target = jnp.where(valid, c * HW + col, -1)
    return hot(iota((NB * 128, CIN * HW), 1) == target)


def window_mask_columns():
    col, _, valid = pixel_target(iota((1, NB * 128), 1), False)
    return hot(iota((HW, NB * 128), 0) == jnp.where(valid, col, -1))


def code_mask_lanes():
    lane = iota((1, 256), 1)
    u_local = lane >> 4
    inner = (u_local >= 1) & (u_local <= UW - 2)
    return hot(iota((128, 256), 0) == jnp.where(inner, u_local * 8, -1))


def own_rows(z, odd):
    j = (iota((z.rows, 1), 0) >> z.shift) - odd * (HALO // 2)
    return (j >= 0) & (j < z.band // 2)


def places(z, odd):
    own = pl.multiple_of(odd * (z.halo // 2), 16)
    halo = pl.multiple_of((1 - odd) * (z.own // 2), 16)
    return own, halo


def mend_coarse(blocks):
    last = HW // 2 - (NB - 1) * (UW - 2)
    rows = blocks[0].shape[0]
    lane = iota((rows, 128), 1)
    halves = [(x[:, :128], x[:, 128:]) for x in blocks]
    done = []
    for b, (low, high) in enumerate(halves):
        before = pltpu.roll(halves[b - 1][1], 32, 1) if b else 0.0
        new_low = jnp.where(lane < 16, before, low)
        if b + 1 < NB:
            after = pltpu.roll(halves[b + 1][0], 96, 1)
            new_high = jnp.where(lane >= 112, after, high)
        else:
            new_high = jnp.where(lane < (last + 1) * 16 - 128, high, 0.0)
        done.append((new_low, new_high))
    return done


def mend_fine(halves):
    rows = halves[0][0].shape[0]
    lane = iota((rows, 128), 1)
    done = []
    for b in range(NB):
        pair = []
        for h in range(2):
            x = halves[b][h]
            before = pltpu.roll(halves[b - 1][h], 16, 1) if b else 0.0
            after = pltpu.roll(halves[b + 1][h], 112, 1) if b + 1 < NB else 0.0
            x = jnp.where(lane < 8, before, x)
            pair.append(jnp.where(lane >= 120, after, x))
        done.append(tuple(pair))
    return done


def pad_frame(z, sh):
    zeros = jnp.zeros((NB, 8, 256), F32)
    sh[:, 0:8, :] = zeros
    sh[:, 8 + z.rows : 16 + z.rows, :] = zeros


def put_frame(z, sh, halves):
    pad_frame(z, sh)
    for b, (low, high) in enumerate(halves):
        sh[b, 8 : 8 + z.rows, 0:128] = low
        sh[b, 8 : 8 + z.rows, 128:256] = high


def put_pixels(z, sh, odd, own, halo):
    pad_frame(z, sh)
    for start, part in zip(places(z, odd), (own, halo)):
        half = part.shape[0] // 2
        rows = pl.ds(pl.multiple_of(8 + start, 8), half)
        for b in range(NB):
            for h in range(2):
                sh[b, rows, h * 128 : h * 128 + 128] = part[
                    h * half : h * half + half, b * 128 : b * 128 + 128
                ]


def fine_taps(z, sh, b):
    up = sh[b, 8 - z.mb : 8 - z.mb + z.rows, :]
    here = sh[b, 8 : 8 + z.rows, :]
    down = sh[b, 8 + z.mb : 8 + z.mb + z.rows, 0:128]
    return jnp.concatenate([up, here, down], axis=1).astype(BF16)


def coarse_taps(z, sh, b):
    down = sh[b, 8 + z.mb : 8 + z.mb + z.rows, :]
    here = sh[b, 8 : 8 + z.rows, :]
    up = sh[b, 8 - z.mb : 8 - z.mb + z.rows, :]
    return [x.astype(BF16) for x in (down, here, up)]


def spread(z, sh, weights):
    taps = [coarse_taps(z, sh, b) for b in range(NB)]
    down, here, up = (jnp.concatenate([t[i] for t in taps], axis=0) for i in range(3))
    nt = ((1,), (1,))
    out = dot(down, weights[0:256], nt) + dot(here, weights[256:512], nt)
    extra = dot(up, weights[512:640], nt)
    return out[:, :128] + extra, out[:, 128:]


def pick_taps(grads):
    lane = iota((CCODE, 128), 1)
    place = lane >> 3
    pieces = []
    for k in range(KS):
        for shift in (-1, 0, 1):
            total = jnp.zeros((CCODE, 128), F32)
            for u in range(1, UW - 1):
                part = grads[u * 16 : u * 16 + 16, k * 128 : k * 128 + 128]
                total = jnp.where(place == u + shift, part, total)
            pieces.append(total)
    pieces.append(jnp.zeros((CCODE, 128), F32))
    step = 64
    while step >= 8:
        half = len(pieces) // 2
        low = (lane & step) == 0
        merged = []
        for x, y in zip(pieces[:half], pieces[half:]):
            other = jnp.where(low, y, x)
            moved = pltpu.roll(other, step, 1)
            if step < 64:
                moved = jnp.where(low, pltpu.roll(other, 128 - step, 1), moved)
            merged.append(jnp.where(low, x, y) + moved)
        pieces = merged
        step //= 2
    return pieces[0]


def to_pixels(z, odd, sh, in_mask):
    start, _ = places(z, odd)
    half = z.own // 2
    rows = pl.ds(pl.multiple_of(8 + start, 8), half)
    flat = jnp.concatenate(
        [
            jnp.concatenate(
                [sh[b, rows, h * 128 : h * 128 + 128] for b in range(NB)], axis=1
            )
            for h in range(2)
        ],
        axis=0,
    )
    flat = flat.astype(BF16) * in_mask
    native = dot(flat, unwindow_columns()).astype(BF16)
    return dot(scatter_rows(z), native).astype(BF16).reshape(z.mb, z.band, z.span)


def build_weights(kernel_pair, outs):
    row = iota((2 * CCODE, NK), 0)
    _, o = tap_target(iota((1, NK), 1))
    values = jnp.where(row < CCODE, kernel_pair[0], kernel_pair[1])
    spreaded = jnp.where((row & (CCODE - 1)) == o, values, 0.0).astype(BF16)
    taps = dot(tap_onehot(), spreaded, ((1,), (1,))).astype(BF16)
    lane = iota((2 * CCODE, 512), 1)
    repeat = hot(iota((2 * CCODE, 512), 0) == ((lane >> 8) * CCODE + (lane & 15)))
    wide_taps = dot(taps, repeat)
    row_u = iota((128, 256), 0) >> 3
    lane_u = iota((128, 256), 1) >> 4
    for which in range(2):
        for k in range(KS):
            total = jnp.zeros((128, 256), F32)
            for shift in (-1, 0, 1):
                q = 3 * k + shift + 1
                piece = wide_taps[8 * q : 8 * q + 8, 256 * which : 256 * which + 256]
                piece = jnp.broadcast_to(piece[None], (16, 8, 256)).reshape(128, 256)
                total = jnp.where(row_u == lane_u + shift, piece, total)
            outs[which][k * 128 : k * 128 + 128, :] = total.astype(BF16)


def edge_kernel(
    z, fields, cotangent, mask, kernel, out, kernel_out, field_buf, cot_buf, mask_buf, sems
):
    odd = lax.rem(lax.axis_index("wide"), 2)
    first = lax.axis_index("section") * z.mb
    start = pl.multiple_of((1 - odd) * (z.band - 16), 16)
    copies = [
        pltpu.make_async_copy(
            source.at[pl.ds(first, z.mb), pl.ds(start, 16), :], buf, sems.at[i]
        )
        for i, (source, buf) in enumerate(
            ((fields, field_buf), (cotangent, cot_buf), (mask, mask_buf))
        )
    ]
    copies.append(pltpu.make_async_copy(kernel, kernel_out, sems.at[3]))
    for copy in copies:
        copy.start()
    lane = 0
    copies[3].wait()
    for copy, buf in zip(copies[:3], (field_buf, cot_buf, mask_buf)):
        copy.wait()
        rows = buf[...].astype(F32)
        rows = jnp.where(odd == 1, rows[:, :HALO], rows[:, HALO:])
        width = rows.shape[2]
        out[:, lane : lane + width] = rows.reshape(z.halo, width).astype(BF16)
        lane += width


def prepare_kernel(
    z, fields, mask, enc_bias, dec_bias, counts, run_mean, run_cov, kernel_own, kernel_other,
    pixels_out, inmask_out, w0_out, w1_out, aux_out,
    field_buf, mask_buf, enc_buf, dec_buf, count_buf, mean_buf, cov_buf, sems,
):
    section = lax.axis_index("section")
    wide = lax.axis_index("wide")
    first = section * z.mb
    copies = [
        pltpu.make_async_copy(source, buf, sems.at[i])
        for i, (source, buf) in enumerate(
            (
                (mask.at[pl.ds(first, z.mb)], mask_buf),
                (fields.at[pl.ds(first, z.mb)], field_buf),
                (counts, count_buf),
                (enc_bias, enc_buf),
                (dec_bias, dec_buf),
                (run_mean, mean_buf),
                (run_cov, cov_buf),
            )
        )
    ]
    for copy in copies:
        copy.start()
    mine, other = kernel_own[...].astype(F32), kernel_other[...].astype(F32)
    leads = section == 0
    build_weights(
        (jnp.where(leads, mine, other), jnp.where(leads, other, mine)), (w0_out, w1_out)
    )
    gather = gather_rows(z)
    for copy in copies[2:]:
        copy.wait()
    lane = iota((8, 128), 1)
    dec_row = jnp.zeros((8, 128), F32)
    for c in range(CIN):
        dec_row = jnp.where(((lane >> 1) & 3) == c, dec_buf[c], dec_row)
    enc_row = jnp.zeros((8, 128), F32)
    mean_row = jnp.zeros((8, 128), F32)
    for o in range(CCODE):
        enc_row = jnp.where((lane & 15) == o, enc_buf[o], enc_row)
        mean_row = jnp.where((lane & 15) == o, mean_buf[o], mean_row)
    aux_out[0:8] = dec_row
    aux_out[8:16] = enc_row
    aux_out[16:24] = mean_row
    aux_out[24:40] = jnp.zeros((16, 128), F32)
    aux_out[24:40, 0:CCODE] = cov_buf[...]
    field_now = wide * z.band // HW
    micro = iota((16, 128), 0) & (z.mb - 1)
    count = jnp.zeros((16, 128), jnp.int32)
    for m in range(z.mb):
        count = jnp.where(micro == m, count_buf[first + m, field_now], count)
    channel_ok = jnp.where(((iota((16, 128), 1) >> 1) & 3) < count, 1.0, 0.0)
    aux_out[40:56] = channel_ok
    copies[0].wait()
    pixel_mask = mask_buf[...].astype(F32).astype(BF16).reshape(z.own, HW)
    framed_mask = dot(gather, pixel_mask).astype(BF16)
    in_mask = dot(framed_mask, window_mask_columns())
    repeats = (z.own // 16, NB)
    in_mask = in_mask * jnp.tile(channel_ok, repeats)
    inmask_out[...] = in_mask.astype(BF16)
    copies[1].wait()
    pixels = field_buf[...].reshape(z.own, z.span)
    windowed = dot(dot(gather, pixels).astype(BF16), window_columns())
    pixels_out[...] = (windowed * in_mask).astype(BF16)


def encode_kernel(
    z, pixels, own_mask, halo, weights, aux,
    taps_out, code_out, slope_out, halomask_out, pay_out,
    sh, masks,
):
    odd = lax.rem(lax.axis_index("wide"), 2)
    rows = z.rows
    gather = gather_halo(z)
    framed_mask = dot(gather, halo[:, 2 * z.span : 2 * z.span + HW]).astype(BF16)
    channel_ok = jnp.tile(aux[40:56], (z.halo // 16, NB))
    halo_mask = dot(framed_mask, window_mask_columns()) * channel_ok
    halomask_out[...] = halo_mask.astype(BF16)
    halo_pixels = dot(dot(gather, halo[:, 0 : z.span]).astype(BF16), window_columns())
    put_pixels(z, sh, odd, pixels[...].astype(F32), halo_pixels * halo_mask)
    for b in range(NB):
        taps_out[b] = fine_taps(z, sh, b)
    own_start, halo_start = places(z, odd)
    for start, part in ((own_start, own_mask), (halo_start, halomask_out)):
        half = part.shape[0] // 2
        for b in range(NB):
            masks[b, pl.ds(start, half), :] = part[0:half, b * 128 : b * 128 + 128]
    code_mask = dot(masks[...].reshape(z.frame, 128), code_mask_lanes())
    bias = jnp.concatenate([aux[8:9], aux[8:9]], axis=1)
    pre = dot(taps_out[...].reshape(z.frame, KS * 128), weights[...]) + bias
    slope = jnp.exp(jnp.minimum(pre, 0.0))
    code = jnp.where(pre > 0, pre, slope - 1.0).astype(BF16).astype(F32)
    slope_out[...] = jnp.where(code_mask > 0.5, slope, -slope).reshape(NB, rows, 256)
    mine_rows = own_rows(z, odd)
    first_sum = jnp.zeros((1, 256), F32)
    count_sum = jnp.zeros((1, 256), F32)
    blocks, weighted = [], []
    for b in range(NB):
        here = code[b * rows : b * rows + rows]
        allowed = jnp.where(mine_rows, code_mask[b * rows : b * rows + rows], 0.0)
        first_sum = first_sum + jnp.sum(here * allowed, axis=0, keepdims=True)
        count_sum = count_sum + jnp.sum(allowed, axis=0, keepdims=True)
        blocks.append(here)
        weighted.append((here * allowed).astype(BF16))
    second = dot(jnp.concatenate(weighted, axis=0), code.astype(BF16), ((0,), (0,)))
    for b, (low, high) in enumerate(mend_coarse(blocks)):
        code_out[b, :, 0:128] = low.astype(BF16)
        code_out[b, :, 128:256] = high.astype(BF16)
    lane_u = iota((16, 256), 1) >> 4
    total = jnp.zeros((16, 256), F32)
    for u in range(1, UW - 1):
        total = jnp.where(lane_u == u, second[u * 16 : u * 16 + 16], total)
    total = fold(total[:, :128] + total[:, 128:], (64, 32, 16))
    diagonal = (iota((8, 128), 1) >> 4) == iota((8, 128), 0)
    pay = [
        jnp.sum(jnp.where(diagonal, total[h * 8 : h * 8 + 8], 0.0), axis=0, keepdims=True)
        for h in range(2)
    ]
    for s in (first_sum, count_sum):
        pay.append(fold(jnp.broadcast_to(s[:, :128] + s[:, 128:], (8, 128)), (64, 32, 16))[0:1])
    pay = jnp.concatenate(pay, axis=0)
    for i in range(pay_out.shape[0]):
        pay_out[i] = pay


def decode_kernel(
    z, cotangent, halo, code, in_mask, halo_mask, weights, aux,
    recon_out, sent_out, pay_out,
    cot_buf, sh, cot_frame, sems,
):
    section = lax.axis_index("section")
    odd = lax.rem(lax.axis_index("wide"), 2)
    rows = z.rows
    copy = pltpu.make_async_copy(
        cotangent.at[pl.ds(section * z.mb, z.mb)], cot_buf, sems.at[0]
    )
    copy.start()
    put_frame(
        z, sh, [(code[b, :, 0:128].astype(F32), code[b, :, 128:256].astype(F32)) for b in range(NB)]
    )
    raws = spread(z, sh, weights)
    columns = window_columns()
    halo_cot = dot(dot(gather_halo(z), halo[:, z.span : 2 * z.span]).astype(BF16), columns)
    copy.wait()
    own_cot = dot(dot(gather_rows(z), cot_buf[...].reshape(z.own, z.span)).astype(BF16), columns)
    put_pixels(
        z, cot_frame, odd, own_cot * in_mask[...].astype(F32), halo_cot * halo_mask[...].astype(F32)
    )
    mine_rows = own_rows(z, odd)
    u_local = (iota((1, 128), 1) >> 3) & (UW - 1)
    inner = mine_rows & (u_local >= 1) & (u_local <= UW - 2)
    grads = []
    bias_sum = jnp.zeros((1, 128), F32)
    for h in range(2):
        raw = raws[h] + aux[0:1]
        slope = jnp.exp(jnp.minimum(raw, 0.0))
        recon = jnp.where(raw > 0, raw, slope - 1.0)
        cs = slice(h * 128, h * 128 + 128)
        for b in range(NB):
            rs = slice(b * rows, b * rows + rows)
            sh[b, 8 : 8 + rows, cs] = recon[rs]
            grad = (cot_frame[b, 8 : 8 + rows, cs] * slope[rs]).astype(BF16).astype(F32)
            bias_sum = bias_sum + jnp.sum(jnp.where(inner, grad, 0.0), axis=0, keepdims=True)
            grads.append(grad)
    recon_out[...] = to_pixels(z, odd, sh, in_mask[...])
    put_frame(z, sh, mend_fine([(grads[b], grads[NB + b]) for b in range(NB)]))
    taps = jnp.concatenate([fine_taps(z, sh, b) for b in range(NB)], axis=0)
    sent_out[...] = dot(taps, weights[...]).astype(BF16).reshape(NB, rows, 256)
    mine = jnp.concatenate(
        [jnp.where(mine_rows, code[b].astype(F32), 0.0).astype(BF16) for b in range(NB)], axis=0
    )
    pay = pick_taps(dot(mine, taps, ((0,), (0,))))
    bias_sum = fold(jnp.broadcast_to(bias_sum, (16, 128)), (64, 32, 16, 8))
    lane = iota((16, 128), 1)
    keep = (lane < 8) & ((lane >> 1) == iota((16, 128), 0))
    column = jnp.sum(jnp.where(keep, bias_sum, 0.0), axis=1, keepdims=True)
    pay_out[...] = jnp.where(lane >= 120, column, pay)


def whiten_kernel(
    z, stats, code, slope, sent, taps, decode_pay, aux,
    grad_out, pay_out, mean_out, cov_out,
):
    odd = lax.rem(lax.axis_index("wide"), 2)
    rows = z.rows
    pay = jnp.sum(stats[...], axis=0)
    count = pay[3:4]
    mean = pay[2:3] / count
    diagonal = (iota((8, 128), 1) >> 4) == iota((8, 128), 0)
    second = jnp.concatenate(
        [
            fold(jnp.where(diagonal, jnp.broadcast_to(pay[h : h + 1], (8, 128)), 0.0), (64, 32, 16))
            for h in range(2)
        ],
        axis=0,
    )
    lane = iota((16, 128), 1)
    row = iota((16, 128), 0)
    wide_mean = jnp.broadcast_to(mean, (16, 128))
    mean_column = jnp.sum(jnp.where(lane == row, wide_mean, 0.0), axis=1, keepdims=True)
    cov = second / jnp.broadcast_to(count, (16, 128)) - mean_column * wide_mean
    mean_out[...] = decay_rate * aux[16:17, 0:CCODE] + (1.0 - decay_rate) * mean[:, 0:CCODE]
    cov_out[...] = decay_rate * aux[24:40, 0:CCODE] + (1.0 - decay_rate) * cov[:, 0:CCODE]
    offset = cov - jnp.where((lane & 15) == row, 1.0, 0.0)
    pulled = jnp.sum(offset * mean_column, axis=0, keepdims=True)
    linear = whiten_weight * mean - 2.0 * whiten_weight * pulled
    linear = jnp.concatenate([linear, linear], axis=1)
    offset = 2.0 * whiten_weight * jnp.concatenate([offset, offset], axis=1)
    same = (iota((256, 256), 0) >> 4) == (iota((256, 256), 1) >> 4)
    matrix = jnp.broadcast_to(offset[None], (16, 16, 256)).reshape(256, 256)
    high, mid, _ = split(jnp.where(same, matrix, 0.0))
    flat = code[...].reshape(z.frame, 256)
    turned = dot(
        jnp.concatenate([flat, flat], axis=1), jnp.concatenate([high, mid], axis=0)
    ) + linear
    mine_rows = own_rows(z, odd)
    lane_u = iota((1, 256), 1) >> 4
    inner = mine_rows & (lane_u >= 1) & (lane_u <= UW - 2)
    last = HW // 2 - (NB - 1) * (UW - 2)
    blocks, mine = [], []
    bias_sum = jnp.zeros((1, 256), F32)
    for b in range(NB):
        signed = slope[b]
        pull = jnp.where(signed > 0, turned[b * rows : b * rows + rows], 0.0)
        grad = ((sent[b].astype(F32) + pull) * jnp.abs(signed)).astype(BF16).astype(F32)
        kept = jnp.where(inner & (lane_u <= last) if b == NB - 1 else inner, grad, 0.0)
        bias_sum = bias_sum + jnp.sum(kept, axis=0, keepdims=True)
        blocks.append(grad)
        mine.append(kept.astype(BF16))
    for b, (low, high) in enumerate(mend_coarse(blocks)):
        grad_out[b, :, 0:128] = low.astype(BF16)
        grad_out[b, :, 128:256] = high.astype(BF16)
    products = dot(
        jnp.concatenate(mine, axis=0), taps[...].reshape(z.frame, KS * 128), ((0,), (0,))
    )
    encode_pay = pick_taps(products)
    bias_sum = fold(
        jnp.broadcast_to(bias_sum[:, :128] + bias_sum[:, 128:], (16, 128)), (64, 32, 16)
    )
    column = jnp.sum(jnp.where(lane == row, bias_sum, 0.0), axis=1, keepdims=True)
    decoded = decode_pay[...]
    biases = jnp.where((lane & 1) == 0, column, decoded)
    coarse = biases.astype(BF16).astype(F32)
    biases = jnp.where((lane & 2) == 0, coarse, biases - coarse)
    encode_pay = jnp.where(lane >= 120, biases, encode_pay)
    decoded = jnp.where(lane >= 120, biases, decoded)
    half = pay_out.shape[0] // 2
    for i in range(half):
        pay_out[i] = encode_pay.astype(BF16)
        pay_out[half + i] = decoded.astype(BF16)


def spread_kernel(z, grad, in_mask, weights, pixels_out, sh):
    odd = lax.rem(lax.axis_index("wide"), 2)
    rows = z.rows
    put_frame(
        z, sh, [(grad[b, :, 0:128].astype(F32), grad[b, :, 128:256].astype(F32)) for b in range(NB)]
    )
    raws = spread(z, sh, weights)
    for h in range(2):
        for b in range(NB):
            sh[b, 8 : 8 + rows, h * 128 : h * 128 + 128] = raws[h][b * rows : b * rows + rows]
    pixels_out[...] = to_pixels(z, odd, sh, in_mask[...])


def place_kernel(z, mine, arrived, pixels_out, order_out, sems):
    first = lax.axis_index("section") * z.mb
    copies = [
        pltpu.make_async_copy(mine, pixels_out.at[0, pl.ds(first, z.mb)], sems.at[0]),
        pltpu.make_async_copy(
            arrived, pixels_out.at[0, pl.ds(z.micro - z.mb - first, z.mb)], sems.at[1]
        ),
    ]
    for copy in copies:
        copy.start()
    order_out[...] = jnp.zeros((8, 128), F32)
    for copy in copies:
        copy.wait()


def finish_kernel(z, parts, order, kernel_out, enc_out, dec_out):
    total = jnp.sum(parts[...].astype(F32), axis=0)
    lane = iota((16, 128), 1)
    row = iota((16, 128), 0)
    for slot, out in ((120, enc_out), (121, dec_out)):
        chosen = (lane == slot) | (lane == slot + 2)
        column = jnp.sum(jnp.where(chosen, total, 0.0), axis=1, keepdims=True)
        flat = jnp.sum(jnp.where(lane == row, column, 0.0), axis=0, keepdims=True)
        out[...] = flat[:, 0 : out.shape[1]]
    onehot = tap_onehot()
    chosen = sum(dot(x, onehot) for x in split(total))
    _, o = tap_target(iota((1, NK), 1))
    kernel_out[...] = jnp.sum(
        jnp.where(iota((16, NK), 0) == o, chosen, 0.0), axis=0, keepdims=True
    )


VMEM = pl.BlockSpec(memory_space=pltpu.VMEM)
HBM = pl.BlockSpec(memory_space=pltpu.HBM)
PARAMS = pltpu.CompilerParams(vmem_limit_bytes=24 * 1024 * 1024)
DMA = pltpu.SemaphoreType.DMA


def shape(*dims, dtype=BF16):
    return jax.ShapeDtypeStruct(dims, dtype)


def shards(sections, wides):
    def run(
        fields, pixel_mask, channel_counts, kernels, enc_bias, dec_bias, cotangent, run_mean, run_cov
    ):
        z = Sizes(fields.shape, sections)
        assert 2 * z.band == HW and z.span == CIN * HW and z.mb == 4
        (
            fields, cotangent, pixel_mask, kernels, channel_counts, enc_bias, dec_bias,
            run_mean, run_cov,
        ) = (
            pltpu.with_memory_space_constraint(x, pltpu.HBM)
            for x in (
                fields, cotangent, pixel_mask, kernels, channel_counts, enc_bias, dec_bias,
                run_mean, run_cov,
            )
        )
        section = lax.axis_index("section")
        leads = section == 0
        swap = [(i, i ^ 1) for i in range(sections)]
        pair = [(i, i ^ 1) for i in range(wides)]
        frame = (NB, z.rows, 256)
        framed = pltpu.VMEM((NB, z.rows + 16, 256), F32)
        band_buf = pltpu.VMEM((z.mb, z.band, z.span), BF16)
        mask_buf = pltpu.VMEM((z.mb, z.band, HW), jnp.int32)
        edge_buf = pltpu.VMEM((z.mb, 16, z.span), BF16)
        heavy = pl.CostEstimate(flops=4_000_000_000, bytes_accessed=4_000_000, transcendentals=0)

        def call(kernel, name, outs, ins, scratch, out_specs=None, cost=None):
            return pl.pallas_call(
                lambda *refs: kernel(z, *refs),
                out_shape=outs,
                in_specs=ins,
                out_specs=out_specs or [VMEM] * len(outs),
                scratch_shapes=scratch,
                compiler_params=PARAMS,
                cost_estimate=cost,
                name=name,
            )

        halo, kernel_own = call(
            edge_kernel,
            "edge",
            [shape(z.halo, 2 * z.span + HW), shape(1, NK)],
            [HBM] * 4,
            [edge_buf, edge_buf, pltpu.VMEM((z.mb, 16, HW), jnp.int32), DMA((4,))],
        )(fields, cotangent, pixel_mask, kernels)
        halo = lax.ppermute(halo, "wide", pair)
        kernel_other = lax.ppermute(kernel_own, "section", swap)
        pixels, in_mask, w0, w1, aux = call(
            prepare_kernel,
            "prepare",
            [
                shape(z.own, NB * 128),
                shape(z.own, NB * 128),
                shape(KS * 128, 256),
                shape(KS * 128, 256),
                shape(56, 128, dtype=F32),
            ],
            [HBM] * 7 + [VMEM] * 2,
            [
                band_buf,
                mask_buf,
                pltpu.SMEM(enc_bias.shape, F32),
                pltpu.SMEM(dec_bias.shape, F32),
                pltpu.SMEM(channel_counts.shape, jnp.int32),
                pltpu.SMEM(run_mean.shape, F32),
                pltpu.VMEM(run_cov.shape, F32),
                DMA((7,)),
            ],
            cost=heavy,
        )(
            fields, pixel_mask, enc_bias, dec_bias, channel_counts, run_mean, run_cov,
            kernel_own, kernel_other,
        )
        taps, code, slope, halo_mask, pay = call(
            encode_kernel,
            "encode",
            [
                shape(NB, z.rows, KS * 128),
                shape(*frame),
                shape(*frame, dtype=F32),
                shape(z.halo, NB * 128),
                shape(sections * wides, 4, 128, dtype=F32),
            ],
            [VMEM] * 5,
            [framed, pltpu.VMEM((NB, z.rows, 128), BF16)],
        )(pixels, in_mask, halo, w0, aux)
        stats = lax.all_to_all(pay, ("section", "wide"), 0, 0)
        recon, sent, decode_pay = call(
            decode_kernel,
            "decode",
            [shape(z.mb, z.band, z.span), shape(*frame), shape(CCODE, 128, dtype=F32)],
            [HBM] + [VMEM] * 6,
            [band_buf, framed, framed, DMA((1,))],
            cost=heavy,
        )(cotangent, halo, code, in_mask, halo_mask, w1, aux)
        grad, pay, new_mean, new_cov = call(
            whiten_kernel,
            "whiten",
            [
                shape(*frame),
                shape(sections * wides, CCODE, 128),
                shape(1, CCODE, dtype=F32),
                shape(CCODE, CCODE, dtype=F32),
            ],
            [VMEM] * 7,
            [],
        )(stats, code, slope, sent, taps, decode_pay, aux)
        parts = lax.all_to_all(pay, ("section", "wide"), 0, 0)
        (pixels,) = call(
            spread_kernel,
            "spread",
            [shape(z.mb, z.band, z.span)],
            [VMEM] * 3,
            [framed],
            cost=heavy,
        )(grad, in_mask, w0)
        mine = jnp.where(leads, pixels, recon)
        arrived = lax.ppermute(jnp.where(leads, recon, pixels), "section", swap)
        pixels_out, order = call(
            place_kernel,
            "place",
            [shape(1, z.micro, z.band, z.span), shape(8, 128, dtype=F32)],
            [VMEM] * 2,
            [DMA((2,))],
            out_specs=[HBM, VMEM],
        )(mine, arrived)
        kernel_grads, enc_grad, dec_grad = call(
            finish_kernel,
            "finish",
            [
                shape(1, NK, dtype=F32),
                shape(1, CCODE, dtype=F32),
                shape(1, CIN, dtype=F32),
            ],
            [VMEM] * 2,
            [],
        )(parts, order)
        return (
            pixels_out,
            kernel_grads,
            enc_grad.reshape(CCODE),
            dec_grad.reshape(CIN),
            new_mean.reshape(CCODE),
            new_cov,
        )

    return run


def solution(mesh):
    in_specs = (
        P(None, "wide", None),
        P(None, "wide", None),
        P(),
        P("section", None),
        P(),
        P(),
        P(None, "wide", None),
        P(),
        P(),
    )
    out_specs = (P("section", None, "wide", None), P("section", None), P(), P(), P(), P())
    run = shards(mesh.shape["section"], mesh.shape["wide"])
    return jax.shard_map(run, mesh=mesh, in_specs=in_specs, out_specs=out_specs, check_vma=False)
```

```python
import jax
import jax.numpy as jnp
from jax import lax
from jax.experimental import pallas as pl
from jax.experimental.pallas import tpu as pltpu
from jax.sharding import PartitionSpec as P

CIN = 4
CCODE = 16
KS = 5
HW = 128

UW = 16
NB = 5
HALO = 8
NK = CCODE * CIN * KS * KS
COPIES = 32

decay_rate = 0.9
whiten_weight = 0.25

F32 = jnp.float32
BF16 = jnp.bfloat16


def iota(shape, dim):
    return lax.broadcasted_iota(jnp.int32, shape, dim)


def hot(mask):
    return jnp.where(mask, 1.0, 0.0).astype(BF16)


def dot(a, b, dims=((1,), (0,))):
    return lax.dot_general(a, b, (dims, ((), ())), preferred_element_type=F32)


def fold(x, unit):
    rolled = [x] + [pltpu.roll(x, step, 1) for step in range(unit, 128, unit)]
    while len(rolled) > 1:
        rolled = [sum(rolled[i : i + 2]) for i in range(0, len(rolled), 2)]
    return rolled[0]


def split(x):
    high = x.astype(BF16)
    rest = x - high.astype(F32)
    mid = rest.astype(BF16)
    return high, mid, (rest - mid.astype(F32)).astype(BF16)


class Sizes:
    def __init__(self, fields, sections):
        self.micro, self.band, self.span = fields
        self.sections = sections
        self.mb = self.micro // sections
        self.jf = self.band // 2 + HALO // 2
        self.rows = self.jf * self.mb
        self.own = self.mb * self.band
        self.halo = self.mb * HALO
        self.shift = self.mb.bit_length() - 1
        self.frame = NB * self.rows
        self.sent = self.halo + self.halo // 2


def tap_target(n):
    o = (n * 5243) >> 19
    t = n - 100 * o
    c = (t * 1311) >> 15
    t = t - 25 * c
    k = (t * 205) >> 10
    l = t - 5 * k
    return (3 * k + (l >> 1)) * 8 + 2 * c + (l & 1), o


def tap_onehot():
    target, _ = tap_target(iota((1, NK), 1))
    return hot(iota((128, NK), 0) == target)


def row_target(z, row):
    half = z.own // 2
    parity = (row >= half).astype(jnp.int32)
    q = row - parity * half
    return (q & (z.mb - 1)) * z.band + 2 * (q >> z.shift) + parity


def gather_rows(z):
    return hot(iota((z.own, z.own), 1) == row_target(z, iota((z.own, 1), 0)))


def scatter_rows(z):
    return hot(iota((z.own, z.own), 0) == row_target(z, iota((1, z.own), 1)))


def gather_halo(z, odd):
    row = iota((2 * z.halo, 1), 0)
    second = (row >= z.halo).astype(jnp.int32)
    row = row - second * z.halo
    half = z.halo // 2
    parity = (row >= half).astype(jnp.int32)
    q = row - parity * half
    m = q & (z.mb - 1)
    r = 2 * (q >> z.shift) + parity
    near = r - odd * (HALO // 2)
    there = (near >= 0) & (near < HALO // 2)
    near = jnp.where(there, z.halo + m * (HALO // 2) + near, -1)
    target = jnp.where(second == 1, near, m * HALO + r)
    return hot(iota((2 * z.halo, z.sent), 1) == target)


def pixel_target(lane, inner):
    u_local = (lane >> 3) & (UW - 1)
    u = (lane >> 7) * (UW - 2) + u_local - 1
    valid = (u >= 0) & (u < HW // 2)
    if inner:
        valid = valid & (u_local >= 1) & (u_local <= UW - 2)
    return 2 * u + (lane & 1), (lane >> 1) & 3, valid


def window_columns():
    col, c, valid = pixel_target(iota((1, NB * 128), 1), False)
    target = jnp.where(valid, c * HW + col, -1)
    return hot(iota((CIN * HW, NB * 128), 0) == target)


def unwindow_columns():
    col, c, valid = pixel_target(iota((NB * 128, 1), 0), True)
    target = jnp.where(valid, c * HW + col, -1)
    return hot(iota((NB * 128, CIN * HW), 1) == target)


def window_mask_columns():
    col, _, valid = pixel_target(iota((1, NB * 128), 1), False)
    return hot(iota((HW, NB * 128), 0) == jnp.where(valid, col, -1))


def code_mask_lanes():
    lane = iota((1, 256), 1)
    u_local = lane >> 4
    inner = (u_local >= 1) & (u_local <= UW - 2)
    return hot(iota((128, 256), 0) == jnp.where(inner, u_local * 8, -1))


def own_rows(z, odd):
    j = (iota((z.rows, 1), 0) >> z.shift) - odd * (HALO // 2)
    return (j >= 0) & (j < z.band // 2)


def places(z, odd):
    own = pl.multiple_of(odd * (z.halo // 2), 16)
    halo = pl.multiple_of((1 - odd) * (z.own // 2), 16)
    return own, halo


def mend_coarse(blocks):
    last = HW // 2 - (NB - 1) * (UW - 2)
    rows = blocks[0].shape[0]
    lane = iota((rows, 128), 1)
    halves = [(x[:, :128], x[:, 128:]) for x in blocks]
    done = []
    for b, (low, high) in enumerate(halves):
        before = pltpu.roll(halves[b - 1][1], 32, 1) if b else 0.0
        new_low = jnp.where(lane < 16, before, low)
        if b + 1 < NB:
            after = pltpu.roll(halves[b + 1][0], 96, 1)
            new_high = jnp.where(lane >= 112, after, high)
        else:
            new_high = jnp.where(lane < (last + 1) * 16 - 128, high, 0.0)
        done.append((new_low, new_high))
    return done


def mend_fine(halves):
    rows = halves[0][0].shape[0]
    lane = iota((rows, 128), 1)
    done = []
    for b in range(NB):
        pair = []
        for h in range(2):
            x = halves[b][h]
            before = pltpu.roll(halves[b - 1][h], 16, 1) if b else 0.0
            after = pltpu.roll(halves[b + 1][h], 112, 1) if b + 1 < NB else 0.0
            x = jnp.where(lane < 8, before, x)
            pair.append(jnp.where(lane >= 120, after, x))
        done.append(tuple(pair))
    return done


def pad_frame(z, sh):
    zeros = jnp.zeros((NB, 8, 256), F32)
    sh[:, 0:8, :] = zeros
    sh[:, 8 + z.rows : 16 + z.rows, :] = zeros


def put_frame(z, sh, halves):
    pad_frame(z, sh)
    for b, (low, high) in enumerate(halves):
        sh[b, 8 : 8 + z.rows, 0:128] = low
        sh[b, 8 : 8 + z.rows, 128:256] = high


def put_pixels(z, sh, odd, own, halo):
    pad_frame(z, sh)
    for start, part in zip(places(z, odd), (own, halo)):
        half = part.shape[0] // 2
        rows = pl.ds(pl.multiple_of(8 + start, 8), half)
        for b in range(NB):
            for h in range(2):
                sh[b, rows, h * 128 : h * 128 + 128] = part[
                    h * half : h * half + half, b * 128 : b * 128 + 128
                ]


def fine_taps(z, sh, b):
    up = sh[b, 8 - z.mb : 8 - z.mb + z.rows, :]
    here = sh[b, 8 : 8 + z.rows, :]
    down = sh[b, 8 + z.mb : 8 + z.mb + z.rows, 0:128]
    return jnp.concatenate([up, here, down], axis=1).astype(BF16)


def coarse_taps(z, sh, b):
    down = sh[b, 8 + z.mb : 8 + z.mb + z.rows, :]
    here = sh[b, 8 : 8 + z.rows, :]
    up = sh[b, 8 - z.mb : 8 - z.mb + z.rows, :]
    return [x.astype(BF16) for x in (down, here, up)]


def spread(z, sh, weights):
    taps = [coarse_taps(z, sh, b) for b in range(NB)]
    down, here, up = (jnp.concatenate([t[i] for t in taps], axis=0) for i in range(3))
    nt = ((1,), (1,))
    out = dot(down, weights[0:256], nt) + dot(here, weights[256:512], nt)
    extra = dot(up, weights[512:640], nt)
    return out[:, :128] + extra, out[:, 128:]


def pick_taps(grads):
    lane = iota((CCODE, 128), 1)
    place = lane >> 3
    pieces = []
    for k in range(KS):
        for shift in (-1, 0, 1):
            total = jnp.zeros((CCODE, 128), F32)
            for u in range(1, UW - 1):
                part = grads[u * 16 : u * 16 + 16, k * 128 : k * 128 + 128]
                total = jnp.where(place == u + shift, part, total)
            pieces.append(total)
    pieces.append(jnp.zeros((CCODE, 128), F32))
    block = lane >> 5
    fours = []
    for first in range(4):
        group = pieces[first::4]
        parts = []
        for j in range(4):
            x = group[j]
            for t in range(1, 4):
                x = jnp.where(block == t, group[(t + j) & 3], x)
            parts.append(x)
        fours.append(
            (parts[0] + pltpu.roll(parts[1], 32, 1))
            + (pltpu.roll(parts[2], 64, 1) + pltpu.roll(parts[3], 96, 1))
        )
    inner = place & 3
    total = None
    for j in range(4):
        x = fours[j]
        for t in range(1, 4):
            x = jnp.where(inner == t, fours[(t + j) & 3], x)
        if j:
            x = jnp.where(inner >= j, pltpu.roll(x, 8 * j, 1), pltpu.roll(x, 96 + 8 * j, 1))
        total = x if total is None else total + x
    return total


def own_frame(z, odd, sh):
    start, _ = places(z, odd)
    half = z.own // 2
    rows = pl.ds(pl.multiple_of(8 + start, 8), half)
    flat = jnp.concatenate(
        [
            jnp.concatenate(
                [sh[b, rows, h * 128 : h * 128 + 128] for b in range(NB)], axis=1
            )
            for h in range(2)
        ],
        axis=0,
    )
    return flat.astype(BF16)


def spread_taps(kernel_pair):
    row = iota((2 * CCODE, NK), 0)
    _, o = tap_target(iota((1, NK), 1))
    values = jnp.where(row < CCODE, kernel_pair[0], kernel_pair[1])
    spreaded = jnp.where((row & (CCODE - 1)) == o, values, 0.0).astype(BF16)
    taps = dot(spreaded, tap_onehot(), ((1,), (1,))).astype(BF16)
    lane = iota((2 * CCODE, 512), 1)
    repeat = hot(iota((2 * CCODE, 512), 0) == ((lane >> 8) * CCODE + (lane & 15)))
    return dot(taps, repeat, ((0,), (0,))).astype(BF16)


def band_weights(wide_taps):
    wide_taps = wide_taps.astype(F32)
    row_u = iota((128, 256), 0) >> 3
    lane_u = iota((128, 256), 1) >> 4
    masks = [row_u == lane_u + shift for shift in (-1, 0, 1)]
    parts = []
    for k in range(KS):
        total = jnp.zeros((128, 256), F32)
        for i, mask in enumerate(masks):
            q = 3 * k + i
            piece = wide_taps[8 * q : 8 * q + 8]
            piece = jnp.broadcast_to(piece[None], (16, 8, 256)).reshape(128, 256)
            total = jnp.where(mask, piece, total)
        parts.append(total.astype(BF16))
    return jnp.concatenate(parts, axis=0)


def edge_kernel(
    z, fields, mask, cotangent, kernel, out, kernel_out,
    field_buf, mask_buf, cot_buf, kernel_buf, sems,
):
    odd = lax.rem(lax.axis_index("wide"), 2)
    first = lax.axis_index("section") * z.mb
    start = pl.multiple_of((1 - odd) * (z.band - 16), 16)
    copies = [
        pltpu.make_async_copy(
            source.at[pl.ds(first, z.mb), pl.ds(start, 16), :], buf, sems.at[i]
        )
        for i, (source, buf) in enumerate(
            ((fields, field_buf), (mask, mask_buf), (cotangent, cot_buf))
        )
    ]
    copies.append(pltpu.make_async_copy(kernel, kernel_buf, sems.at[3]))
    for copy in copies:
        copy.start()
    out[z.halo : z.sent, z.span : z.span + HW] = jnp.zeros((z.sent - z.halo, HW), BF16)
    for copy in copies:
        copy.wait()
    kernel_out[...] = jnp.broadcast_to(kernel_buf[...].astype(F32), (COPIES, NK)).astype(BF16)

    def edge_rows(buf, count):
        rows = buf[...].astype(F32)
        rows = jnp.where(odd == 1, rows[:, :count], rows[:, 16 - count :])
        return rows.reshape(z.mb * count, rows.shape[2]).astype(BF16)

    out[0 : z.halo, 0 : z.span] = edge_rows(field_buf, HALO)
    out[0 : z.halo, z.span : z.span + HW] = edge_rows(mask_buf, HALO)
    rows = cot_buf[...].astype(F32)
    rows = jnp.where(odd == 1, rows[:, :HALO], rows[:, 16 - HALO :])
    rows = [
        jnp.where(odd == 1, x[: HALO // 2], x[HALO // 2 :]) for x in (rows[m] for m in range(z.mb))
    ]
    out[z.halo : z.sent, 0 : z.span] = jnp.concatenate(rows, axis=0).astype(BF16)


def prepare_kernel(
    z, fields, mask, cotangent, counts, enc_bias, dec_bias, run_mean, run_cov,
    pixels_out, cot_out, inmask_out, mask_out, aux_out,
    count_buf, enc_buf, dec_buf, mean_buf, cov_buf, sems,
):
    section = lax.axis_index("section")
    wide = lax.axis_index("wide")
    first = section * z.mb
    mine_rows = pl.ds(first, z.mb)
    copies = [
        pltpu.make_async_copy(source, buf, sems.at[i])
        for i, (source, buf) in enumerate(
            (
                (counts, count_buf),
                (enc_bias, enc_buf),
                (dec_bias, dec_buf),
                (run_mean, mean_buf),
                (run_cov, cov_buf),
            )
        )
    ]
    for copy in copies:
        copy.start()
    gather = gather_rows(z)
    columns = window_columns()
    mask_columns = window_mask_columns()
    pixel_mask = mask[mine_rows].astype(F32).astype(BF16).reshape(z.own, HW)
    framed_mask = dot(gather, pixel_mask).astype(BF16)
    mask_out[...] = framed_mask
    in_mask = dot(framed_mask, mask_columns)
    pixels = jnp.concatenate(
        [x[mine_rows].reshape(z.own, z.span) for x in (fields, cotangent)], axis=1
    )
    pixels = dot(gather, pixels).astype(BF16)
    pixels = jnp.concatenate([pixels[:, 0 : z.span], pixels[:, z.span :]], axis=0)
    windowed = dot(pixels, columns)
    for copy in copies:
        copy.wait()
    lane = iota((8, 128), 1)
    dec_row = jnp.zeros((8, 128), F32)
    for c in range(CIN):
        dec_row = jnp.where(((lane >> 1) & 3) == c, dec_buf[c], dec_row)
    enc_row = jnp.zeros((8, 128), F32)
    mean_row = jnp.zeros((8, 128), F32)
    for o in range(CCODE):
        enc_row = jnp.where((lane & 15) == o, enc_buf[o], enc_row)
        mean_row = jnp.where((lane & 15) == o, mean_buf[o], mean_row)
    aux_out[0:8] = dec_row
    aux_out[8:16] = enc_row
    aux_out[16:24] = mean_row
    aux_out[24:40] = jnp.zeros((16, 128), F32)
    aux_out[24:40, 0:CCODE] = cov_buf[...]
    field_now = wide * z.band // HW
    micro = iota((16, 128), 0) & (z.mb - 1)
    count = jnp.zeros((16, 128), jnp.int32)
    for m in range(z.mb):
        count = jnp.where(micro == m, count_buf[first + m, field_now], count)
    channel_ok = jnp.where(((iota((16, 128), 1) >> 1) & 3) < count, 1.0, 0.0)
    aux_out[40:56] = channel_ok
    in_mask = in_mask * jnp.tile(channel_ok, (z.own // 16, NB))
    inmask_out[...] = in_mask.astype(BF16)
    pixels_out[...] = (windowed[0 : z.own] * in_mask).astype(BF16)
    cot_out[...] = (windowed[z.own : 2 * z.own] * in_mask).astype(BF16)


def taps_kernel(z, kernel_own, kernel_other, weights_out):
    mine, other = (x[0:16].astype(F32)[0:1] for x in (kernel_own, kernel_other))
    leads = lax.axis_index("section") == 0
    weights_out[...] = spread_taps((jnp.where(leads, mine, other), jnp.where(leads, other, mine)))


def local_taps(sh, b, rows, step):
    up = sh[b, 16 - step : 16 - step + rows, :]
    here = sh[b, 16 : 16 + rows, :]
    down = sh[b, 16 + step : 16 + step + rows, 0:128]
    return jnp.concatenate([up, here, down], axis=1).astype(BF16)


def encode_rows(taps, weights, bias, masks, mine):
    code_mask = dot(masks, code_mask_lanes())
    pre = dot(taps, band_weights(weights)) + bias
    slope = jnp.exp(jnp.minimum(pre, 0.0))
    code = jnp.where(pre > 0, pre, slope - 1.0).astype(BF16).astype(F32)
    slope = jnp.where(code_mask > 0.5, slope, -slope)
    allowed = code_mask if mine is None else jnp.where(mine, code_mask, 0.0)
    weighted = code * allowed
    second = dot(weighted.astype(BF16), code.astype(BF16), ((0,), (0,)))
    sums = [jnp.sum(x, axis=0, keepdims=True) for x in (weighted, allowed)]
    lane_u = iota((16, 256), 1) >> 4
    total = jnp.zeros((16, 256), F32)
    for u in range(1, UW - 1):
        total = jnp.where(lane_u == u, second[u * 16 : u * 16 + 16], total)
    total = fold(total[:, :128] + total[:, 128:], 16)
    diagonal = (iota((8, 128), 1) >> 4) == iota((8, 128), 0)
    pay = [
        jnp.sum(jnp.where(diagonal, total[h * 8 : h * 8 + 8], 0.0), axis=0, keepdims=True)
        for h in range(2)
    ]
    for s in sums:
        pay.append(fold(jnp.broadcast_to(s[:, :128] + s[:, 128:], (8, 128)), 16)[0:1])
    return code, slope, jnp.concatenate(pay, axis=0)


def put_codes(code, slope, count, start, code_out, slope_out):
    blocks = [code[b * count : b * count + count] for b in range(NB)]
    rows = pl.ds(start, count)
    for b, (low, high) in enumerate(mend_coarse(blocks)):
        code_out[b, rows, 0:128] = low.astype(BF16)
        code_out[b, rows, 128:256] = high.astype(BF16)
        slope_out[b, rows, :] = slope[b * count : b * count + count]


def inner_kernel(z, pixels, own_mask, weights, aux, taps_out, code_out, slope_out, pay_out, sh):
    odd = lax.rem(lax.axis_index("wide"), 2)
    half = z.own // 2
    count = half - 16
    zeros = jnp.zeros((NB, 16, 256), F32)
    sh[:, 0:16, :] = zeros
    sh[:, half : half + 16, :] = zeros
    here = pl.ds(pl.multiple_of((1 - odd) * 16, 16), half)
    for b in range(NB):
        for h in range(2):
            sh[b, here, h * 128 : h * 128 + 128] = pixels[
                h * half : h * half + half, b * 128 : b * 128 + 128
            ].astype(F32)
    start = pl.multiple_of(odd * 32, 16)
    taps = [local_taps(sh, b, count, z.mb) for b in range(NB)]
    for b in range(NB):
        taps_out[b, pl.ds(start, count), :] = taps[b]
    kept = pl.ds(pl.multiple_of(odd * 16, 16), count)
    masks = jnp.concatenate([own_mask[kept, b * 128 : b * 128 + 128] for b in range(NB)], axis=0)
    bias = jnp.concatenate([aux[8:9], aux[8:9]], axis=1)
    code, slope, pay = encode_rows(
        jnp.concatenate(taps, axis=0), weights[:, 0:256], bias, masks, None
    )
    pay_out[...] = pay
    put_codes(code, slope, count, start, code_out, slope_out)


def encode_kernel(
    z, pixels, own_mask, halo, weights, aux, inner_pay, taps_in, code_in, slope_in,
    taps_out, code_out, slope_out, cot_out, pay_out,
    sh, pays, sem,
):
    odd = lax.rem(lax.axis_index("wide"), 2)
    half = z.own // 2
    count = 32
    gather = gather_halo(z, odd)
    framed_mask = dot(gather[0 : z.halo], halo[:, z.span : z.span + HW]).astype(BF16)
    channel_ok = jnp.tile(aux[40:56], (z.halo // 16, NB))
    halo_mask = dot(framed_mask, window_mask_columns()) * channel_ok
    halo_pixels = dot(dot(gather, halo[:, 0 : z.span]).astype(BF16), window_columns())
    halo_x = halo_pixels[0 : z.halo] * halo_mask
    zeros = jnp.zeros((NB, 16, 256), F32)
    sh[:, 0:16, :] = zeros
    sh[:, 48:64, :] = zeros
    own_start = pl.multiple_of((1 - odd) * (half - 32), 16)
    own_there = pl.ds(pl.multiple_of(odd * 32, 16), 32)
    halo_there = pl.ds(pl.multiple_of((2 - odd) * 16, 16), 16)
    for b in range(NB):
        for h in range(2):
            cs = slice(b * 128, b * 128 + 128)
            own = pixels[pl.ds(pl.multiple_of(own_start + h * half, 16), 32), cs]
            sh[b, own_there, h * 128 : h * 128 + 128] = own.astype(F32)
            sh[b, halo_there, h * 128 : h * 128 + 128] = halo_x[h * 16 : h * 16 + 16, cs]
    start = pl.multiple_of((1 - odd) * (z.rows - count), 16)
    taps = [local_taps(sh, b, count, z.mb) for b in range(NB)]
    for b in range(NB):
        taps_out[b, pl.ds(start, count), :] = taps[b]
    edge_mask = own_mask[pl.ds(pl.multiple_of((1 - odd) * (half - 16), 16), 16), :].astype(F32)
    first = jnp.where(odd == 1, halo_mask[0:16], edge_mask)
    later = jnp.where(odd == 1, edge_mask, halo_mask[0:16])
    masks = jnp.concatenate(
        [x[:, b * 128 : b * 128 + 128] for b in range(NB) for x in (first, later)], axis=0
    ).astype(BF16)
    bias = jnp.concatenate([aux[8:9], aux[8:9]], axis=1)
    mine = ((iota((NB * count, 1), 0) >> 4) & 1) == odd
    code, slope, pay = encode_rows(
        jnp.concatenate(taps, axis=0), weights[:, 0:256], bias, masks, mine
    )
    pay = pay + inner_pay[...]
    for i in range(pays.shape[0]):
        pays[i] = pay
    copy = pltpu.make_async_copy(pays, pay_out, sem.at[0])
    copy.start()
    put_codes(code, slope, count, start, code_out, slope_out)
    cot_out[...] = (halo_pixels[z.halo : 2 * z.halo] * halo_mask).astype(BF16)
    copy.wait()


def decode_kernel(
    z, code, own_cot, halo_cot, weights, aux,
    recon_out, sent_out, pay_out,
    sh, cot_frame,
):
    odd = lax.rem(lax.axis_index("wide"), 2)
    rows = z.rows
    put_frame(
        z, sh, [(code[b, :, 0:128].astype(F32), code[b, :, 128:256].astype(F32)) for b in range(NB)]
    )
    banded = band_weights(weights[:, 256:512])
    raws = spread(z, sh, banded)
    put_pixels(z, cot_frame, odd, own_cot[...].astype(F32), halo_cot[...].astype(F32))
    mine_rows = own_rows(z, odd)
    u_local = (iota((1, 128), 1) >> 3) & (UW - 1)
    inner = mine_rows & (u_local >= 1) & (u_local <= UW - 2)
    grads = []
    bias_sum = jnp.zeros((1, 128), F32)
    for h in range(2):
        raw = raws[h] + aux[0:1]
        slope = jnp.exp(jnp.minimum(raw, 0.0))
        recon = jnp.where(raw > 0, raw, slope - 1.0)
        cs = slice(h * 128, h * 128 + 128)
        for b in range(NB):
            rs = slice(b * rows, b * rows + rows)
            sh[b, 8 : 8 + rows, cs] = recon[rs]
            grad = (cot_frame[b, 8 : 8 + rows, cs] * slope[rs]).astype(BF16).astype(F32)
            bias_sum = bias_sum + jnp.sum(jnp.where(inner, grad, 0.0), axis=0, keepdims=True)
            grads.append(grad)
    recon_out[...] = own_frame(z, odd, sh)
    put_frame(z, sh, mend_fine([(grads[b], grads[NB + b]) for b in range(NB)]))
    taps = jnp.concatenate([fine_taps(z, sh, b) for b in range(NB)], axis=0)
    sent_out[...] = dot(taps, banded).astype(BF16).reshape(NB, rows, 256)
    mine = jnp.concatenate(
        [jnp.where(mine_rows, code[b].astype(F32), 0.0).astype(BF16) for b in range(NB)], axis=0
    )
    pay = pick_taps(dot(mine, taps, ((0,), (0,))))
    bias_sum = fold(jnp.broadcast_to(bias_sum, (16, 128)), 8)
    lane = iota((16, 128), 1)
    keep = (lane < 8) & ((lane >> 1) == iota((16, 128), 0))
    column = jnp.sum(jnp.where(keep, bias_sum, 0.0), axis=1, keepdims=True)
    pay_out[...] = jnp.where(lane >= 120, column, pay)


def whiten_kernel(
    z, stats, code, slope, sent, taps, decode_pay, aux,
    grad_out, pay_out, moments_out,
    pays, sem,
):
    odd = lax.rem(lax.axis_index("wide"), 2)
    rows = z.rows
    pay = jnp.sum(stats[...], axis=0)
    count = pay[3:4]
    mean = pay[2:3] / count
    diagonal = (iota((8, 128), 1) >> 4) == iota((8, 128), 0)
    second = jnp.concatenate(
        [
            fold(jnp.where(diagonal, jnp.broadcast_to(pay[h : h + 1], (8, 128)), 0.0), 16)
            for h in range(2)
        ],
        axis=0,
    )
    lane = iota((16, 128), 1)
    row = iota((16, 128), 0)
    wide_mean = jnp.broadcast_to(mean, (16, 128))
    mean_column = jnp.sum(jnp.where(lane == row, wide_mean, 0.0), axis=1, keepdims=True)
    cov = second / jnp.broadcast_to(count, (16, 128)) - mean_column * wide_mean
    moments_out[0:CCODE] = cov
    moments_out[CCODE:] = jnp.broadcast_to(mean, (8, 128))
    offset = cov - jnp.where((lane & 15) == row, 1.0, 0.0)
    pulled = jnp.sum(offset * mean_column, axis=0, keepdims=True)
    linear = whiten_weight * mean - 2.0 * whiten_weight * pulled
    linear = jnp.concatenate([linear, linear], axis=1)
    offset = 2.0 * whiten_weight * jnp.concatenate([offset, offset], axis=1)
    same = (iota((256, 256), 0) >> 4) == (iota((256, 256), 1) >> 4)
    matrix = jnp.broadcast_to(offset[None], (16, 16, 256)).reshape(256, 256)
    high, mid, _ = split(jnp.where(same, matrix, 0.0))
    flat = code[...].reshape(z.frame, 256)
    turned = dot(
        jnp.concatenate([flat, flat], axis=1), jnp.concatenate([high, mid], axis=0)
    ) + linear
    mine_rows = own_rows(z, odd)
    lane_u = iota((1, 256), 1) >> 4
    inner = mine_rows & (lane_u >= 1) & (lane_u <= UW - 2)
    last = HW // 2 - (NB - 1) * (UW - 2)
    blocks, mine = [], []
    bias_sum = jnp.zeros((1, 256), F32)
    for b in range(NB):
        signed = slope[b]
        pull = jnp.where(signed > 0, turned[b * rows : b * rows + rows], 0.0)
        grad = ((sent[b].astype(F32) + pull) * jnp.abs(signed)).astype(BF16).astype(F32)
        kept = jnp.where(inner & (lane_u <= last) if b == NB - 1 else inner, grad, 0.0)
        bias_sum = bias_sum + jnp.sum(kept, axis=0, keepdims=True)
        blocks.append(grad)
        mine.append(kept.astype(BF16))
    products = dot(
        jnp.concatenate(mine, axis=0), taps[...].reshape(z.frame, KS * 128), ((0,), (0,))
    )
    encode_pay = pick_taps(products)
    bias_sum = fold(jnp.broadcast_to(bias_sum[:, :128] + bias_sum[:, 128:], (16, 128)), 16)
    column = jnp.sum(jnp.where(lane == row, bias_sum, 0.0), axis=1, keepdims=True)
    decoded = decode_pay[...]
    biases = jnp.where((lane & 1) == 0, column, decoded)
    coarse = biases.astype(BF16).astype(F32)
    biases = jnp.where((lane & 2) == 0, coarse, biases - coarse)
    encode_pay = jnp.where(lane >= 120, biases, encode_pay)
    decoded = jnp.where(lane >= 120, biases, decoded)
    half = pays.shape[0] // 2
    for i in range(half):
        pays[i] = encode_pay.astype(BF16)
        pays[half + i] = decoded.astype(BF16)
    copy = pltpu.make_async_copy(pays, pay_out, sem.at[0])
    copy.start()
    for b, (low, high) in enumerate(mend_coarse(blocks)):
        grad_out[b, :, 0:128] = low.astype(BF16)
        grad_out[b, :, 128:256] = high.astype(BF16)
    copy.wait()


def spread_kernel(
    z, grad, mask, weights, recon, aux, moments,
    pixels_out, send_out, onehot_out, mean_out, cov_out,
    sh, mine, means, covs, sems,
):
    section = lax.axis_index("section")
    odd = lax.rem(lax.axis_index("wide"), 2)
    rows = z.rows
    put_frame(
        z, sh, [(grad[b, :, 0:128].astype(F32), grad[b, :, 128:256].astype(F32)) for b in range(NB)]
    )
    raws = spread(z, sh, band_weights(weights[:, 0:256]))
    for h in range(2):
        for b in range(NB):
            sh[b, 8 : 8 + rows, h * 128 : h * 128 + 128] = raws[h][b * rows : b * rows + rows]
    in_mask = dot(mask[...], window_mask_columns()) * jnp.tile(aux[40:56], (z.own // 16, NB))
    in_mask = in_mask.astype(BF16)
    flat = own_frame(z, odd, sh) * in_mask
    other = recon[...] * in_mask
    leads = section == 0
    flat, other = jnp.where(leads, flat, other), jnp.where(leads, other, flat)
    native = dot(jnp.concatenate([flat, other], axis=0), unwindow_columns()).astype(BF16)
    scatter = scatter_rows(z)
    whole = (z.mb, z.band, z.span)
    mine[...] = dot(scatter, native[0 : z.own]).astype(BF16).reshape(whole)
    means[...] = decay_rate * aux[16:17, 0:CCODE] + (1.0 - decay_rate) * moments[16:17, 0:CCODE]
    covs[...] = decay_rate * aux[24:40, 0:CCODE] + (1.0 - decay_rate) * moments[0:16, 0:CCODE]
    copies = [
        pltpu.make_async_copy(source, target, sems.at[i])
        for i, (source, target) in enumerate(
            (
                (mine, pixels_out.at[0, pl.ds(section * z.mb, z.mb)]),
                (means, mean_out),
                (covs, cov_out),
            )
        )
    ]
    for copy in copies:
        copy.start()
    send_out[...] = dot(scatter, native[z.own : 2 * z.own]).astype(BF16).reshape(whole)
    onehot_out[...] = tap_onehot()
    for copy in copies:
        copy.wait()


def total_kernel(z, parts, out):
    out[...] = jnp.sum(parts[...].astype(F32), axis=0)


def finish_kernel(
    z, sums, arrived, onehot, half_done, pixels_out, kernel_out, enc_out, dec_out,
    kernels, encs, decs, sems,
):
    there = z.micro - z.mb - lax.axis_index("section") * z.mb
    copies = [
        pltpu.make_async_copy(source, target, sems.at[i])
        for i, (source, target) in enumerate(
            (
                (arrived, pixels_out.at[0, pl.ds(there, z.mb)]),
                (encs, enc_out),
                (decs, dec_out),
                (kernels, kernel_out),
            )
        )
    ]
    copies[0].start()
    total = sums[...]
    chosen = dot(jnp.concatenate(split(total), axis=0), onehot[...])
    chosen = chosen[0:16] + chosen[16:32] + chosen[32:48]
    _, o = tap_target(iota((1, NK), 1))
    kernels[...] = jnp.sum(jnp.where(iota((16, NK), 0) == o, chosen, 0.0), axis=0, keepdims=True)
    copies[3].start()
    lane = iota((16, 128), 1)
    row = iota((16, 128), 0)
    for slot, out in ((120, encs), (121, decs)):
        chosen = (lane == slot) | (lane == slot + 2)
        column = jnp.sum(jnp.where(chosen, total, 0.0), axis=1, keepdims=True)
        flat = jnp.sum(jnp.where(lane == row, column, 0.0), axis=0, keepdims=True)
        out[...] = flat[:, 0 : out.shape[1]]
    copies[1].start()
    copies[2].start()
    for copy in copies:
        copy.wait()


VMEM = pl.BlockSpec(memory_space=pltpu.VMEM)
HBM = pl.BlockSpec(memory_space=pltpu.HBM)
PARAMS = pltpu.CompilerParams(vmem_limit_bytes=24 * 1024 * 1024)
DMA = pltpu.SemaphoreType.DMA


def shape(*dims, dtype=BF16):
    return jax.ShapeDtypeStruct(dims, dtype)


def shards(sections, wides):
    def run(
        fields, pixel_mask, channel_counts, kernels, enc_bias, dec_bias, cotangent, run_mean, run_cov
    ):
        z = Sizes(fields.shape, sections)
        assert 2 * z.band == HW and z.span == CIN * HW and z.mb == 4
        whole = (fields, pixel_mask, cotangent)
        (
            fields, cotangent, pixel_mask, kernels, channel_counts, enc_bias, dec_bias,
            run_mean, run_cov,
        ) = (
            pltpu.with_memory_space_constraint(x, pltpu.HBM)
            for x in (
                fields, cotangent, pixel_mask, kernels, channel_counts, enc_bias, dec_bias,
                run_mean, run_cov,
            )
        )
        swap = [(i, i ^ 1) for i in range(sections)]
        pair = [(i, i ^ 1) for i in range(wides)]
        frame = (NB, z.rows, 256)
        framed = pltpu.VMEM((NB, z.rows + 16, 256), F32)
        band_buf = pltpu.VMEM((z.mb, z.band, z.span), BF16)
        edge_buf = pltpu.VMEM((z.mb, 16, z.span), BF16)
        heavy = pl.CostEstimate(flops=4_000_000_000, bytes_accessed=4_000_000, transcendentals=0)

        def call(kernel, name, outs, ins, scratch, out_specs=None, cost=None, alias=None):
            return pl.pallas_call(
                lambda *refs: kernel(z, *refs),
                out_shape=outs,
                in_specs=ins,
                out_specs=out_specs or [VMEM] * len(outs),
                scratch_shapes=scratch,
                compiler_params=PARAMS,
                cost_estimate=cost,
                input_output_aliases=alias or {},
                name=name,
            )

        halo, kernel_own = call(
            edge_kernel,
            "edge",
            [shape(z.sent, z.span + HW), shape(COPIES, NK)],
            [HBM] * 4,
            [
                edge_buf,
                pltpu.VMEM((z.mb, 16, HW), jnp.int32),
                edge_buf,
                pltpu.VMEM((1, NK), BF16),
                DMA((4,)),
            ],
        )(fields, pixel_mask, cotangent, kernels)
        halo = lax.ppermute(halo, "wide", pair)
        kernel_other = lax.ppermute(kernel_own, "section", swap)
        pixels, own_cot, in_mask, mask, aux = call(
            prepare_kernel,
            "prepare",
            [
                shape(z.own, NB * 128),
                shape(z.own, NB * 128),
                shape(z.own, NB * 128),
                shape(z.own, HW),
                shape(56, 128, dtype=F32),
            ],
            [VMEM] * 3 + [HBM] * 5,
            [
                pltpu.SMEM(channel_counts.shape, jnp.int32),
                pltpu.SMEM(enc_bias.shape, F32),
                pltpu.SMEM(dec_bias.shape, F32),
                pltpu.SMEM(run_mean.shape, F32),
                pltpu.VMEM(run_cov.shape, F32),
                DMA((5,)),
            ],
            cost=heavy,
        )(*whole, channel_counts, enc_bias, dec_bias, run_mean, run_cov)
        (weights,) = call(taps_kernel, "taps", [shape(128, 512)], [VMEM] * 2, [])(
            kernel_own, kernel_other
        )
        coded = [shape(NB, z.rows, KS * 128), shape(*frame), shape(*frame, dtype=F32)]
        taps, code, slope, pay = call(
            inner_kernel,
            "inner",
            coded + [shape(4, 128, dtype=F32)],
            [VMEM] * 4,
            [pltpu.VMEM((NB, z.own // 2 + 16, 256), F32)],
            cost=heavy,
        )(pixels, in_mask, weights, aux)
        taps, code, slope, halo_cot, pay = call(
            encode_kernel,
            "encode",
            coded + [shape(z.halo, NB * 128), shape(sections * wides, 4, 128, dtype=F32)],
            [VMEM] * 9,
            [
                pltpu.VMEM((NB, 64, 256), F32),
                pltpu.VMEM((sections * wides, 4, 128), F32),
                DMA((1,)),
            ],
            out_specs=[VMEM] * 4 + [HBM],
            alias={6: 0, 7: 1, 8: 2},
        )(pixels, in_mask, halo, weights, aux, pay, taps, code, slope)
        stats = lax.all_to_all(pay, ("section", "wide"), 0, 0)
        recon, sent, decode_pay = call(
            decode_kernel,
            "decode",
            [shape(z.own, NB * 128), shape(*frame), shape(CCODE, 128, dtype=F32)],
            [VMEM] * 5,
            [framed, framed],
            cost=heavy,
        )(code, own_cot, halo_cot, weights, aux)
        grad, pay, moments = call(
            whiten_kernel,
            "whiten",
            [
                shape(*frame),
                shape(sections * wides, CCODE, 128),
                shape(CCODE + 8, 128, dtype=F32),
            ],
            [VMEM] * 7,
            [pltpu.VMEM((sections * wides, CCODE, 128), BF16), DMA((1,))],
            out_specs=[VMEM, HBM, VMEM],
            alias={3: 0},
        )(stats, code, slope, sent, taps, decode_pay, aux)
        parts = lax.all_to_all(pay, ("section", "wide"), 0, 0)
        half_done, sending, onehot, new_mean, new_cov = call(
            spread_kernel,
            "spread",
            [
                shape(1, z.micro, z.band, z.span),
                shape(z.mb, z.band, z.span),
                shape(128, NK),
                shape(1, CCODE, dtype=F32),
                shape(CCODE, CCODE, dtype=F32),
            ],
            [VMEM] * 6,
            [
                framed,
                band_buf,
                pltpu.VMEM((1, CCODE), F32),
                pltpu.VMEM((CCODE, CCODE), F32),
                DMA((3,)),
            ],
            out_specs=[HBM, VMEM, VMEM, HBM, HBM],
            cost=heavy,
        )(grad, mask, weights, recon, aux, moments)
        arrived = lax.ppermute(sending, "section", swap)
        (sums,) = call(
            total_kernel,
            "total",
            [shape(CCODE, 128, dtype=F32)],
            [VMEM],
            [],
            cost=pl.CostEstimate(flops=100_000_000_000, bytes_accessed=0, transcendentals=0),
        )(parts)
        pixels_out, kernel_grads, enc_grad, dec_grad = call(
            finish_kernel,
            "finish",
            [
                shape(1, z.micro, z.band, z.span),
                shape(1, NK, dtype=F32),
                shape(1, CCODE, dtype=F32),
                shape(1, CIN, dtype=F32),
            ],
            [VMEM] * 3 + [HBM],
            [
                pltpu.VMEM((1, NK), F32),
                pltpu.VMEM((1, CCODE), F32),
                pltpu.VMEM((1, CIN), F32),
                DMA((4,)),
            ],
            out_specs=[HBM] * 4,
            alias={3: 0},
        )(sums, arrived, onehot, half_done)
        return (
            pixels_out,
            kernel_grads,
            enc_grad.reshape(CCODE),
            dec_grad.reshape(CIN),
            new_mean.reshape(CCODE),
            new_cov,
        )

    return run


def solution(mesh):
    in_specs = (
        P(None, "wide", None),
        P(None, "wide", None),
        P(),
        P("section", None),
        P(),
        P(),
        P(None, "wide", None),
        P(),
        P(),
    )
    out_specs = (P("section", None, "wide", None), P("section", None), P(), P(), P(), P())
    run = shards(mesh.shape["section"], mesh.shape["wide"])
    return jax.shard_map(run, mesh=mesh, in_specs=in_specs, out_specs=out_specs, check_vma=False)
```

```python
import jax
import jax.numpy as jnp
from jax import lax
from jax.experimental import pallas as pl
from jax.experimental.pallas import tpu as pltpu
from jax.sharding import PartitionSpec as P

CIN = 4
CCODE = 16
KS = 5
HW = 128

UW = 16
NB = 5
HALO = 8
NK = CCODE * CIN * KS * KS
COPIES = 32

decay_rate = 0.9
whiten_weight = 0.25

F32 = jnp.float32
BF16 = jnp.bfloat16


def iota(shape, dim):
    return lax.broadcasted_iota(jnp.int32, shape, dim)


def hot(mask):
    return jnp.where(mask, 1.0, 0.0).astype(BF16)


def dot(a, b, dims=((1,), (0,))):
    return lax.dot_general(a, b, (dims, ((), ())), preferred_element_type=F32)


def fold(x, unit):
    rolled = [x] + [pltpu.roll(x, step, 1) for step in range(unit, 128, unit)]
    while len(rolled) > 1:
        rolled = [sum(rolled[i : i + 2]) for i in range(0, len(rolled), 2)]
    return rolled[0]


def split(x):
    high = x.astype(BF16)
    rest = x - high.astype(F32)
    mid = rest.astype(BF16)
    return high, mid, (rest - mid.astype(F32)).astype(BF16)


class Sizes:
    def __init__(self, fields, sections):
        self.micro, self.band, self.span = fields
        self.sections = sections
        self.mb = self.micro // sections
        self.jf = self.band // 2 + HALO // 2
        self.rows = self.jf * self.mb
        self.own = self.mb * self.band
        self.halo = self.mb * HALO
        self.shift = self.mb.bit_length() - 1
        self.frame = NB * self.rows
        self.sent = self.halo + self.halo // 2


def tap_target(n):
    o = (n * 5243) >> 19
    t = n - 100 * o
    c = (t * 1311) >> 15
    t = t - 25 * c
    k = (t * 205) >> 10
    l = t - 5 * k
    return (3 * k + (l >> 1)) * 8 + 2 * c + (l & 1), o


def tap_onehot():
    target, _ = tap_target(iota((1, NK), 1))
    return hot(iota((128, NK), 0) == target)


def row_target(z, row):
    half = z.own // 2
    parity = (row >= half).astype(jnp.int32)
    q = row - parity * half
    return (q & (z.mb - 1)) * z.band + 2 * (q >> z.shift) + parity


def gather_rows(z):
    return hot(iota((z.own, z.own), 1) == row_target(z, iota((z.own, 1), 0)))


def scatter_rows(z):
    return hot(iota((z.own, z.own), 0) == row_target(z, iota((1, z.own), 1)))


def pixel_target(lane, inner):
    u_local = (lane >> 3) & (UW - 1)
    u = (lane >> 7) * (UW - 2) + u_local - 1
    valid = (u >= 0) & (u < HW // 2)
    if inner:
        valid = valid & (u_local >= 1) & (u_local <= UW - 2)
    return 2 * u + (lane & 1), (lane >> 1) & 3, valid


def window_columns():
    col, c, valid = pixel_target(iota((1, NB * 128), 1), False)
    target = jnp.where(valid, c * HW + col, -1)
    return hot(iota((CIN * HW, NB * 128), 0) == target)


def unwindow_columns():
    col, c, valid = pixel_target(iota((NB * 128, 1), 0), True)
    target = jnp.where(valid, c * HW + col, -1)
    return hot(iota((NB * 128, CIN * HW), 1) == target)


def window_mask_columns():
    col, _, valid = pixel_target(iota((1, NB * 128), 1), False)
    return hot(iota((HW, NB * 128), 0) == jnp.where(valid, col, -1))


def code_mask_lanes():
    lane = iota((1, 256), 1)
    u_local = lane >> 4
    inner = (u_local >= 1) & (u_local <= UW - 2)
    return hot(iota((128, 256), 0) == jnp.where(inner, u_local * 8, -1))


def own_rows(z, odd):
    j = (iota((z.rows, 1), 0) >> z.shift) - odd * (HALO // 2)
    return (j >= 0) & (j < z.band // 2)


def places(z, odd):
    own = pl.multiple_of(odd * (z.halo // 2), 16)
    halo = pl.multiple_of((1 - odd) * (z.own // 2), 16)
    return own, halo


def mend_coarse(blocks):
    last = HW // 2 - (NB - 1) * (UW - 2)
    rows = blocks[0].shape[0]
    lane = iota((rows, 128), 1)
    halves = [(x[:, :128], x[:, 128:]) for x in blocks]
    done = []
    for b, (low, high) in enumerate(halves):
        before = pltpu.roll(halves[b - 1][1], 32, 1) if b else 0.0
        new_low = jnp.where(lane < 16, before, low)
        if b + 1 < NB:
            after = pltpu.roll(halves[b + 1][0], 96, 1)
            new_high = jnp.where(lane >= 112, after, high)
        else:
            new_high = jnp.where(lane < (last + 1) * 16 - 128, high, 0.0)
        done.append((new_low, new_high))
    return done


def mend_fine(halves):
    rows = halves[0][0].shape[0]
    lane = iota((rows, 128), 1)
    done = []
    for b in range(NB):
        pair = []
        for h in range(2):
            x = halves[b][h]
            before = pltpu.roll(halves[b - 1][h], 16, 1) if b else 0.0
            after = pltpu.roll(halves[b + 1][h], 112, 1) if b + 1 < NB else 0.0
            x = jnp.where(lane < 8, before, x)
            pair.append(jnp.where(lane >= 120, after, x))
        done.append(tuple(pair))
    return done


def pad_frame(z, sh):
    zeros = jnp.zeros((NB, 8, 256), F32)
    sh[:, 0:8, :] = zeros
    sh[:, 8 + z.rows : 16 + z.rows, :] = zeros


def put_frame(z, sh, halves):
    pad_frame(z, sh)
    for b, (low, high) in enumerate(halves):
        sh[b, 8 : 8 + z.rows, 0:128] = low
        sh[b, 8 : 8 + z.rows, 128:256] = high


def put_pixels(z, sh, odd, own, halo):
    pad_frame(z, sh)
    for start, part in zip(places(z, odd), (own, halo)):
        half = part.shape[0] // 2
        rows = pl.ds(pl.multiple_of(8 + start, 8), half)
        for b in range(NB):
            for h in range(2):
                sh[b, rows, h * 128 : h * 128 + 128] = part[
                    h * half : h * half + half, b * 128 : b * 128 + 128
                ]


def fine_taps(z, sh, b):
    up = sh[b, 8 - z.mb : 8 - z.mb + z.rows, :]
    here = sh[b, 8 : 8 + z.rows, :]
    down = sh[b, 8 + z.mb : 8 + z.mb + z.rows, 0:128]
    return jnp.concatenate([up, here, down], axis=1).astype(BF16)


def coarse_taps(z, sh, b):
    down = sh[b, 8 + z.mb : 8 + z.mb + z.rows, :]
    here = sh[b, 8 : 8 + z.rows, :]
    up = sh[b, 8 - z.mb : 8 - z.mb + z.rows, :]
    return [x.astype(BF16) for x in (down, here, up)]


def spread(z, sh, weights):
    taps = [coarse_taps(z, sh, b) for b in range(NB)]
    down, here, up = (jnp.concatenate([t[i] for t in taps], axis=0) for i in range(3))
    nt = ((1,), (1,))
    out = dot(down, weights[0:256], nt) + dot(here, weights[256:512], nt)
    extra = dot(up, weights[512:640], nt)
    return out[:, :128] + extra, out[:, 128:]


def pick_taps(grads):
    lane = iota((CCODE, 128), 1)
    place = lane >> 3
    pieces = []
    for k in range(KS):
        for shift in (-1, 0, 1):
            total = jnp.zeros((CCODE, 128), F32)
            for u in range(1, UW - 1):
                part = grads[u * 16 : u * 16 + 16, k * 128 : k * 128 + 128]
                total = jnp.where(place == u + shift, part, total)
            pieces.append(total)
    pieces.append(jnp.zeros((CCODE, 128), F32))
    block = lane >> 5
    fours = []
    for first in range(4):
        group = pieces[first::4]
        parts = []
        for j in range(4):
            x = group[j]
            for t in range(1, 4):
                x = jnp.where(block == t, group[(t + j) & 3], x)
            parts.append(x)
        fours.append(
            (parts[0] + pltpu.roll(parts[1], 32, 1))
            + (pltpu.roll(parts[2], 64, 1) + pltpu.roll(parts[3], 96, 1))
        )
    inner = place & 3
    total = None
    for j in range(4):
        x = fours[j]
        for t in range(1, 4):
            x = jnp.where(inner == t, fours[(t + j) & 3], x)
        if j:
            x = jnp.where(inner >= j, pltpu.roll(x, 8 * j, 1), pltpu.roll(x, 96 + 8 * j, 1))
        total = x if total is None else total + x
    return total


def own_frame(z, odd, sh):
    start, _ = places(z, odd)
    half = z.own // 2
    rows = pl.ds(pl.multiple_of(8 + start, 8), half)
    flat = jnp.concatenate(
        [
            jnp.concatenate(
                [sh[b, rows, h * 128 : h * 128 + 128] for b in range(NB)], axis=1
            )
            for h in range(2)
        ],
        axis=0,
    )
    return flat.astype(BF16)


def spread_taps(kernel_pair):
    row = iota((2 * CCODE, NK), 0)
    _, o = tap_target(iota((1, NK), 1))
    values = jnp.where(row < CCODE, kernel_pair[0], kernel_pair[1])
    spreaded = jnp.where((row & (CCODE - 1)) == o, values, 0.0).astype(BF16)
    taps = dot(spreaded, tap_onehot(), ((1,), (1,))).astype(BF16)
    lane = iota((2 * CCODE, 512), 1)
    repeat = hot(iota((2 * CCODE, 512), 0) == ((lane >> 8) * CCODE + (lane & 15)))
    return dot(taps, repeat, ((0,), (0,))).astype(BF16)


def band_weights(wide_taps):
    wide_taps = wide_taps.astype(F32)
    row_u = iota((128, 256), 0) >> 3
    lane_u = iota((128, 256), 1) >> 4
    masks = [row_u == lane_u + shift for shift in (-1, 0, 1)]
    parts = []
    for k in range(KS):
        total = jnp.zeros((128, 256), F32)
        for i, mask in enumerate(masks):
            q = 3 * k + i
            piece = wide_taps[8 * q : 8 * q + 8]
            piece = jnp.broadcast_to(piece[None], (16, 8, 256)).reshape(128, 256)
            total = jnp.where(mask, piece, total)
        parts.append(total.astype(BF16))
    return jnp.concatenate(parts, axis=0)


def edge_kernel(
    z, fields, mask, cotangent, kernel, out, kernel_out,
    field_buf, mask_buf, cot_buf, kernel_buf, sems,
):
    odd = lax.rem(lax.axis_index("wide"), 2)
    first = lax.axis_index("section") * z.mb
    start = pl.multiple_of((1 - odd) * (z.band - 16), 16)
    copies = [
        pltpu.make_async_copy(
            source.at[pl.ds(first, z.mb), pl.ds(start, 16), :], buf, sems.at[i]
        )
        for i, (source, buf) in enumerate(
            ((fields, field_buf), (mask, mask_buf), (cotangent, cot_buf))
        )
    ]
    copies.append(pltpu.make_async_copy(kernel, kernel_buf, sems.at[3]))
    for copy in copies:
        copy.start()
    out[z.halo : z.sent, z.span : z.span + HW] = jnp.zeros((z.sent - z.halo, HW), BF16)
    for copy in copies:
        copy.wait()
    kernel_out[...] = jnp.broadcast_to(kernel_buf[...].astype(F32), (COPIES, NK)).astype(BF16)

    def beside(buf):
        rows = buf[...].astype(F32)
        return jnp.where(odd == 1, rows[:, :HALO], rows[:, HALO:])

    def ordered(rows, firsts):
        return jnp.concatenate(
            [rows[:, j + h] for h in range(2) for j in firsts], axis=0
        ).astype(BF16)

    mask_rows = beside(mask_buf)
    allowed = jnp.concatenate([mask_rows] * CIN, axis=2)
    every, half = range(0, HALO, 2), range(0, HALO // 2, 2)
    out[0 : z.halo, 0 : z.span] = ordered(beside(field_buf) * allowed, every)
    out[0 : z.halo, z.span : z.span + HW] = ordered(mask_rows, every)
    near = beside(cot_buf) * allowed
    near = jnp.where(odd == 1, near[:, : HALO // 2], near[:, HALO // 2 :])
    out[z.halo : z.sent, 0 : z.span] = ordered(near, half)


def prepare_kernel(
    z, fields, mask, counts, enc_bias, dec_bias, run_mean, run_cov,
    pixels_out, inmask_out, aux_out,
    count_buf, enc_buf, dec_buf, mean_buf, cov_buf, sems,
):
    section = lax.axis_index("section")
    wide = lax.axis_index("wide")
    first = section * z.mb
    mine_rows = pl.ds(first, z.mb)
    copies = [
        pltpu.make_async_copy(source, buf, sems.at[i])
        for i, (source, buf) in enumerate(
            (
                (counts, count_buf),
                (enc_bias, enc_buf),
                (dec_bias, dec_buf),
                (run_mean, mean_buf),
                (run_cov, cov_buf),
            )
        )
    ]
    for copy in copies:
        copy.start()
    gather = gather_rows(z)
    columns = window_columns()
    mask_columns = window_mask_columns()
    pixel_mask = mask[mine_rows].astype(F32).astype(BF16).reshape(z.own, HW)
    framed_mask = dot(gather, pixel_mask).astype(BF16)
    in_mask = dot(framed_mask, mask_columns)
    windowed = dot(
        dot(gather, fields[mine_rows].reshape(z.own, z.span)).astype(BF16), columns
    )
    for copy in copies:
        copy.wait()
    lane = iota((8, 128), 1)
    dec_row = jnp.zeros((8, 128), F32)
    for c in range(CIN):
        dec_row = jnp.where(((lane >> 1) & 3) == c, dec_buf[c], dec_row)
    enc_row = jnp.zeros((8, 128), F32)
    mean_row = jnp.zeros((8, 128), F32)
    for o in range(CCODE):
        enc_row = jnp.where((lane & 15) == o, enc_buf[o], enc_row)
        mean_row = jnp.where((lane & 15) == o, mean_buf[o], mean_row)
    aux_out[0:8] = dec_row
    aux_out[8:16] = enc_row
    aux_out[16:24] = mean_row
    aux_out[24:40] = jnp.zeros((16, 128), F32)
    aux_out[24:40, 0:CCODE] = cov_buf[...]
    field_now = wide * z.band // HW
    micro = iota((16, 128), 0) & (z.mb - 1)
    count = jnp.zeros((16, 128), jnp.int32)
    for m in range(z.mb):
        count = jnp.where(micro == m, count_buf[first + m, field_now], count)
    channel_ok = jnp.where(((iota((16, 128), 1) >> 1) & 3) < count, 1.0, 0.0)
    aux_out[40:56] = channel_ok
    in_mask = in_mask * jnp.tile(channel_ok, (z.own // 16, NB))
    inmask_out[...] = in_mask.astype(BF16)
    pixels_out[...] = (windowed * in_mask).astype(BF16)


def taps_kernel(z, kernel_own, kernel_other, weights_out):
    mine, other = (x[0:16].astype(F32)[0:1] for x in (kernel_own, kernel_other))
    leads = lax.axis_index("section") == 0
    weights_out[...] = spread_taps((jnp.where(leads, mine, other), jnp.where(leads, other, mine)))


def local_taps(sh, b, rows, step):
    up = sh[b, 16 - step : 16 - step + rows, :]
    here = sh[b, 16 : 16 + rows, :]
    down = sh[b, 16 + step : 16 + step + rows, 0:128]
    return jnp.concatenate([up, here, down], axis=1).astype(BF16)


def encode_rows(taps, banded, bias, masks, mine):
    code_mask = dot(masks, code_mask_lanes())
    pre = dot(taps, banded) + bias
    slope = jnp.exp(jnp.minimum(pre, 0.0))
    code = jnp.where(pre > 0, pre, slope - 1.0).astype(BF16).astype(F32)
    slope = jnp.where(code_mask > 0.5, slope, -slope)
    allowed = code_mask if mine is None else jnp.where(mine, code_mask, 0.0)
    weighted = code * allowed
    halves = [
        jnp.concatenate([x[:, 0:128], x[:, 128:256]], axis=0).astype(BF16) for x in (weighted, code)
    ]
    second = dot(*halves, ((0,), (0,)))
    sums = [jnp.sum(x, axis=0, keepdims=True) for x in (weighted, allowed)]
    lane_u = iota((16, 128), 1) >> 4
    total = second[0:16]
    for u in range(1, UW // 2):
        total = jnp.where(lane_u == u, second[u * 16 : u * 16 + 16], total)
    total = fold(total, 16)
    diagonal = (iota((8, 128), 1) >> 4) == iota((8, 128), 0)
    pay = [
        jnp.sum(jnp.where(diagonal, total[h * 8 : h * 8 + 8], 0.0), axis=0, keepdims=True)
        for h in range(2)
    ]
    for s in sums:
        pay.append(fold(jnp.broadcast_to(s[:, :128] + s[:, 128:], (8, 128)), 16)[0:1])
    return code, slope, jnp.concatenate(pay, axis=0)


def put_codes(blocks, count, start, code_out):
    rows = pl.ds(start, count)
    for b, (low, high) in enumerate(mend_coarse(blocks)):
        code_out[b, rows, 0:128] = low.astype(BF16)
        code_out[b, rows, 128:256] = high.astype(BF16)


def inner_kernel(
    z, pixels, own_mask, weights, aux, taps_out, code_out, slope_out, pay_out, band_out, sh
):
    odd = lax.rem(lax.axis_index("wide"), 2)
    half = z.own // 2
    count = half - 16
    zeros = jnp.zeros((NB, 16, 256), F32)
    sh[:, 0:16, :] = zeros
    sh[:, half : half + 16, :] = zeros
    here = pl.ds(pl.multiple_of((1 - odd) * 16, 16), half)
    for b in range(NB):
        for h in range(2):
            sh[b, here, h * 128 : h * 128 + 128] = pixels[
                h * half : h * half + half, b * 128 : b * 128 + 128
            ].astype(F32)
    start = pl.multiple_of(odd * 32, 16)
    taps = [local_taps(sh, b, count, z.mb) for b in range(NB)]
    for b in range(NB):
        taps_out[b, pl.ds(start, count), :] = taps[b]
    kept = pl.ds(pl.multiple_of(odd * 16, 16), count)
    masks = jnp.concatenate([own_mask[kept, b * 128 : b * 128 + 128] for b in range(NB)], axis=0)
    bias = jnp.concatenate([aux[8:9], aux[8:9]], axis=1)
    banded = band_weights(weights[:, 0:256])
    band_out[...] = banded
    code, slope, pay = encode_rows(jnp.concatenate(taps, axis=0), banded, bias, masks, None)
    pay_out[...] = pay
    for b in range(NB):
        rs = slice(b * count, b * count + count)
        code_out[b, pl.ds(start, count), :] = code[rs].astype(BF16)
        slope_out[b, pl.ds(start, count), :] = slope[rs]


def encode_kernel(
    z, pixels, own_mask, halo, banded, aux, inner_pay, taps_in, code_in, slope_in,
    taps_out, code_out, slope_out, cot_out, pay_out,
    sh, pays, sem,
):
    odd = lax.rem(lax.axis_index("wide"), 2)
    half = z.own // 2
    count = 32
    channel_ok = jnp.tile(aux[40:56], (1, NB))
    halo_mask = dot(halo[0:16, z.span : z.span + HW], window_mask_columns())
    halo_pixels = dot(halo[:, 0 : z.span], window_columns())
    halo_x = halo_pixels[0 : z.halo] * jnp.tile(channel_ok, (2, 1))
    zeros = jnp.zeros((NB, 16, 256), F32)
    sh[:, 0:16, :] = zeros
    sh[:, 48:64, :] = zeros
    own_start = pl.multiple_of((1 - odd) * (half - 32), 16)
    own_there = pl.ds(pl.multiple_of(odd * 32, 16), 32)
    halo_there = pl.ds(pl.multiple_of((2 - odd) * 16, 16), 16)
    for b in range(NB):
        for h in range(2):
            cs = slice(b * 128, b * 128 + 128)
            own = pixels[pl.ds(pl.multiple_of(own_start + h * half, 16), 32), cs]
            sh[b, own_there, h * 128 : h * 128 + 128] = own.astype(F32)
            sh[b, halo_there, h * 128 : h * 128 + 128] = halo_x[h * 16 : h * 16 + 16, cs]
    start = pl.multiple_of((1 - odd) * (z.rows - count), 16)
    taps = [local_taps(sh, b, count, z.mb) for b in range(NB)]
    for b in range(NB):
        taps_out[b, pl.ds(start, count), :] = taps[b]
    edge_mask = own_mask[pl.ds(pl.multiple_of((1 - odd) * (half - 16), 16), 16), :].astype(F32)
    first = jnp.where(odd == 1, halo_mask, edge_mask)
    later = jnp.where(odd == 1, edge_mask, halo_mask)
    masks = jnp.concatenate(
        [x[:, b * 128 : b * 128 + 128] for b in range(NB) for x in (first, later)], axis=0
    ).astype(BF16)
    bias = jnp.concatenate([aux[8:9], aux[8:9]], axis=1)
    mine = ((iota((NB * count, 1), 0) >> 4) & 1) == odd
    code, slope, pay = encode_rows(jnp.concatenate(taps, axis=0), banded[...], bias, masks, mine)
    pay = pay + inner_pay[...]
    for i in range(pays.shape[0]):
        pays[i] = pay
    copy = pltpu.make_async_copy(pays, pay_out, sem.at[0])
    copy.start()
    for b in range(NB):
        slope_out[b, pl.ds(start, count), :] = slope[b * count : b * count + count]
    put_codes([code[b * count : b * count + count] for b in range(NB)], count, start, code_out)
    inner = z.rows - count
    inner_start = pl.multiple_of(odd * count, 16)
    put_codes(
        [code_in[b, pl.ds(inner_start, inner), :].astype(F32) for b in range(NB)],
        inner, inner_start, code_out,
    )
    near = halo_pixels[z.halo : z.sent] * channel_ok
    nothing = jnp.zeros((8, NB * 128), F32)
    for h in range(2):
        rows = near[h * 8 : h * 8 + 8]
        rows = [jnp.where(odd == 1, nothing, rows), jnp.where(odd == 1, rows, nothing)]
        cot_out[h * 16 : h * 16 + 16, :] = jnp.concatenate(rows, axis=0).astype(BF16)
    copy.wait()


def decode_kernel(
    z, cotangent, code, in_mask, halo_cot, weights, aux,
    sent_out, pay_out,
    sh, cot_frame,
):
    odd = lax.rem(lax.axis_index("wide"), 2)
    mine = pl.ds(lax.axis_index("section") * z.mb, z.mb)
    rows = z.rows
    put_frame(
        z, sh, [(code[b, :, 0:128].astype(F32), code[b, :, 128:256].astype(F32)) for b in range(NB)]
    )
    banded = band_weights(weights[:, 256:512])
    raws = spread(z, sh, banded)
    gather = gather_rows(z)
    columns = window_columns()
    own_cot = dot(dot(gather, cotangent[mine].reshape(z.own, z.span)).astype(BF16), columns)
    put_pixels(z, cot_frame, odd, own_cot * in_mask[...].astype(F32), halo_cot[...].astype(F32))
    mine_rows = own_rows(z, odd)
    u_local = (iota((1, 128), 1) >> 3) & (UW - 1)
    inner = mine_rows & (u_local >= 1) & (u_local <= UW - 2)
    grads = []
    bias_sum = jnp.zeros((1, 128), F32)
    for h in range(2):
        raw = raws[h] + aux[0:1]
        slope = jnp.exp(jnp.minimum(raw, 0.0))
        cs = slice(h * 128, h * 128 + 128)
        for b in range(NB):
            rs = slice(b * rows, b * rows + rows)
            grad = (cot_frame[b, 8 : 8 + rows, cs] * slope[rs]).astype(BF16).astype(F32)
            bias_sum = bias_sum + jnp.sum(jnp.where(inner, grad, 0.0), axis=0, keepdims=True)
            grads.append(grad)
    put_frame(z, sh, mend_fine([(grads[b], grads[NB + b]) for b in range(NB)]))
    taps = jnp.concatenate([fine_taps(z, sh, b) for b in range(NB)], axis=0)
    sent_out[...] = dot(taps, banded).astype(BF16).reshape(NB, rows, 256)
    mine = jnp.concatenate(
        [jnp.where(mine_rows, code[b].astype(F32), 0.0).astype(BF16) for b in range(NB)], axis=0
    )
    pay = pick_taps(dot(mine, taps, ((0,), (0,))))
    bias_sum = fold(jnp.broadcast_to(bias_sum, (16, 128)), 8)
    lane = iota((16, 128), 1)
    keep = (lane < 8) & ((lane >> 1) == iota((16, 128), 0))
    column = jnp.sum(jnp.where(keep, bias_sum, 0.0), axis=1, keepdims=True)
    pay_out[...] = jnp.where(lane >= 120, column, pay)


def whiten_kernel(
    z, stats, code, slope, sent, taps, decode_pay, aux,
    grad_out, pay_out, moments_out,
    pays, sem,
):
    odd = lax.rem(lax.axis_index("wide"), 2)
    rows = z.rows
    pay = jnp.sum(stats[...], axis=0)
    count = pay[3:4]
    mean = pay[2:3] / count
    diagonal = (iota((8, 128), 1) >> 4) == iota((8, 128), 0)
    second = jnp.concatenate(
        [
            fold(jnp.where(diagonal, jnp.broadcast_to(pay[h : h + 1], (8, 128)), 0.0), 16)
            for h in range(2)
        ],
        axis=0,
    )
    lane = iota((16, 128), 1)
    row = iota((16, 128), 0)
    wide_mean = jnp.broadcast_to(mean, (16, 128))
    mean_column = jnp.sum(jnp.where(lane == row, wide_mean, 0.0), axis=1, keepdims=True)
    cov = second / jnp.broadcast_to(count, (16, 128)) - mean_column * wide_mean
    moments_out[0:CCODE] = cov
    moments_out[CCODE:] = jnp.broadcast_to(mean, (8, 128))
    offset = cov - jnp.where((lane & 15) == row, 1.0, 0.0)
    pulled = jnp.sum(offset * mean_column, axis=0, keepdims=True)
    linear = whiten_weight * mean - 2.0 * whiten_weight * pulled
    linear = jnp.concatenate([linear, linear], axis=1)
    matrix = jnp.tile(2.0 * whiten_weight * offset, (8, 1))
    matrix = jnp.where((iota((128, 128), 0) >> 4) == (iota((128, 128), 1) >> 4), matrix, 0.0)
    high = matrix.astype(BF16)
    matrix = jnp.concatenate([high, (matrix - high.astype(F32)).astype(BF16)], axis=0)
    flat = code[...].reshape(z.frame, 256)
    flat = jnp.concatenate(
        [jnp.concatenate([x, x], axis=1) for x in (flat[:, 0:128], flat[:, 128:256])], axis=0
    )
    turned = dot(flat, matrix)
    turned = jnp.concatenate([turned[0 : z.frame], turned[z.frame :]], axis=1) + linear
    mine_rows = own_rows(z, odd)
    lane_u = iota((1, 256), 1) >> 4
    inner = mine_rows & (lane_u >= 1) & (lane_u <= UW - 2)
    last = HW // 2 - (NB - 1) * (UW - 2)
    blocks, mine = [], []
    bias_sum = jnp.zeros((1, 256), F32)
    for b in range(NB):
        signed = slope[b]
        pull = jnp.where(signed > 0, turned[b * rows : b * rows + rows], 0.0)
        grad = ((sent[b].astype(F32) + pull) * jnp.abs(signed)).astype(BF16).astype(F32)
        kept = jnp.where(inner & (lane_u <= last) if b == NB - 1 else inner, grad, 0.0)
        bias_sum = bias_sum + jnp.sum(kept, axis=0, keepdims=True)
        blocks.append(grad)
        mine.append(kept.astype(BF16))
    products = dot(
        jnp.concatenate(mine, axis=0), taps[...].reshape(z.frame, KS * 128), ((0,), (0,))
    )
    encode_pay = pick_taps(products)
    bias_sum = fold(jnp.broadcast_to(bias_sum[:, :128] + bias_sum[:, 128:], (16, 128)), 16)
    column = jnp.sum(jnp.where(lane == row, bias_sum, 0.0), axis=1, keepdims=True)
    decoded = decode_pay[...]
    biases = jnp.where((lane & 1) == 0, column, decoded)
    coarse = biases.astype(BF16).astype(F32)
    biases = jnp.where((lane & 2) == 0, coarse, biases - coarse)
    encode_pay = jnp.where(lane >= 120, biases, encode_pay)
    decoded = jnp.where(lane >= 120, biases, decoded)
    half = pays.shape[0] // 2
    for i in range(half):
        pays[i] = encode_pay.astype(BF16)
        pays[half + i] = decoded.astype(BF16)
    copy = pltpu.make_async_copy(pays, pay_out, sem.at[0])
    copy.start()
    for b, (low, high) in enumerate(mend_coarse(blocks)):
        grad_out[b, :, 0:128] = low.astype(BF16)
        grad_out[b, :, 128:256] = high.astype(BF16)
    copy.wait()


def picture(z, decodes, grad, code, in_mask, weights, aux, sh):
    odd = lax.rem(lax.axis_index("wide"), 2)
    rows = z.rows
    frames = [
        jnp.where(decodes, code[b].astype(F32), grad[b].astype(F32)) for b in range(NB)
    ]
    put_frame(z, sh, [(x[:, 0:128], x[:, 128:256]) for x in frames])
    chosen = jnp.where(decodes, weights[:, 256:512].astype(F32), weights[:, 0:256].astype(F32))
    raws = spread(z, sh, band_weights(chosen))
    for h in range(2):
        raw = raws[h] + aux[0:1]
        raw = jnp.where(raw > 0, raw, jnp.exp(jnp.minimum(raw, 0.0)) - 1.0)
        raw = jnp.where(decodes, raw, raws[h])
        for b in range(NB):
            sh[b, 8 : 8 + rows, h * 128 : h * 128 + 128] = raw[b * rows : b * rows + rows]
    flat = own_frame(z, odd, sh) * in_mask[...]
    native = dot(flat, unwindow_columns()).astype(BF16)
    return dot(scatter_rows(z), native).astype(BF16).reshape(z.mb, z.band, z.span)


def send_kernel(z, grad, code, in_mask, weights, aux, send_out, sh):
    decodes = lax.axis_index("section") == 0
    send_out[...] = picture(z, decodes, grad, code, in_mask, weights, aux, sh)


def keep_kernel(
    z, grad, code, in_mask, weights, aux, moments,
    pixels_out, onehot_out, mean_out, cov_out,
    sh, mine, means, covs, sems,
):
    section = lax.axis_index("section")
    means[...] = decay_rate * aux[16:17, 0:CCODE] + (1.0 - decay_rate) * moments[16:17, 0:CCODE]
    covs[...] = decay_rate * aux[24:40, 0:CCODE] + (1.0 - decay_rate) * moments[0:16, 0:CCODE]
    mine[...] = picture(z, section == 1, grad, code, in_mask, weights, aux, sh)
    copies = [
        pltpu.make_async_copy(source, target, sems.at[i])
        for i, (source, target) in enumerate(
            (
                (mine, pixels_out.at[0, pl.ds(section * z.mb, z.mb)]),
                (means, mean_out),
                (covs, cov_out),
            )
        )
    ]
    for copy in copies:
        copy.start()
    onehot_out[...] = tap_onehot()
    for copy in copies:
        copy.wait()


def total_kernel(z, parts, out):
    out[...] = jnp.sum(parts[...].astype(F32), axis=0)


def finish_kernel(
    z, sums, arrived, onehot, half_done, pixels_out, kernel_out, enc_out, dec_out,
    kernels, encs, decs, sems,
):
    there = z.micro - z.mb - lax.axis_index("section") * z.mb
    copies = [
        pltpu.make_async_copy(source, target, sems.at[i])
        for i, (source, target) in enumerate(
            (
                (arrived, pixels_out.at[0, pl.ds(there, z.mb)]),
                (encs, enc_out),
                (decs, dec_out),
                (kernels, kernel_out),
            )
        )
    ]
    copies[0].start()
    total = sums[...]
    chosen = dot(jnp.concatenate(split(total), axis=0), onehot[...])
    chosen = chosen[0:16] + chosen[16:32] + chosen[32:48]
    _, o = tap_target(iota((1, NK), 1))
    kernels[...] = jnp.sum(jnp.where(iota((16, NK), 0) == o, chosen, 0.0), axis=0, keepdims=True)
    copies[3].start()
    lane = iota((16, 128), 1)
    row = iota((16, 128), 0)
    for slot, out in ((120, encs), (121, decs)):
        chosen = (lane == slot) | (lane == slot + 2)
        column = jnp.sum(jnp.where(chosen, total, 0.0), axis=1, keepdims=True)
        flat = jnp.sum(jnp.where(lane == row, column, 0.0), axis=0, keepdims=True)
        out[...] = flat[:, 0 : out.shape[1]]
    copies[1].start()
    copies[2].start()
    for copy in copies:
        copy.wait()


VMEM = pl.BlockSpec(memory_space=pltpu.VMEM)
HBM = pl.BlockSpec(memory_space=pltpu.HBM)
PARAMS = pltpu.CompilerParams(vmem_limit_bytes=24 * 1024 * 1024)
DMA = pltpu.SemaphoreType.DMA


def shape(*dims, dtype=BF16):
    return jax.ShapeDtypeStruct(dims, dtype)


def shards(sections, wides):
    def run(
        fields, pixel_mask, channel_counts, kernels, enc_bias, dec_bias, cotangent, run_mean, run_cov
    ):
        z = Sizes(fields.shape, sections)
        assert 2 * z.band == HW and z.span == CIN * HW and z.mb == 4
        whole = (fields, pixel_mask, cotangent)
        (
            fields, cotangent, pixel_mask, kernels, channel_counts, enc_bias, dec_bias,
            run_mean, run_cov,
        ) = (
            pltpu.with_memory_space_constraint(x, pltpu.HBM)
            for x in (
                fields, cotangent, pixel_mask, kernels, channel_counts, enc_bias, dec_bias,
                run_mean, run_cov,
            )
        )
        swap = [(i, i ^ 1) for i in range(sections)]
        pair = [(i, i ^ 1) for i in range(wides)]
        frame = (NB, z.rows, 256)
        framed = pltpu.VMEM((NB, z.rows + 16, 256), F32)
        band_buf = pltpu.VMEM((z.mb, z.band, z.span), BF16)
        edge_buf = pltpu.VMEM((z.mb, 16, z.span), BF16)
        heavy = pl.CostEstimate(flops=4_000_000_000, bytes_accessed=4_000_000, transcendentals=0)

        def call(kernel, name, outs, ins, scratch, out_specs=None, cost=None, alias=None):
            return pl.pallas_call(
                lambda *refs: kernel(z, *refs),
                out_shape=outs,
                in_specs=ins,
                out_specs=out_specs or [VMEM] * len(outs),
                scratch_shapes=scratch,
                compiler_params=PARAMS,
                cost_estimate=cost,
                input_output_aliases=alias or {},
                name=name,
            )

        halo, kernel_own = call(
            edge_kernel,
            "edge",
            [shape(z.sent, z.span + HW), shape(COPIES, NK)],
            [HBM] * 4,
            [
                edge_buf,
                pltpu.VMEM((z.mb, 16, HW), jnp.int32),
                edge_buf,
                pltpu.VMEM((1, NK), BF16),
                DMA((4,)),
            ],
        )(fields, pixel_mask, cotangent, kernels)
        halo = lax.ppermute(halo, "wide", pair)
        kernel_other = lax.ppermute(kernel_own, "section", swap)
        pixels, in_mask, aux = call(
            prepare_kernel,
            "prepare",
            [
                shape(z.own, NB * 128),
                shape(z.own, NB * 128),
                shape(56, 128, dtype=F32),
            ],
            [VMEM] * 2 + [HBM] * 5,
            [
                pltpu.SMEM(channel_counts.shape, jnp.int32),
                pltpu.SMEM(enc_bias.shape, F32),
                pltpu.SMEM(dec_bias.shape, F32),
                pltpu.SMEM(run_mean.shape, F32),
                pltpu.VMEM(run_cov.shape, F32),
                DMA((5,)),
            ],
            cost=heavy,
        )(*whole[:2], channel_counts, enc_bias, dec_bias, run_mean, run_cov)
        (weights,) = call(taps_kernel, "taps", [shape(128, 512)], [VMEM] * 2, [])(
            kernel_own, kernel_other
        )
        coded = [shape(NB, z.rows, KS * 128), shape(*frame), shape(*frame, dtype=F32)]
        taps, code, slope, pay, banded = call(
            inner_kernel,
            "inner",
            coded + [shape(4, 128, dtype=F32), shape(KS * 128, 256)],
            [VMEM] * 4,
            [pltpu.VMEM((NB, z.own // 2 + 16, 256), F32)],
            cost=heavy,
        )(pixels, in_mask, weights, aux)
        taps, code, slope, halo_cot, pay = call(
            encode_kernel,
            "encode",
            coded + [shape(z.halo, NB * 128), shape(sections * wides, 4, 128, dtype=F32)],
            [VMEM] * 9,
            [
                pltpu.VMEM((NB, 64, 256), F32),
                pltpu.VMEM((sections * wides, 4, 128), F32),
                DMA((1,)),
            ],
            out_specs=[VMEM] * 4 + [HBM],
            alias={6: 0, 7: 1, 8: 2},
        )(pixels, in_mask, halo, banded, aux, pay, taps, code, slope)
        stats = lax.all_to_all(pay, ("section", "wide"), 0, 0)
        sent, decode_pay = call(
            decode_kernel,
            "decode",
            [shape(*frame), shape(CCODE, 128, dtype=F32)],
            [VMEM] * 6,
            [framed, framed],
            cost=heavy,
        )(whole[2], code, in_mask, halo_cot, weights, aux)
        grad, pay, moments = call(
            whiten_kernel,
            "whiten",
            [
                shape(*frame),
                shape(sections * wides, CCODE, 128),
                shape(CCODE + 8, 128, dtype=F32),
            ],
            [VMEM] * 7,
            [pltpu.VMEM((sections * wides, CCODE, 128), BF16), DMA((1,))],
            out_specs=[VMEM, HBM, VMEM],
            alias={3: 0},
        )(stats, code, slope, sent, taps, decode_pay, aux)
        parts = lax.all_to_all(pay, ("section", "wide"), 0, 0)
        (sending,) = call(
            send_kernel,
            "send",
            [shape(z.mb, z.band, z.span)],
            [VMEM] * 5,
            [framed],
            cost=heavy,
        )(grad, code, in_mask, weights, aux)
        arrived = lax.ppermute(sending, "section", swap)
        half_done, onehot, new_mean, new_cov = call(
            keep_kernel,
            "keep",
            [
                shape(1, z.micro, z.band, z.span),
                shape(128, NK),
                shape(1, CCODE, dtype=F32),
                shape(CCODE, CCODE, dtype=F32),
            ],
            [VMEM] * 6,
            [
                framed,
                band_buf,
                pltpu.VMEM((1, CCODE), F32),
                pltpu.VMEM((CCODE, CCODE), F32),
                DMA((3,)),
            ],
            out_specs=[HBM, VMEM, HBM, HBM],
            cost=heavy,
        )(grad, code, in_mask, weights, aux, moments)
        (sums,) = call(
            total_kernel,
            "total",
            [shape(CCODE, 128, dtype=F32)],
            [VMEM],
            [],
            cost=pl.CostEstimate(flops=100_000_000_000, bytes_accessed=0, transcendentals=0),
        )(parts)
        pixels_out, kernel_grads, enc_grad, dec_grad = call(
            finish_kernel,
            "finish",
            [
                shape(1, z.micro, z.band, z.span),
                shape(1, NK, dtype=F32),
                shape(1, CCODE, dtype=F32),
                shape(1, CIN, dtype=F32),
            ],
            [VMEM] * 3 + [HBM],
            [
                pltpu.VMEM((1, NK), F32),
                pltpu.VMEM((1, CCODE), F32),
                pltpu.VMEM((1, CIN), F32),
                DMA((4,)),
            ],
            out_specs=[HBM] * 4,
            alias={3: 0},
        )(sums, arrived, onehot, half_done)
        return (
            pixels_out,
            kernel_grads,
            enc_grad.reshape(CCODE),
            dec_grad.reshape(CIN),
            new_mean.reshape(CCODE),
            new_cov,
        )

    return run


def solution(mesh):
    in_specs = (
        P(None, "wide", None),
        P(None, "wide", None),
        P(),
        P("section", None),
        P(),
        P(),
        P(None, "wide", None),
        P(),
        P(),
    )
    out_specs = (P("section", None, "wide", None), P("section", None), P(), P(), P(), P())
    run = shards(mesh.shape["section"], mesh.shape["wide"])
    return jax.shard_map(run, mesh=mesh, in_specs=in_specs, out_specs=out_specs, check_vma=False)
```

```python
import jax
import jax.numpy as jnp
from jax import lax
from jax.experimental import pallas as pl
from jax.experimental.pallas import tpu as pltpu
from jax.sharding import PartitionSpec as P

CIN = 4
CCODE = 16
KS = 5
HW = 128

UW = 16
NB = 5
HALO = 8
NK = CCODE * CIN * KS * KS
COPIES = 32

decay_rate = 0.9
whiten_weight = 0.25

F32 = jnp.float32
BF16 = jnp.bfloat16


def iota(shape, dim):
    return lax.broadcasted_iota(jnp.int32, shape, dim)


def hot(mask):
    return jnp.where(mask, 1.0, 0.0).astype(BF16)


def dot(a, b, dims=((1,), (0,))):
    return lax.dot_general(a, b, (dims, ((), ())), preferred_element_type=F32)


def fold(x, unit):
    rolled = [x] + [pltpu.roll(x, step, 1) for step in range(unit, 128, unit)]
    while len(rolled) > 1:
        rolled = [sum(rolled[i : i + 2]) for i in range(0, len(rolled), 2)]
    return rolled[0]


def split(x):
    high = x.astype(BF16)
    rest = x - high.astype(F32)
    mid = rest.astype(BF16)
    return high, mid, (rest - mid.astype(F32)).astype(BF16)


class Sizes:
    def __init__(self, fields, sections):
        self.micro, self.band, self.span = fields
        self.sections = sections
        self.mb = self.micro // sections
        self.jf = self.band // 2 + HALO // 2
        self.rows = self.jf * self.mb
        self.own = self.mb * self.band
        self.halo = self.mb * HALO
        self.shift = self.mb.bit_length() - 1
        self.frame = NB * self.rows
        self.near = self.halo // 2
        self.sent = CIN * (self.halo + self.near) + self.near


def tap_target(n):
    o = (n * 5243) >> 19
    t = n - 100 * o
    c = (t * 1311) >> 15
    t = t - 25 * c
    k = (t * 205) >> 10
    l = t - 5 * k
    return (3 * k + (l >> 1)) * 8 + 2 * c + (l & 1), o


def tap_onehot():
    target, _ = tap_target(iota((1, NK), 1))
    return hot(iota((128, NK), 0) == target)


def row_target(z, row):
    half = z.own // 2
    parity = (row >= half).astype(jnp.int32)
    q = row - parity * half
    return (q & (z.mb - 1)) * z.band + 2 * (q >> z.shift) + parity


def gather_rows(z):
    return hot(iota((z.own, z.own), 1) == row_target(z, iota((z.own, 1), 0)))


def scatter_rows(z):
    return hot(iota((z.own, z.own), 0) == row_target(z, iota((1, z.own), 1)))


def pixel_target(lane, inner):
    u_local = (lane >> 3) & (UW - 1)
    u = (lane >> 7) * (UW - 2) + u_local - 1
    valid = (u >= 0) & (u < HW // 2)
    if inner:
        valid = valid & (u_local >= 1) & (u_local <= UW - 2)
    return 2 * u + (lane & 1), (lane >> 1) & 3, valid


def window_columns():
    col, c, valid = pixel_target(iota((1, NB * 128), 1), False)
    target = jnp.where(valid, c * HW + col, -1)
    return hot(iota((CIN * HW, NB * 128), 0) == target)


def unwindow_columns():
    col, c, valid = pixel_target(iota((NB * 128, 1), 0), True)
    target = jnp.where(valid, c * HW + col, -1)
    return hot(iota((NB * 128, CIN * HW), 1) == target)


def window_mask_columns():
    col, _, valid = pixel_target(iota((1, NB * 128), 1), False)
    return hot(iota((HW, NB * 128), 0) == jnp.where(valid, col, -1))


def code_mask_lanes():
    lane = iota((1, 256), 1)
    u_local = lane >> 4
    inner = (u_local >= 1) & (u_local <= UW - 2)
    return hot(iota((128, 256), 0) == jnp.where(inner, u_local * 8, -1))


def own_rows(z, odd):
    j = (iota((z.rows, 1), 0) >> z.shift) - odd * (HALO // 2)
    return (j >= 0) & (j < z.band // 2)


def places(z, odd):
    own = pl.multiple_of(odd * (z.halo // 2), 16)
    halo = pl.multiple_of((1 - odd) * (z.own // 2), 16)
    return own, halo


def mend_coarse(blocks):
    last = HW // 2 - (NB - 1) * (UW - 2)
    rows = blocks[0].shape[0]
    lane = iota((rows, 128), 1)
    halves = [(x[:, :128], x[:, 128:]) for x in blocks]
    done = []
    for b, (low, high) in enumerate(halves):
        before = pltpu.roll(halves[b - 1][1], 32, 1) if b else 0.0
        new_low = jnp.where(lane < 16, before, low)
        if b + 1 < NB:
            after = pltpu.roll(halves[b + 1][0], 96, 1)
            new_high = jnp.where(lane >= 112, after, high)
        else:
            new_high = jnp.where(lane < (last + 1) * 16 - 128, high, 0.0)
        done.append((new_low, new_high))
    return done


def mend_fine(halves):
    rows = halves[0][0].shape[0]
    lane = iota((rows, 128), 1)
    done = []
    for b in range(NB):
        pair = []
        for h in range(2):
            x = halves[b][h]
            before = pltpu.roll(halves[b - 1][h], 16, 1) if b else 0.0
            after = pltpu.roll(halves[b + 1][h], 112, 1) if b + 1 < NB else 0.0
            x = jnp.where(lane < 8, before, x)
            pair.append(jnp.where(lane >= 120, after, x))
        done.append(tuple(pair))
    return done


def pad_frame(z, sh):
    zeros = jnp.zeros((NB, 8, 256), F32)
    sh[:, 0:8, :] = zeros
    sh[:, 8 + z.rows : 16 + z.rows, :] = zeros


def put_frame(z, sh, halves):
    pad_frame(z, sh)
    for b, (low, high) in enumerate(halves):
        sh[b, 8 : 8 + z.rows, 0:128] = low
        sh[b, 8 : 8 + z.rows, 128:256] = high


def put_pixels(z, sh, odd, own, halo):
    pad_frame(z, sh)
    for start, part in zip(places(z, odd), (own, halo)):
        half = part.shape[0] // 2
        rows = pl.ds(pl.multiple_of(8 + start, 8), half)
        for b in range(NB):
            for h in range(2):
                sh[b, rows, h * 128 : h * 128 + 128] = part[
                    h * half : h * half + half, b * 128 : b * 128 + 128
                ]


def fine_taps(z, sh, b):
    up = sh[b, 8 - z.mb : 8 - z.mb + z.rows, :]
    here = sh[b, 8 : 8 + z.rows, :]
    down = sh[b, 8 + z.mb : 8 + z.mb + z.rows, 0:128]
    return jnp.concatenate([up, here, down], axis=1).astype(BF16)


def coarse_taps(z, sh, b):
    down = sh[b, 8 + z.mb : 8 + z.mb + z.rows, :]
    here = sh[b, 8 : 8 + z.rows, :]
    up = sh[b, 8 - z.mb : 8 - z.mb + z.rows, :]
    return [x.astype(BF16) for x in (down, here, up)]


def spread(z, sh, weights):
    taps = [coarse_taps(z, sh, b) for b in range(NB)]
    down, here, up = (jnp.concatenate([t[i] for t in taps], axis=0) for i in range(3))
    nt = ((1,), (1,))
    out = dot(down, weights[0:256], nt) + dot(here, weights[256:512], nt)
    extra = dot(up, weights[512:640], nt)
    return out[:, :128] + extra, out[:, 128:]


def pick_taps(grads):
    lane = iota((CCODE, 128), 1)
    place = lane >> 3
    pieces = []
    for k in range(KS):
        for shift in (-1, 0, 1):
            total = jnp.zeros((CCODE, 128), F32)
            for u in range(1, UW - 1):
                part = grads[u * 16 : u * 16 + 16, k * 128 : k * 128 + 128]
                total = jnp.where(place == u + shift, part, total)
            pieces.append(total)
    pieces.append(jnp.zeros((CCODE, 128), F32))
    block = lane >> 5
    fours = []
    for first in range(4):
        group = pieces[first::4]
        parts = []
        for j in range(4):
            x = group[j]
            for t in range(1, 4):
                x = jnp.where(block == t, group[(t + j) & 3], x)
            parts.append(x)
        fours.append(
            (parts[0] + pltpu.roll(parts[1], 32, 1))
            + (pltpu.roll(parts[2], 64, 1) + pltpu.roll(parts[3], 96, 1))
        )
    inner = place & 3
    total = None
    for j in range(4):
        x = fours[j]
        for t in range(1, 4):
            x = jnp.where(inner == t, fours[(t + j) & 3], x)
        if j:
            x = jnp.where(inner >= j, pltpu.roll(x, 8 * j, 1), pltpu.roll(x, 96 + 8 * j, 1))
        total = x if total is None else total + x
    return total


def own_frame(z, odd, sh):
    start, _ = places(z, odd)
    half = z.own // 2
    rows = pl.ds(pl.multiple_of(8 + start, 8), half)
    flat = jnp.concatenate(
        [
            jnp.concatenate(
                [sh[b, rows, h * 128 : h * 128 + 128] for b in range(NB)], axis=1
            )
            for h in range(2)
        ],
        axis=0,
    )
    return flat.astype(BF16)


def kernel_rows(flat):
    taps = CIN * KS * KS
    pad = jnp.zeros((1, 256 - NK % 128), F32)
    flat = jnp.concatenate([flat, pad], axis=1)
    lane = iota((1, 128), 1)
    row = iota((CCODE, 128), 0)
    rows = jnp.zeros((CCODE, 128), F32)
    for o in range(CCODE):
        chunk, shift = divmod(o * taps, 128)
        x = flat[:, chunk * 128 : chunk * 128 + 128]
        if shift:
            after = flat[:, chunk * 128 + 128 : chunk * 128 + 256]
            x = jnp.where(
                lane < 128 - shift,
                pltpu.roll(x, 128 - shift, 1),
                pltpu.roll(after, 128 - shift, 1),
            )
        rows = jnp.where(row == o, jnp.broadcast_to(x, (CCODE, 128)), rows)
    return rows


def spread_taps(kernel_pair):
    taps = CIN * KS * KS
    rows = jnp.concatenate([kernel_rows(x) for x in kernel_pair for _ in range(8)], axis=0)
    lane = iota((1, 128), 1)
    target, _ = tap_target(jnp.minimum(lane, taps - 1))
    slots = hot(iota((128, 128), 0) == jnp.where(lane < taps, target, -1))
    wide = dot(slots, rows.T.astype(BF16)).astype(BF16)
    halves = [wide[:, 0:128], wide[:, 128:256]]
    return jnp.concatenate([x for x in halves for _ in range(2)], axis=1)


def band_weights(wide_taps):
    wide_taps = wide_taps.astype(F32)
    row_u = iota((128, 256), 0) >> 3
    lane_u = iota((128, 256), 1) >> 4
    masks = [row_u == lane_u + shift for shift in (-1, 0, 1)]
    parts = []
    for k in range(KS):
        total = jnp.zeros((128, 256), F32)
        for i, mask in enumerate(masks):
            q = 3 * k + i
            piece = wide_taps[8 * q : 8 * q + 8]
            piece = jnp.broadcast_to(piece[None], (16, 8, 256)).reshape(128, 256)
            total = jnp.where(mask, piece, total)
        parts.append(total.astype(BF16))
    return jnp.concatenate(parts, axis=0)


def edge_kernel(
    z, fields, mask, cotangent, kernel, out, kernel_out,
    field_buf, mask_buf, cot_buf, kernel_buf, sems,
):
    odd = lax.rem(lax.axis_index("wide"), 2)
    first = lax.axis_index("section") * z.mb
    start = pl.multiple_of((1 - odd) * (z.band - 16), 16)
    copies = [
        pltpu.make_async_copy(
            source.at[pl.ds(first, z.mb), pl.ds(start, 16), :], buf, sems.at[i]
        )
        for i, (source, buf) in enumerate(
            ((fields, field_buf), (mask, mask_buf), (cotangent, cot_buf))
        )
    ]
    copies.append(pltpu.make_async_copy(kernel, kernel_buf, sems.at[3]))
    for copy in copies:
        copy.start()
    for copy in copies:
        copy.wait()
    kernel_out[...] = jnp.broadcast_to(kernel_buf[...].astype(F32), (COPIES, NK)).astype(BF16)

    def beside(buf):
        rows = buf[...].astype(F32)
        return jnp.where(odd == 1, rows[:, :HALO], rows[:, HALO:])

    def ordered(rows, firsts):
        return jnp.concatenate(
            [rows[:, j + h] for h in range(2) for j in firsts], axis=0
        ).astype(BF16)

    mask_rows = beside(mask_buf)
    allowed = jnp.concatenate([mask_rows] * CIN, axis=2)
    every, half = range(0, HALO, 2), range(0, HALO // 2, 2)
    near = beside(cot_buf) * allowed
    near = jnp.where(odd == 1, near[:, : HALO // 2], near[:, HALO // 2 :])
    pieces = ordered(beside(field_buf) * allowed, every), ordered(near, half)
    start = 0
    for piece in pieces:
        count = piece.shape[0]
        for c in range(CIN):
            out[start : start + count, :] = piece[:, c * HW : c * HW + HW]
            start += count
    out[start : z.sent, :] = ordered(mask_rows, every)[0 : z.near]


def prepare_kernel(
    z, fields, mask, counts, enc_bias, dec_bias, run_mean, run_cov,
    pixels_out, inmask_out, aux_out,
    count_buf, enc_buf, dec_buf, mean_buf, cov_buf, sems,
):
    section = lax.axis_index("section")
    wide = lax.axis_index("wide")
    first = section * z.mb
    mine_rows = pl.ds(first, z.mb)
    copies = [
        pltpu.make_async_copy(source, buf, sems.at[i])
        for i, (source, buf) in enumerate(
            (
                (counts, count_buf),
                (enc_bias, enc_buf),
                (dec_bias, dec_buf),
                (run_mean, mean_buf),
                (run_cov, cov_buf),
            )
        )
    ]
    for copy in copies:
        copy.start()
    gather = gather_rows(z)
    columns = window_columns()
    mask_columns = window_mask_columns()
    pixel_mask = mask[mine_rows].astype(F32).astype(BF16).reshape(z.own, HW)
    pixels = fields[mine_rows].reshape(z.own, z.span)
    framed = dot(gather, jnp.concatenate([pixel_mask, pixels], axis=1)).astype(BF16)
    in_mask = dot(framed[:, 0:HW], mask_columns)
    windowed = dot(framed[:, HW:], columns)
    for copy in copies:
        copy.wait()
    lane = iota((8, 128), 1)
    dec_row = jnp.zeros((8, 128), F32)
    for c in range(CIN):
        dec_row = jnp.where(((lane >> 1) & 3) == c, dec_buf[c], dec_row)
    enc_row = jnp.zeros((8, 128), F32)
    mean_row = jnp.zeros((8, 128), F32)
    for o in range(CCODE):
        enc_row = jnp.where((lane & 15) == o, enc_buf[o], enc_row)
        mean_row = jnp.where((lane & 15) == o, mean_buf[o], mean_row)
    aux_out[0:8] = dec_row
    aux_out[8:16] = enc_row
    aux_out[16:24] = mean_row
    aux_out[24:40] = jnp.zeros((16, 128), F32)
    aux_out[24:40, 0:CCODE] = cov_buf[...]
    field_now = wide * z.band // HW
    micro = iota((16, 128), 0) & (z.mb - 1)
    count = jnp.zeros((16, 128), jnp.int32)
    for m in range(z.mb):
        count = jnp.where(micro == m, count_buf[first + m, field_now], count)
    channel_ok = jnp.where(((iota((16, 128), 1) >> 1) & 3) < count, 1.0, 0.0)
    aux_out[40:56] = channel_ok
    in_mask = in_mask * jnp.tile(channel_ok, (z.own // 16, NB))
    inmask_out[...] = in_mask.astype(BF16)
    pixels_out[...] = (windowed * in_mask).astype(BF16)


def taps_kernel(z, kernel_own, kernel_other, weights_out):
    mine, other = (x[0:16].astype(F32)[0:1] for x in (kernel_own, kernel_other))
    leads = lax.axis_index("section") == 0
    weights_out[...] = spread_taps((jnp.where(leads, mine, other), jnp.where(leads, other, mine)))


def local_taps(sh, b, rows, step):
    up = sh[b, 16 - step : 16 - step + rows, :]
    here = sh[b, 16 : 16 + rows, :]
    down = sh[b, 16 + step : 16 + step + rows, 0:128]
    return jnp.concatenate([up, here, down], axis=1).astype(BF16)


def encode_rows(taps, banded, bias, masks, mine):
    code_mask = dot(masks, code_mask_lanes())
    pre = dot(taps, banded) + bias
    slope = jnp.exp(jnp.minimum(pre, 0.0))
    code = jnp.where(pre > 0, pre, slope - 1.0).astype(BF16).astype(F32)
    slope = jnp.where(code_mask > 0.5, slope, -slope)
    allowed = code_mask if mine is None else jnp.where(mine, code_mask, 0.0)
    weighted = code * allowed
    halves = [
        jnp.concatenate([x[:, 0:128], x[:, 128:256]], axis=0).astype(BF16) for x in (weighted, code)
    ]
    second = dot(*halves, ((0,), (0,)))
    sums = [jnp.sum(x, axis=0, keepdims=True) for x in (weighted, allowed)]
    lane_u = iota((16, 128), 1) >> 4
    total = second[0:16]
    for u in range(1, UW // 2):
        total = jnp.where(lane_u == u, second[u * 16 : u * 16 + 16], total)
    total = fold(total, 16)
    diagonal = (iota((8, 128), 1) >> 4) == iota((8, 128), 0)
    pay = [
        jnp.sum(jnp.where(diagonal, total[h * 8 : h * 8 + 8], 0.0), axis=0, keepdims=True)
        for h in range(2)
    ]
    for s in sums:
        pay.append(fold(jnp.broadcast_to(s[:, :128] + s[:, 128:], (8, 128)), 16)[0:1])
    return code, slope, jnp.concatenate(pay, axis=0)


def inner_kernel(
    z, pixels, own_mask, weights, aux, taps_out, code_out, slope_out, pay_out, band_out, sh
):
    odd = lax.rem(lax.axis_index("wide"), 2)
    half = z.own // 2
    count = half - 16
    zeros = jnp.zeros((NB, 16, 256), F32)
    sh[:, 0:16, :] = zeros
    sh[:, half : half + 16, :] = zeros
    here = pl.ds(pl.multiple_of((1 - odd) * 16, 16), half)
    for b in range(NB):
        for h in range(2):
            sh[b, here, h * 128 : h * 128 + 128] = pixels[
                h * half : h * half + half, b * 128 : b * 128 + 128
            ].astype(F32)
    start = pl.multiple_of(odd * 32, 16)
    taps = [local_taps(sh, b, count, z.mb) for b in range(NB)]
    for b in range(NB):
        taps_out[b, pl.ds(start, count), :] = taps[b]
    kept = pl.ds(pl.multiple_of(odd * 16, 16), count)
    masks = jnp.concatenate([own_mask[kept, b * 128 : b * 128 + 128] for b in range(NB)], axis=0)
    bias = jnp.concatenate([aux[8:9], aux[8:9]], axis=1)
    banded = band_weights(weights[:, 0:256])
    band_out[...] = banded
    code, slope, pay = encode_rows(jnp.concatenate(taps, axis=0), banded, bias, masks, None)
    pay_out[...] = pay
    for b in range(NB):
        rs = slice(b * count, b * count + count)
        code_out[b, pl.ds(start, count), :] = code[rs].astype(BF16)
        slope_out[b, pl.ds(start, count), :] = slope[rs]


def encode_kernel(
    z, pixels, own_mask, halo, banded, aux, inner_pay, taps_in, code_in, slope_in,
    taps_out, code_out, slope_out, cot_out, pay_out,
    sh,
):
    odd = lax.rem(lax.axis_index("wide"), 2)
    half = z.own // 2
    count = 32
    channel_ok = jnp.tile(aux[40:56], (1, NB))
    middle, end = CIN * z.halo, CIN * (z.halo + z.near)
    halo_mask = dot(halo[end : z.sent, :], window_mask_columns())
    halo_rows = [
        jnp.concatenate([halo[i : i + count, :] for i in range(start, stop, count)], axis=1)
        for start, stop, count in ((0, middle, z.halo), (middle, end, z.near))
    ]
    halo_pixels = dot(jnp.concatenate(halo_rows, axis=0), window_columns())
    halo_x = halo_pixels[0 : z.halo] * jnp.tile(channel_ok, (2, 1))
    zeros = jnp.zeros((NB, 16, 256), F32)
    sh[:, 0:16, :] = zeros
    sh[:, 48:64, :] = zeros
    own_start = pl.multiple_of((1 - odd) * (half - 32), 16)
    own_there = pl.ds(pl.multiple_of(odd * 32, 16), 32)
    halo_there = pl.ds(pl.multiple_of((2 - odd) * 16, 16), 16)
    for b in range(NB):
        for h in range(2):
            cs = slice(b * 128, b * 128 + 128)
            own = pixels[pl.ds(pl.multiple_of(own_start + h * half, 16), 32), cs]
            sh[b, own_there, h * 128 : h * 128 + 128] = own.astype(F32)
            sh[b, halo_there, h * 128 : h * 128 + 128] = halo_x[h * 16 : h * 16 + 16, cs]
    start = pl.multiple_of((1 - odd) * (z.rows - count), 16)
    taps = [local_taps(sh, b, count, z.mb) for b in range(NB)]
    for b in range(NB):
        taps_out[b, pl.ds(start, count), :] = taps[b]
    edge_mask = own_mask[pl.ds(pl.multiple_of((1 - odd) * (half - 16), 16), 16), :].astype(F32)
    first = jnp.where(odd == 1, halo_mask, edge_mask)
    later = jnp.where(odd == 1, edge_mask, halo_mask)
    masks = jnp.concatenate(
        [x[:, b * 128 : b * 128 + 128] for b in range(NB) for x in (first, later)], axis=0
    ).astype(BF16)
    bias = jnp.concatenate([aux[8:9], aux[8:9]], axis=1)
    mine = ((iota((NB * count, 1), 0) >> 4) & 1) == odd
    code, slope, pay = encode_rows(jnp.concatenate(taps, axis=0), banded[...], bias, masks, mine)
    pay = pay + inner_pay[...]
    pay_out[...] = pay
    for b in range(NB):
        rs = slice(b * count, b * count + count)
        code_out[b, pl.ds(start, count), :] = code[rs].astype(BF16)
        slope_out[b, pl.ds(start, count), :] = slope[rs]
    near = halo_pixels[z.halo : z.halo + z.near] * channel_ok
    nothing = jnp.zeros((8, NB * 128), F32)
    for h in range(2):
        rows = near[h * 8 : h * 8 + 8]
        rows = [jnp.where(odd == 1, nothing, rows), jnp.where(odd == 1, rows, nothing)]
        cot_out[h * 16 : h * 16 + 16, :] = jnp.concatenate(rows, axis=0).astype(BF16)


def decode_kernel(
    z, cotangent, code, in_mask, halo_cot, weights, aux,
    sent_out, pay_out,
    sh, cot_frame,
):
    odd = lax.rem(lax.axis_index("wide"), 2)
    mine = pl.ds(lax.axis_index("section") * z.mb, z.mb)
    rows = z.rows
    put_frame(z, sh, mend_coarse([code[b].astype(F32) for b in range(NB)]))
    banded = band_weights(weights[:, 256:512])
    raws = spread(z, sh, banded)
    gather = gather_rows(z)
    columns = window_columns()
    own_cot = dot(dot(gather, cotangent[mine].reshape(z.own, z.span)).astype(BF16), columns)
    put_pixels(z, cot_frame, odd, own_cot * in_mask[...].astype(F32), halo_cot[...].astype(F32))
    mine_rows = own_rows(z, odd)
    u_local = (iota((1, 128), 1) >> 3) & (UW - 1)
    inner = mine_rows & (u_local >= 1) & (u_local <= UW - 2)
    grads = []
    bias_sum = jnp.zeros((1, 128), F32)
    for h in range(2):
        raw = raws[h] + aux[0:1]
        slope = jnp.exp(jnp.minimum(raw, 0.0))
        cs = slice(h * 128, h * 128 + 128)
        for b in range(NB):
            rs = slice(b * rows, b * rows + rows)
            grad = (cot_frame[b, 8 : 8 + rows, cs] * slope[rs]).astype(BF16).astype(F32)
            bias_sum = bias_sum + jnp.sum(jnp.where(inner, grad, 0.0), axis=0, keepdims=True)
            grads.append(grad)
    put_frame(z, sh, mend_fine([(grads[b], grads[NB + b]) for b in range(NB)]))
    taps = jnp.concatenate([fine_taps(z, sh, b) for b in range(NB)], axis=0)
    sent_out[...] = dot(taps, banded).astype(BF16).reshape(NB, rows, 256)
    last = HW // 2 - (NB - 1) * (UW - 2)
    within = mine_rows & ((iota((1, 256), 1) >> 4) <= last)
    mine = jnp.concatenate(
        [
            jnp.where(within if b == NB - 1 else mine_rows, code[b].astype(F32), 0.0).astype(BF16)
            for b in range(NB)
        ],
        axis=0,
    )
    pay = pick_taps(dot(mine, taps, ((0,), (0,))))
    bias_sum = fold(jnp.broadcast_to(bias_sum, (16, 128)), 8)
    lane = iota((16, 128), 1)
    keep = (lane < 8) & ((lane >> 1) == iota((16, 128), 0))
    column = jnp.sum(jnp.where(keep, bias_sum, 0.0), axis=1, keepdims=True)
    pay_out[...] = jnp.where(lane >= 120, column, pay)


def whiten_kernel(
    z, stats, code, slope, sent, taps, decode_pay, aux,
    grad_out, pay_out, moments_out,
):
    odd = lax.rem(lax.axis_index("wide"), 2)
    rows = z.rows
    pay = jnp.sum(stats[...], axis=0)
    count = pay[3:4]
    mean = pay[2:3] / count
    diagonal = (iota((8, 128), 1) >> 4) == iota((8, 128), 0)
    second = jnp.concatenate(
        [
            fold(jnp.where(diagonal, jnp.broadcast_to(pay[h : h + 1], (8, 128)), 0.0), 16)
            for h in range(2)
        ],
        axis=0,
    )
    lane = iota((16, 128), 1)
    row = iota((16, 128), 0)
    wide_mean = jnp.broadcast_to(mean, (16, 128))
    mean_column = jnp.sum(jnp.where(lane == row, wide_mean, 0.0), axis=1, keepdims=True)
    cov = second / jnp.broadcast_to(count, (16, 128)) - mean_column * wide_mean
    moments_out[0:CCODE] = cov
    moments_out[CCODE:] = jnp.broadcast_to(mean, (8, 128))
    offset = cov - jnp.where((lane & 15) == row, 1.0, 0.0)
    pulled = jnp.sum(offset * mean_column, axis=0, keepdims=True)
    linear = whiten_weight * mean - 2.0 * whiten_weight * pulled
    linear = jnp.concatenate([linear, linear], axis=1)
    matrix = jnp.tile(2.0 * whiten_weight * offset, (8, 1))
    matrix = jnp.where((iota((128, 128), 0) >> 4) == (iota((128, 128), 1) >> 4), matrix, 0.0)
    high = matrix.astype(BF16)
    matrix = jnp.concatenate([high, (matrix - high.astype(F32)).astype(BF16)], axis=0)
    flat = code[...].reshape(z.frame, 256)
    flat = jnp.concatenate(
        [jnp.concatenate([x, x], axis=1) for x in (flat[:, 0:128], flat[:, 128:256])], axis=0
    )
    turned = dot(flat, matrix)
    turned = jnp.concatenate([turned[0 : z.frame], turned[z.frame :]], axis=1) + linear
    mine_rows = own_rows(z, odd)
    lane_u = iota((1, 256), 1) >> 4
    inner = mine_rows & (lane_u >= 1) & (lane_u <= UW - 2)
    last = HW // 2 - (NB - 1) * (UW - 2)
    blocks, mine = [], []
    bias_sum = jnp.zeros((1, 256), F32)
    for b in range(NB):
        signed = slope[b]
        pull = jnp.where(signed > 0, turned[b * rows : b * rows + rows], 0.0)
        grad = ((sent[b].astype(F32) + pull) * jnp.abs(signed)).astype(BF16).astype(F32)
        kept = jnp.where(inner & (lane_u <= last) if b == NB - 1 else inner, grad, 0.0)
        bias_sum = bias_sum + jnp.sum(kept, axis=0, keepdims=True)
        blocks.append(grad)
        mine.append(kept.astype(BF16))
    products = dot(
        jnp.concatenate(mine, axis=0), taps[...].reshape(z.frame, KS * 128), ((0,), (0,))
    )
    encode_pay = pick_taps(products)
    bias_sum = fold(jnp.broadcast_to(bias_sum[:, :128] + bias_sum[:, 128:], (16, 128)), 16)
    column = jnp.sum(jnp.where(lane == row, bias_sum, 0.0), axis=1, keepdims=True)
    decoded = decode_pay[...]
    biases = jnp.where((lane & 1) == 0, column, decoded)
    coarse = biases.astype(BF16).astype(F32)
    biases = jnp.where((lane & 2) == 0, coarse, biases - coarse)
    encode_pay = jnp.where(lane >= 120, biases, encode_pay)
    decoded = jnp.where(lane >= 120, biases, decoded)
    pay_out[0] = encode_pay.astype(BF16)
    pay_out[1] = decoded.astype(BF16)
    for b, (low, high) in enumerate(mend_coarse(blocks)):
        grad_out[b, :, 0:128] = low.astype(BF16)
        grad_out[b, :, 128:256] = high.astype(BF16)


def picture(z, decodes, grad, code, in_mask, weights, aux, sh):
    odd = lax.rem(lax.axis_index("wide"), 2)
    rows = z.rows
    frames = [
        jnp.where(decodes, code[b].astype(F32), grad[b].astype(F32)) for b in range(NB)
    ]
    put_frame(z, sh, mend_coarse(frames))
    chosen = jnp.where(decodes, weights[:, 256:512].astype(F32), weights[:, 0:256].astype(F32))
    raws = spread(z, sh, band_weights(chosen))
    for h in range(2):
        raw = raws[h] + aux[0:1]
        raw = jnp.where(raw > 0, raw, jnp.exp(jnp.minimum(raw, 0.0)) - 1.0)
        raw = jnp.where(decodes, raw, raws[h])
        for b in range(NB):
            sh[b, 8 : 8 + rows, h * 128 : h * 128 + 128] = raw[b * rows : b * rows + rows]
    flat = own_frame(z, odd, sh) * in_mask[...]
    native = dot(flat, unwindow_columns()).astype(BF16)
    return dot(scatter_rows(z), native).astype(BF16).reshape(z.mb, z.band, z.span)


def send_kernel(z, grad, code, in_mask, weights, aux, send_out, sh):
    decodes = lax.axis_index("section") == 0
    send_out[...] = picture(z, decodes, grad, code, in_mask, weights, aux, sh)


def keep_kernel(
    z, grad, code, in_mask, weights, aux, moments,
    pixels_out, onehot_out, mean_out, cov_out,
    sh, mine, means, covs, sems,
):
    section = lax.axis_index("section")
    means[...] = decay_rate * aux[16:17, 0:CCODE] + (1.0 - decay_rate) * moments[16:17, 0:CCODE]
    covs[...] = decay_rate * aux[24:40, 0:CCODE] + (1.0 - decay_rate) * moments[0:16, 0:CCODE]
    mine[...] = picture(z, section == 1, grad, code, in_mask, weights, aux, sh)
    copies = [
        pltpu.make_async_copy(source, target, sems.at[i])
        for i, (source, target) in enumerate(
            (
                (mine, pixels_out.at[0, pl.ds(section * z.mb, z.mb)]),
                (means, mean_out),
                (covs, cov_out),
            )
        )
    ]
    for copy in copies:
        copy.start()
    onehot_out[...] = tap_onehot()
    for copy in copies:
        copy.wait()


def total_kernel(z, parts, out):
    out[...] = jnp.sum(parts[...].astype(F32), axis=0)


def finish_kernel(
    z, sums, arrived, onehot, half_done, pixels_out, kernel_out, enc_out, dec_out,
    kernels, encs, decs, sems,
):
    there = z.micro - z.mb - lax.axis_index("section") * z.mb
    copies = [
        pltpu.make_async_copy(source, target, sems.at[i])
        for i, (source, target) in enumerate(
            (
                (arrived, pixels_out.at[0, pl.ds(there, z.mb)]),
                (encs, enc_out),
                (decs, dec_out),
                (kernels, kernel_out),
            )
        )
    ]
    copies[0].start()
    total = sums[...]
    chosen = dot(jnp.concatenate(split(total), axis=0), onehot[...])
    chosen = chosen[0:16] + chosen[16:32] + chosen[32:48]
    _, o = tap_target(iota((1, NK), 1))
    kernels[...] = jnp.sum(jnp.where(iota((16, NK), 0) == o, chosen, 0.0), axis=0, keepdims=True)
    copies[3].start()
    lane = iota((16, 128), 1)
    row = iota((16, 128), 0)
    for slot, out in ((120, encs), (121, decs)):
        chosen = (lane == slot) | (lane == slot + 2)
        column = jnp.sum(jnp.where(chosen, total, 0.0), axis=1, keepdims=True)
        flat = jnp.sum(jnp.where(lane == row, column, 0.0), axis=0, keepdims=True)
        out[...] = flat[:, 0 : out.shape[1]]
    copies[1].start()
    copies[2].start()
    for copy in copies:
        copy.wait()


VMEM = pl.BlockSpec(memory_space=pltpu.VMEM)
HBM = pl.BlockSpec(memory_space=pltpu.HBM)
PARAMS = pltpu.CompilerParams(vmem_limit_bytes=24 * 1024 * 1024)
DMA = pltpu.SemaphoreType.DMA


def shape(*dims, dtype=BF16):
    return jax.ShapeDtypeStruct(dims, dtype)


def shards(sections, wides):
    def run(
        fields, pixel_mask, channel_counts, kernels, enc_bias, dec_bias, cotangent, run_mean, run_cov
    ):
        z = Sizes(fields.shape, sections)
        assert 2 * z.band == HW and z.span == CIN * HW and z.mb == 4
        whole = (fields, pixel_mask, cotangent)
        (
            fields, cotangent, pixel_mask, kernels, channel_counts, enc_bias, dec_bias,
            run_mean, run_cov,
        ) = (
            pltpu.with_memory_space_constraint(x, pltpu.HBM)
            for x in (
                fields, cotangent, pixel_mask, kernels, channel_counts, enc_bias, dec_bias,
                run_mean, run_cov,
            )
        )
        swap = [(i, i ^ 1) for i in range(sections)]
        pair = [(i, i ^ 1) for i in range(wides)]
        frame = (NB, z.rows, 256)
        framed = pltpu.VMEM((NB, z.rows + 16, 256), F32)
        band_buf = pltpu.VMEM((z.mb, z.band, z.span), BF16)
        edge_buf = pltpu.VMEM((z.mb, 16, z.span), BF16)
        heavy = pl.CostEstimate(flops=4_000_000_000, bytes_accessed=4_000_000, transcendentals=0)

        def call(kernel, name, outs, ins, scratch, out_specs=None, cost=None, alias=None):
            return pl.pallas_call(
                lambda *refs: kernel(z, *refs),
                out_shape=outs,
                in_specs=ins,
                out_specs=out_specs or [VMEM] * len(outs),
                scratch_shapes=scratch,
                compiler_params=PARAMS,
                cost_estimate=cost,
                input_output_aliases=alias or {},
                name=name,
            )

        halo, kernel_own = call(
            edge_kernel,
            "edge",
            [shape(z.sent, HW), shape(COPIES, NK)],
            [HBM] * 4,
            [
                edge_buf,
                pltpu.VMEM((z.mb, 16, HW), jnp.int32),
                edge_buf,
                pltpu.VMEM((1, NK), BF16),
                DMA((4,)),
            ],
        )(fields, pixel_mask, cotangent, kernels)
        halo = lax.ppermute(halo, "wide", pair)
        kernel_other = lax.ppermute(kernel_own, "section", swap)
        pixels, in_mask, aux = call(
            prepare_kernel,
            "prepare",
            [
                shape(z.own, NB * 128),
                shape(z.own, NB * 128),
                shape(56, 128, dtype=F32),
            ],
            [VMEM] * 2 + [HBM] * 5,
            [
                pltpu.SMEM(channel_counts.shape, jnp.int32),
                pltpu.SMEM(enc_bias.shape, F32),
                pltpu.SMEM(dec_bias.shape, F32),
                pltpu.SMEM(run_mean.shape, F32),
                pltpu.VMEM(run_cov.shape, F32),
                DMA((5,)),
            ],
            cost=heavy,
        )(*whole[:2], channel_counts, enc_bias, dec_bias, run_mean, run_cov)
        (weights,) = call(taps_kernel, "taps", [shape(128, 512)], [VMEM] * 2, [])(
            kernel_own, kernel_other
        )
        coded = [shape(NB, z.rows, KS * 128), shape(*frame), shape(*frame, dtype=F32)]
        taps, code, slope, pay, banded = call(
            inner_kernel,
            "inner",
            coded + [shape(4, 128, dtype=F32), shape(KS * 128, 256)],
            [VMEM] * 4,
            [pltpu.VMEM((NB, z.own // 2 + 16, 256), F32)],
            cost=heavy,
        )(pixels, in_mask, weights, aux)
        taps, code, slope, halo_cot, pay = call(
            encode_kernel,
            "encode",
            coded + [shape(z.halo, NB * 128), shape(4, 128, dtype=F32)],
            [VMEM] * 9,
            [pltpu.VMEM((NB, 64, 256), F32)],
            alias={6: 0, 7: 1, 8: 2},
        )(pixels, in_mask, halo, banded, aux, pay, taps, code, slope)
        pay = jnp.broadcast_to(pay[None], (sections * wides, 4, 128))
        stats = lax.all_to_all(pay, ("section", "wide"), 0, 0)
        sent, decode_pay = call(
            decode_kernel,
            "decode",
            [shape(*frame), shape(CCODE, 128, dtype=F32)],
            [VMEM] * 6,
            [framed, framed],
            cost=heavy,
        )(whole[2], code, in_mask, halo_cot, weights, aux)
        grad, pay, moments = call(
            whiten_kernel,
            "whiten",
            [
                shape(*frame),
                shape(sections, CCODE, 128),
                shape(CCODE + 8, 128, dtype=F32),
            ],
            [VMEM] * 7,
            [],
            alias={3: 0},
        )(stats, code, slope, sent, taps, decode_pay, aux)
        pay = jnp.broadcast_to(pay[:, None], (sections, wides, CCODE, 128))
        pay = pay.reshape(sections * wides, CCODE, 128)
        parts = lax.all_to_all(pay, ("section", "wide"), 0, 0)
        (sending,) = call(
            send_kernel,
            "send",
            [shape(z.mb, z.band, z.span)],
            [VMEM] * 5,
            [framed],
            cost=heavy,
        )(grad, code, in_mask, weights, aux)
        arrived = lax.ppermute(sending, "section", swap)
        half_done, onehot, new_mean, new_cov = call(
            keep_kernel,
            "keep",
            [
                shape(1, z.micro, z.band, z.span),
                shape(128, NK),
                shape(1, CCODE, dtype=F32),
                shape(CCODE, CCODE, dtype=F32),
            ],
            [VMEM] * 6,
            [
                framed,
                band_buf,
                pltpu.VMEM((1, CCODE), F32),
                pltpu.VMEM((CCODE, CCODE), F32),
                DMA((3,)),
            ],
            out_specs=[HBM, VMEM, HBM, HBM],
            cost=heavy,
        )(grad, code, in_mask, weights, aux, moments)
        (sums,) = call(
            total_kernel,
            "total",
            [shape(CCODE, 128, dtype=F32)],
            [VMEM],
            [],
            cost=pl.CostEstimate(flops=100_000_000_000, bytes_accessed=0, transcendentals=0),
        )(parts)
        pixels_out, kernel_grads, enc_grad, dec_grad = call(
            finish_kernel,
            "finish",
            [
                shape(1, z.micro, z.band, z.span),
                shape(1, NK, dtype=F32),
                shape(1, CCODE, dtype=F32),
                shape(1, CIN, dtype=F32),
            ],
            [VMEM] * 3 + [HBM],
            [
                pltpu.VMEM((1, NK), F32),
                pltpu.VMEM((1, CCODE), F32),
                pltpu.VMEM((1, CIN), F32),
                DMA((4,)),
            ],
            out_specs=[HBM] * 4,
            alias={3: 0},
        )(sums, arrived, onehot, half_done)
        return (
            pixels_out,
            kernel_grads,
            enc_grad.reshape(CCODE),
            dec_grad.reshape(CIN),
            new_mean.reshape(CCODE),
            new_cov,
        )

    return run


def solution(mesh):
    in_specs = (
        P(None, "wide", None),
        P(None, "wide", None),
        P(),
        P("section", None),
        P(),
        P(),
        P(None, "wide", None),
        P(),
        P(),
    )
    out_specs = (P("section", None, "wide", None), P("section", None), P(), P(), P(), P())
    run = shards(mesh.shape["section"], mesh.shape["wide"])
    return jax.shard_map(run, mesh=mesh, in_specs=in_specs, out_specs=out_specs, check_vma=False)
```

```python
import jax
import jax.numpy as jnp
from jax import lax
from jax.experimental import pallas as pl
from jax.experimental.pallas import tpu as pltpu
from jax.sharding import PartitionSpec as P

CIN = 4
CCODE = 16
KS = 5
HW = 128

UW = 16
NB = 5
HALO = 8
NK = CCODE * CIN * KS * KS
COPIES = 32

decay_rate = 0.9
whiten_weight = 0.25

F32 = jnp.float32
BF16 = jnp.bfloat16


def iota(shape, dim):
    return lax.broadcasted_iota(jnp.int32, shape, dim)


def hot(mask):
    return jnp.where(mask, 1.0, 0.0).astype(BF16)


def dot(a, b, dims=((1,), (0,))):
    return lax.dot_general(a, b, (dims, ((), ())), preferred_element_type=F32)


def fold(x, unit):
    rolled = [x] + [pltpu.roll(x, step, 1) for step in range(unit, 128, unit)]
    while len(rolled) > 1:
        rolled = [sum(rolled[i : i + 2]) for i in range(0, len(rolled), 2)]
    return rolled[0]


def lanes_from(x, source):
    return jnp.take_along_axis(x, source, axis=1, mode="promise_in_bounds")


def split(x):
    high = x.astype(BF16)
    rest = x - high.astype(F32)
    mid = rest.astype(BF16)
    return high, mid, (rest - mid.astype(F32)).astype(BF16)


class Sizes:
    def __init__(self, fields, sections):
        self.micro, self.band, self.span = fields
        self.sections = sections
        self.mb = self.micro // sections
        self.jf = self.band // 2 + HALO // 2
        self.rows = self.jf * self.mb
        self.own = self.mb * self.band
        self.halo = self.mb * HALO
        self.shift = self.mb.bit_length() - 1
        self.frame = NB * self.rows
        self.near = self.halo // 2
        self.sent = CIN * (self.halo + self.near) + self.near


def tap_target(n):
    o = (n * 5243) >> 19
    t = n - 100 * o
    c = (t * 1311) >> 15
    t = t - 25 * c
    k = (t * 205) >> 10
    l = t - 5 * k
    return (3 * k + (l >> 1)) * 8 + 2 * c + (l & 1), o


def tap_onehot():
    target, _ = tap_target(iota((1, NK), 1))
    return hot(iota((128, NK), 0) == target)


def row_target(z, row):
    half = z.own // 2
    parity = (row >= half).astype(jnp.int32)
    q = row - parity * half
    return (q & (z.mb - 1)) * z.band + 2 * (q >> z.shift) + parity


def gather_rows(z):
    return hot(iota((z.own, z.own), 1) == row_target(z, iota((z.own, 1), 0)))


def scatter_rows(z):
    return hot(iota((z.own, z.own), 0) == row_target(z, iota((1, z.own), 1)))


def pixel_target(lane, inner):
    u_local = (lane >> 3) & (UW - 1)
    u = (lane >> 7) * (UW - 2) + u_local - 1
    valid = (u >= 0) & (u < HW // 2)
    if inner:
        valid = valid & (u_local >= 1) & (u_local <= UW - 2)
    return 2 * u + (lane & 1), (lane >> 1) & 3, valid


def window_columns():
    col, c, valid = pixel_target(iota((1, NB * 128), 1), False)
    target = jnp.where(valid, c * HW + col, -1)
    return hot(iota((CIN * HW, NB * 128), 0) == target)


def unwindow_columns():
    col, c, valid = pixel_target(iota((NB * 128, 1), 0), True)
    target = jnp.where(valid, c * HW + col, -1)
    return hot(iota((NB * 128, CIN * HW), 1) == target)


def window_mask_columns():
    col, _, valid = pixel_target(iota((1, NB * 128), 1), False)
    return hot(iota((HW, NB * 128), 0) == jnp.where(valid, col, -1))


def code_mask_lanes():
    lane = iota((1, 256), 1)
    u_local = lane >> 4
    inner = (u_local >= 1) & (u_local <= UW - 2)
    return hot(iota((128, 256), 0) == jnp.where(inner, u_local * 8, -1))


def own_rows(z, odd):
    j = (iota((z.rows, 1), 0) >> z.shift) - odd * (HALO // 2)
    return (j >= 0) & (j < z.band // 2)


def places(z, odd):
    own = pl.multiple_of(odd * (z.halo // 2), 16)
    halo = pl.multiple_of((1 - odd) * (z.own // 2), 16)
    return own, halo


def mend_coarse(blocks):
    last = HW // 2 - (NB - 1) * (UW - 2)
    rows = blocks[0].shape[0]
    lane = iota((rows, 128), 1)
    halves = [(x[:, :128], x[:, 128:]) for x in blocks]
    done = []
    for b, (low, high) in enumerate(halves):
        before = pltpu.roll(halves[b - 1][1], 32, 1) if b else 0.0
        new_low = jnp.where(lane < 16, before, low)
        if b + 1 < NB:
            after = pltpu.roll(halves[b + 1][0], 96, 1)
            new_high = jnp.where(lane >= 112, after, high)
        else:
            new_high = jnp.where(lane < (last + 1) * 16 - 128, high, 0.0)
        done.append((new_low, new_high))
    return done


def mend_fine(halves):
    rows = halves[0][0].shape[0]
    lane = iota((rows, 128), 1)
    done = []
    for b in range(NB):
        pair = []
        for h in range(2):
            x = halves[b][h]
            before = pltpu.roll(halves[b - 1][h], 16, 1) if b else 0.0
            after = pltpu.roll(halves[b + 1][h], 112, 1) if b + 1 < NB else 0.0
            x = jnp.where(lane < 8, before, x)
            pair.append(jnp.where(lane >= 120, after, x))
        done.append(tuple(pair))
    return done


def pad_frame(z, sh):
    zeros = jnp.zeros((NB, 8, 256), F32)
    sh[:, 0:8, :] = zeros
    sh[:, 8 + z.rows : 16 + z.rows, :] = zeros


def put_frame(z, sh, halves):
    pad_frame(z, sh)
    for b, (low, high) in enumerate(halves):
        sh[b, 8 : 8 + z.rows, 0:128] = low
        sh[b, 8 : 8 + z.rows, 128:256] = high


def put_pixels(z, sh, odd, own, halo):
    pad_frame(z, sh)
    for start, part in zip(places(z, odd), (own, halo)):
        half = part.shape[0] // 2
        rows = pl.ds(pl.multiple_of(8 + start, 8), half)
        for b in range(NB):
            for h in range(2):
                sh[b, rows, h * 128 : h * 128 + 128] = part[
                    h * half : h * half + half, b * 128 : b * 128 + 128
                ]


def fine_taps(z, sh, b):
    up = sh[b, 8 - z.mb : 8 - z.mb + z.rows, :]
    here = sh[b, 8 : 8 + z.rows, :]
    down = sh[b, 8 + z.mb : 8 + z.mb + z.rows, 0:128]
    return jnp.concatenate([up, here, down], axis=1).astype(BF16)


def coarse_taps(z, sh, b):
    down = sh[b, 8 + z.mb : 8 + z.mb + z.rows, :]
    here = sh[b, 8 : 8 + z.rows, :]
    up = sh[b, 8 - z.mb : 8 - z.mb + z.rows, :]
    return [x.astype(BF16) for x in (down, here, up)]


def spread(z, sh, weights):
    taps = [coarse_taps(z, sh, b) for b in range(NB)]
    down, here, up = (jnp.concatenate([t[i] for t in taps], axis=0) for i in range(3))
    nt = ((1,), (1,))
    out = dot(down, weights[0:256], nt) + dot(here, weights[256:512], nt)
    extra = dot(up, weights[512:640], nt)
    return out[:, :128] + extra, out[:, 128:]


def pick_taps(grads):
    lane = iota((CCODE, 128), 1)
    place = lane >> 3
    pieces = []
    for k in range(KS):
        for shift in (-1, 0, 1):
            total = jnp.zeros((CCODE, 128), F32)
            for u in range(1, UW - 1):
                part = grads[u * 16 : u * 16 + 16, k * 128 : k * 128 + 128]
                total = jnp.where(place == u + shift, part, total)
            pieces.append(total)
    pieces.append(jnp.zeros((CCODE, 128), F32))
    block = lane >> 5
    fours = []
    for first in range(4):
        group = pieces[first::4]
        parts = []
        for j in range(4):
            x = group[j]
            for t in range(1, 4):
                x = jnp.where(block == t, group[(t + j) & 3], x)
            parts.append(x)
        fours.append(
            (parts[0] + pltpu.roll(parts[1], 32, 1))
            + (pltpu.roll(parts[2], 64, 1) + pltpu.roll(parts[3], 96, 1))
        )
    inner = place & 3
    total = None
    for j in range(4):
        x = fours[j]
        for t in range(1, 4):
            x = jnp.where(inner == t, fours[(t + j) & 3], x)
        if j:
            x = jnp.where(inner >= j, pltpu.roll(x, 8 * j, 1), pltpu.roll(x, 96 + 8 * j, 1))
        total = x if total is None else total + x
    return total


def own_frame(z, odd, sh):
    start, _ = places(z, odd)
    half = z.own // 2
    rows = pl.ds(pl.multiple_of(8 + start, 8), half)
    flat = jnp.concatenate(
        [
            jnp.concatenate(
                [sh[b, rows, h * 128 : h * 128 + 128] for b in range(NB)], axis=1
            )
            for h in range(2)
        ],
        axis=0,
    )
    return flat.astype(BF16)


def kernel_rows(flat):
    taps = CIN * KS * KS
    pad = jnp.zeros((1, 256 - NK % 128), F32)
    flat = jnp.concatenate([flat, pad], axis=1)
    lane = iota((1, 128), 1)
    row = iota((CCODE, 128), 0)
    rows = jnp.zeros((CCODE, 128), F32)
    for o in range(CCODE):
        chunk, shift = divmod(o * taps, 128)
        x = flat[:, chunk * 128 : chunk * 128 + 128]
        if shift:
            after = flat[:, chunk * 128 + 128 : chunk * 128 + 256]
            x = jnp.where(
                lane < 128 - shift,
                pltpu.roll(x, 128 - shift, 1),
                pltpu.roll(after, 128 - shift, 1),
            )
        rows = jnp.where(row == o, jnp.broadcast_to(x, (CCODE, 128)), rows)
    return rows


def spread_taps(kernel_pair):
    taps = CIN * KS * KS
    rows = jnp.concatenate([kernel_rows(x) for x in kernel_pair for _ in range(8)], axis=0)
    lane = iota((1, 128), 1)
    target, _ = tap_target(jnp.minimum(lane, taps - 1))
    slots = hot(iota((128, 128), 0) == jnp.where(lane < taps, target, -1))
    wide = dot(slots, rows.T.astype(BF16)).astype(BF16)
    halves = [wide[:, 0:128], wide[:, 128:256]]
    return jnp.concatenate([x for x in halves for _ in range(2)], axis=1)


def band_weights(wide_taps):
    wide_taps = wide_taps.astype(F32)
    row_u = iota((128, 256), 0) >> 3
    lane_u = iota((128, 256), 1) >> 4
    masks = [row_u == lane_u + shift for shift in (-1, 0, 1)]
    parts = []
    for k in range(KS):
        total = jnp.zeros((128, 256), F32)
        for i, mask in enumerate(masks):
            q = 3 * k + i
            piece = wide_taps[8 * q : 8 * q + 8]
            piece = jnp.broadcast_to(piece[None], (16, 8, 256)).reshape(128, 256)
            total = jnp.where(mask, piece, total)
        parts.append(total.astype(BF16))
    return jnp.concatenate(parts, axis=0)


def edge_kernel(
    z, fields, mask, cotangent, kernel, out, kernel_out,
    field_buf, mask_buf, cot_buf, kernel_buf, sems,
):
    odd = lax.rem(lax.axis_index("wide"), 2)
    first = lax.axis_index("section") * z.mb
    start = pl.multiple_of((1 - odd) * (z.band - 16), 16)
    copies = [
        pltpu.make_async_copy(
            source.at[pl.ds(first, z.mb), pl.ds(start, 16), :], buf, sems.at[i]
        )
        for i, (source, buf) in enumerate(
            ((fields, field_buf), (mask, mask_buf), (cotangent, cot_buf))
        )
    ]
    copies.append(pltpu.make_async_copy(kernel, kernel_buf, sems.at[3]))
    for copy in copies:
        copy.start()
    for copy in copies:
        copy.wait()
    kernel_out[...] = jnp.broadcast_to(kernel_buf[...].astype(F32), (COPIES, NK)).astype(BF16)

    def beside(buf):
        rows = buf[...].astype(F32)
        return jnp.where(odd == 1, rows[:, :HALO], rows[:, HALO:])

    def ordered(rows, firsts):
        return jnp.concatenate(
            [rows[:, j + h] for h in range(2) for j in firsts], axis=0
        ).astype(BF16)

    mask_rows = beside(mask_buf)
    allowed = jnp.concatenate([mask_rows] * CIN, axis=2)
    every, half = range(0, HALO, 2), range(0, HALO // 2, 2)
    near = beside(cot_buf) * allowed
    near = jnp.where(odd == 1, near[:, : HALO // 2], near[:, HALO // 2 :])
    pieces = ordered(beside(field_buf) * allowed, every), ordered(near, half)
    start = 0
    for piece in pieces:
        count = piece.shape[0]
        for c in range(CIN):
            out[start : start + count, :] = piece[:, c * HW : c * HW + HW]
            start += count
    out[start : z.sent, :] = ordered(mask_rows, every)[0 : z.near]


def prepare_kernel(
    z, fields, mask, counts, enc_bias, dec_bias, run_mean, run_cov,
    pixels_out, inmask_out, aux_out,
    count_buf, enc_buf, dec_buf, mean_buf, cov_buf, sems,
):
    section = lax.axis_index("section")
    wide = lax.axis_index("wide")
    first = section * z.mb
    mine_rows = pl.ds(first, z.mb)
    copies = [
        pltpu.make_async_copy(source, buf, sems.at[i])
        for i, (source, buf) in enumerate(
            (
                (counts, count_buf),
                (enc_bias, enc_buf),
                (dec_bias, dec_buf),
                (run_mean, mean_buf),
                (run_cov, cov_buf),
            )
        )
    ]
    for copy in copies:
        copy.start()
    gather = gather_rows(z)
    columns = window_columns()
    mask_columns = window_mask_columns()
    pixel_mask = mask[mine_rows].astype(F32).astype(BF16).reshape(z.own, HW)
    pixels = fields[mine_rows].reshape(z.own, z.span)
    framed = dot(gather, jnp.concatenate([pixel_mask, pixels], axis=1)).astype(BF16)
    in_mask = dot(framed[:, 0:HW], mask_columns)
    windowed = dot(framed[:, HW:], columns)
    for copy in copies:
        copy.wait()
    lane = iota((8, 128), 1)
    dec_row = jnp.zeros((8, 128), F32)
    for c in range(CIN):
        dec_row = jnp.where(((lane >> 1) & 3) == c, dec_buf[c], dec_row)
    enc_row = jnp.zeros((8, 128), F32)
    mean_row = jnp.zeros((8, 128), F32)
    for o in range(CCODE):
        enc_row = jnp.where((lane & 15) == o, enc_buf[o], enc_row)
        mean_row = jnp.where((lane & 15) == o, mean_buf[o], mean_row)
    aux_out[0:8] = dec_row
    aux_out[8:16] = enc_row
    aux_out[16:24] = mean_row
    aux_out[24:40] = jnp.zeros((16, 128), F32)
    aux_out[24:40, 0:CCODE] = cov_buf[...]
    field_now = wide * z.band // HW
    micro = iota((16, 128), 0) & (z.mb - 1)
    count = jnp.zeros((16, 128), jnp.int32)
    for m in range(z.mb):
        count = jnp.where(micro == m, count_buf[first + m, field_now], count)
    channel_ok = jnp.where(((iota((16, 128), 1) >> 1) & 3) < count, 1.0, 0.0)
    aux_out[40:56] = channel_ok
    in_mask = in_mask * jnp.tile(channel_ok, (z.own // 16, NB))
    inmask_out[...] = in_mask.astype(BF16)
    pixels_out[...] = (windowed * in_mask).astype(BF16)


def taps_kernel(z, kernel_own, kernel_other, weights_out):
    mine, other = (x[0:16].astype(F32)[0:1] for x in (kernel_own, kernel_other))
    leads = lax.axis_index("section") == 0
    weights_out[...] = spread_taps((jnp.where(leads, mine, other), jnp.where(leads, other, mine)))


def local_taps(sh, b, rows, step):
    up = sh[b, 16 - step : 16 - step + rows, :]
    here = sh[b, 16 : 16 + rows, :]
    down = sh[b, 16 + step : 16 + step + rows, 0:128]
    return jnp.concatenate([up, here, down], axis=1).astype(BF16)


def encode_rows(taps, banded, bias, masks, mine):
    code_mask = dot(masks, code_mask_lanes())
    pre = dot(taps, banded) + bias
    slope = jnp.exp(jnp.minimum(pre, 0.0))
    code = jnp.where(pre > 0, pre, slope - 1.0).astype(BF16).astype(F32)
    slope = jnp.where(code_mask > 0.5, slope, -slope)
    allowed = code_mask if mine is None else jnp.where(mine, code_mask, 0.0)
    weighted = code * allowed
    halves = [
        jnp.concatenate([x[:, 0:128], x[:, 128:256]], axis=0).astype(BF16) for x in (weighted, code)
    ]
    second = dot(*halves, ((0,), (0,)))
    sums = [jnp.sum(x, axis=0, keepdims=True) for x in (weighted, allowed)]
    lane_u = iota((16, 128), 1) >> 4
    total = second[0:16]
    for u in range(1, UW // 2):
        total = jnp.where(lane_u == u, second[u * 16 : u * 16 + 16], total)
    total = fold(total, 16)
    diagonal = (iota((8, 128), 1) >> 4) == iota((8, 128), 0)
    pay = [
        jnp.sum(jnp.where(diagonal, total[h * 8 : h * 8 + 8], 0.0), axis=0, keepdims=True)
        for h in range(2)
    ]
    first, count = (
        fold(jnp.broadcast_to(x[:, :128] + x[:, 128:], (8, 128)), 16) for x in sums
    )
    lane = iota((8, 128), 1)
    inner, group = lane & 15, lane >> 4
    first = lanes_from(first, jnp.where(inner == 0, group, group + 8))
    spare = jnp.where(inner == 2, count, first)[0:1]
    pay[1] = jnp.where(inner[0:1] < 8, spare, pay[1])
    return code, slope, jnp.concatenate(pay, axis=0)


def inner_kernel(
    z, pixels, own_mask, weights, aux, taps_out, code_out, slope_out, pay_out, band_out, sh
):
    odd = lax.rem(lax.axis_index("wide"), 2)
    half = z.own // 2
    count = half - 16
    zeros = jnp.zeros((NB, 16, 256), F32)
    sh[:, 0:16, :] = zeros
    sh[:, half : half + 16, :] = zeros
    here = pl.ds(pl.multiple_of((1 - odd) * 16, 16), half)
    for b in range(NB):
        for h in range(2):
            sh[b, here, h * 128 : h * 128 + 128] = pixels[
                h * half : h * half + half, b * 128 : b * 128 + 128
            ].astype(F32)
    start = pl.multiple_of(odd * 32, 16)
    taps = [local_taps(sh, b, count, z.mb) for b in range(NB)]
    for b in range(NB):
        taps_out[b, pl.ds(start, count), :] = taps[b]
    kept = pl.ds(pl.multiple_of(odd * 16, 16), count)
    masks = jnp.concatenate([own_mask[kept, b * 128 : b * 128 + 128] for b in range(NB)], axis=0)
    bias = jnp.concatenate([aux[8:9], aux[8:9]], axis=1)
    banded = band_weights(weights[:, 0:256])
    band_out[...] = banded
    code, slope, pay = encode_rows(jnp.concatenate(taps, axis=0), banded, bias, masks, None)
    pay_out[...] = pay
    for b in range(NB):
        rs = slice(b * count, b * count + count)
        code_out[b, pl.ds(start, count), :] = code[rs].astype(BF16)
        slope_out[b, pl.ds(start, count), :] = slope[rs]


def encode_kernel(
    z, pixels, own_mask, halo, banded, aux, inner_pay, taps_in, code_in, slope_in,
    taps_out, code_out, slope_out, cot_out, pay_out,
    sh,
):
    odd = lax.rem(lax.axis_index("wide"), 2)
    half = z.own // 2
    count = 32
    channel_ok = jnp.tile(aux[40:56], (1, NB))
    middle, end = CIN * z.halo, CIN * (z.halo + z.near)
    halo_mask = dot(halo[end : z.sent, :], window_mask_columns())
    halo_rows = [
        jnp.concatenate([halo[i : i + count, :] for i in range(start, stop, count)], axis=1)
        for start, stop, count in ((0, middle, z.halo), (middle, end, z.near))
    ]
    halo_pixels = dot(jnp.concatenate(halo_rows, axis=0), window_columns())
    halo_x = halo_pixels[0 : z.halo] * jnp.tile(channel_ok, (2, 1))
    zeros = jnp.zeros((NB, 16, 256), F32)
    sh[:, 0:16, :] = zeros
    sh[:, 48:64, :] = zeros
    own_start = pl.multiple_of((1 - odd) * (half - 32), 16)
    own_there = pl.ds(pl.multiple_of(odd * 32, 16), 32)
    halo_there = pl.ds(pl.multiple_of((2 - odd) * 16, 16), 16)
    for b in range(NB):
        for h in range(2):
            cs = slice(b * 128, b * 128 + 128)
            own = pixels[pl.ds(pl.multiple_of(own_start + h * half, 16), 32), cs]
            sh[b, own_there, h * 128 : h * 128 + 128] = own.astype(F32)
            sh[b, halo_there, h * 128 : h * 128 + 128] = halo_x[h * 16 : h * 16 + 16, cs]
    start = pl.multiple_of((1 - odd) * (z.rows - count), 16)
    taps = [local_taps(sh, b, count, z.mb) for b in range(NB)]
    for b in range(NB):
        taps_out[b, pl.ds(start, count), :] = taps[b]
    edge_mask = own_mask[pl.ds(pl.multiple_of((1 - odd) * (half - 16), 16), 16), :].astype(F32)
    first = jnp.where(odd == 1, halo_mask, edge_mask)
    later = jnp.where(odd == 1, edge_mask, halo_mask)
    masks = jnp.concatenate(
        [x[:, b * 128 : b * 128 + 128] for b in range(NB) for x in (first, later)], axis=0
    ).astype(BF16)
    bias = jnp.concatenate([aux[8:9], aux[8:9]], axis=1)
    mine = ((iota((NB * count, 1), 0) >> 4) & 1) == odd
    code, slope, pay = encode_rows(jnp.concatenate(taps, axis=0), banded[...], bias, masks, mine)
    pay = pay + inner_pay[...]
    pay_out[...] = pay
    for b in range(NB):
        rs = slice(b * count, b * count + count)
        code_out[b, pl.ds(start, count), :] = code[rs].astype(BF16)
        slope_out[b, pl.ds(start, count), :] = slope[rs]
    near = halo_pixels[z.halo : z.halo + z.near] * channel_ok
    nothing = jnp.zeros((8, NB * 128), F32)
    for h in range(2):
        rows = near[h * 8 : h * 8 + 8]
        rows = [jnp.where(odd == 1, nothing, rows), jnp.where(odd == 1, rows, nothing)]
        cot_out[h * 16 : h * 16 + 16, :] = jnp.concatenate(rows, axis=0).astype(BF16)


def decode_kernel(
    z, cotangent, code, in_mask, halo_cot, weights, aux,
    sent_out, pay_out,
    sh, cot_frame,
):
    odd = lax.rem(lax.axis_index("wide"), 2)
    mine = pl.ds(lax.axis_index("section") * z.mb, z.mb)
    rows = z.rows
    put_frame(z, sh, mend_coarse([code[b].astype(F32) for b in range(NB)]))
    banded = band_weights(weights[:, 256:512])
    raws = spread(z, sh, banded)
    gather = gather_rows(z)
    columns = window_columns()
    own_cot = dot(dot(gather, cotangent[mine].reshape(z.own, z.span)).astype(BF16), columns)
    put_pixels(z, cot_frame, odd, own_cot * in_mask[...].astype(F32), halo_cot[...].astype(F32))
    mine_rows = own_rows(z, odd)
    u_local = (iota((1, 128), 1) >> 3) & (UW - 1)
    inner = mine_rows & (u_local >= 1) & (u_local <= UW - 2)
    grads = []
    bias_sum = jnp.zeros((1, 128), F32)
    for h in range(2):
        raw = raws[h] + aux[0:1]
        slope = jnp.exp(jnp.minimum(raw, 0.0))
        cs = slice(h * 128, h * 128 + 128)
        for b in range(NB):
            rs = slice(b * rows, b * rows + rows)
            grad = (cot_frame[b, 8 : 8 + rows, cs] * slope[rs]).astype(BF16).astype(F32)
            bias_sum = bias_sum + jnp.sum(jnp.where(inner, grad, 0.0), axis=0, keepdims=True)
            grads.append(grad)
    put_frame(z, sh, mend_fine([(grads[b], grads[NB + b]) for b in range(NB)]))
    taps = jnp.concatenate([fine_taps(z, sh, b) for b in range(NB)], axis=0)
    sent_out[...] = dot(taps, banded).astype(BF16).reshape(NB, rows, 256)
    last = HW // 2 - (NB - 1) * (UW - 2)
    within = mine_rows & ((iota((1, 256), 1) >> 4) <= last)
    mine = jnp.concatenate(
        [
            jnp.where(within if b == NB - 1 else mine_rows, code[b].astype(F32), 0.0).astype(BF16)
            for b in range(NB)
        ],
        axis=0,
    )
    pay = pick_taps(dot(mine, taps, ((0,), (0,))))
    bias_sum = fold(jnp.broadcast_to(bias_sum, (16, 128)), 8)
    lane = iota((16, 128), 1)
    keep = (lane < 8) & ((lane >> 1) == iota((16, 128), 0))
    column = jnp.sum(jnp.where(keep, bias_sum, 0.0), axis=1, keepdims=True)
    pay_out[...] = jnp.where(lane >= 120, column, pay)


def whiten_kernel(
    z, stats, code, slope, sent, taps, decode_pay, aux,
    grad_out, pay_out, moments_out,
):
    odd = lax.rem(lax.axis_index("wide"), 2)
    rows = z.rows
    pay = jnp.sum(stats[...], axis=0)
    lane = iota((8, 128), 1)
    inner, step = lane & 15, iota((8, 128), 0)
    low, high = (jnp.broadcast_to(pay[h : h + 1], (8, 128)) for h in range(2))
    count = lanes_from(high, jnp.full((8, 128), 2, jnp.int32))[0:1]
    first = lanes_from(high, jnp.where(inner < 8, 16 * inner, 16 * (inner - 8) + 1))[0:1]
    mean = first / count
    columns = jnp.concatenate([lanes_from(high, 16 * step + h) for h in range(2)], axis=0)
    diagonal = (lane >> 4) == step
    mirrored = lanes_from(low, jnp.where(inner < 8, 16 * inner + 8 + step, 0))
    low, high = (fold(jnp.where(diagonal, x, 0.0), 16) for x in (low, high))
    second = jnp.concatenate([low, jnp.where(inner < 8, mirrored, high)], axis=0)
    lane = iota((16, 128), 1)
    row = iota((16, 128), 0)
    wide_mean = jnp.broadcast_to(mean, (16, 128))
    total = jnp.broadcast_to(count, (16, 128))
    mean_column = columns / total
    cov = second / total - mean_column * wide_mean
    moments_out[0:CCODE] = cov
    moments_out[CCODE:] = jnp.broadcast_to(mean, (8, 128))
    offset = cov - jnp.where((lane & 15) == row, 1.0, 0.0)
    pulled = jnp.sum(offset * mean_column, axis=0, keepdims=True)
    linear = whiten_weight * mean - 2.0 * whiten_weight * pulled
    linear = jnp.concatenate([linear, linear], axis=1)
    matrix = jnp.tile(2.0 * whiten_weight * offset, (8, 1))
    matrix = jnp.where((iota((128, 128), 0) >> 4) == (iota((128, 128), 1) >> 4), matrix, 0.0)
    high = matrix.astype(BF16)
    matrix = jnp.concatenate([high, (matrix - high.astype(F32)).astype(BF16)], axis=0)
    flat = code[...].reshape(z.frame, 256)
    flat = jnp.concatenate(
        [jnp.concatenate([x, x], axis=1) for x in (flat[:, 0:128], flat[:, 128:256])], axis=0
    )
    turned = dot(flat, matrix)
    turned = jnp.concatenate([turned[0 : z.frame], turned[z.frame :]], axis=1) + linear
    mine_rows = own_rows(z, odd)
    lane_u = iota((1, 256), 1) >> 4
    inner = mine_rows & (lane_u >= 1) & (lane_u <= UW - 2)
    last = HW // 2 - (NB - 1) * (UW - 2)
    blocks, mine = [], []
    bias_sum = jnp.zeros((1, 256), F32)
    for b in range(NB):
        signed = slope[b]
        pull = jnp.where(signed > 0, turned[b * rows : b * rows + rows], 0.0)
        grad = ((sent[b].astype(F32) + pull) * jnp.abs(signed)).astype(BF16).astype(F32)
        kept = jnp.where(inner & (lane_u <= last) if b == NB - 1 else inner, grad, 0.0)
        bias_sum = bias_sum + jnp.sum(kept, axis=0, keepdims=True)
        blocks.append(grad)
        mine.append(kept.astype(BF16))
    products = dot(
        jnp.concatenate(mine, axis=0), taps[...].reshape(z.frame, KS * 128), ((0,), (0,))
    )
    encode_pay = pick_taps(products)
    bias_sum = fold(jnp.broadcast_to(bias_sum[:, :128] + bias_sum[:, 128:], (16, 128)), 16)
    column = jnp.sum(jnp.where(lane == row, bias_sum, 0.0), axis=1, keepdims=True)
    decoded = decode_pay[...]
    biases = jnp.where((lane & 1) == 0, column, decoded)
    coarse = biases.astype(BF16).astype(F32)
    biases = jnp.where((lane & 2) == 0, coarse, biases - coarse)
    encode_pay = jnp.where(lane >= 120, biases, encode_pay)
    decoded = jnp.where(lane >= 120, biases, decoded)
    pay_out[0] = encode_pay.astype(BF16)
    pay_out[1] = decoded.astype(BF16)
    for b, (low, high) in enumerate(mend_coarse(blocks)):
        grad_out[b, :, 0:128] = low.astype(BF16)
        grad_out[b, :, 128:256] = high.astype(BF16)


def picture(z, decodes, grad, code, in_mask, weights, aux, sh):
    odd = lax.rem(lax.axis_index("wide"), 2)
    rows = z.rows
    frames = [
        jnp.where(decodes, code[b].astype(F32), grad[b].astype(F32)) for b in range(NB)
    ]
    put_frame(z, sh, mend_coarse(frames))
    chosen = jnp.where(decodes, weights[:, 256:512].astype(F32), weights[:, 0:256].astype(F32))
    raws = spread(z, sh, band_weights(chosen))
    for h in range(2):
        raw = raws[h] + aux[0:1]
        raw = jnp.where(raw > 0, raw, jnp.exp(jnp.minimum(raw, 0.0)) - 1.0)
        raw = jnp.where(decodes, raw, raws[h])
        for b in range(NB):
            sh[b, 8 : 8 + rows, h * 128 : h * 128 + 128] = raw[b * rows : b * rows + rows]
    flat = own_frame(z, odd, sh) * in_mask[...]
    native = dot(flat, unwindow_columns()).astype(BF16)
    return dot(scatter_rows(z), native).astype(BF16).reshape(z.mb, z.band, z.span)


def send_kernel(z, grad, code, in_mask, weights, aux, send_out, sh):
    decodes = lax.axis_index("section") == 0
    send_out[...] = picture(z, decodes, grad, code, in_mask, weights, aux, sh)


def keep_kernel(
    z, grad, code, in_mask, weights, aux, moments,
    pixels_out, onehot_out, mean_out, cov_out,
    sh, mine, means, covs, sems,
):
    section = lax.axis_index("section")
    means[...] = decay_rate * aux[16:17, 0:CCODE] + (1.0 - decay_rate) * moments[16:17, 0:CCODE]
    covs[...] = decay_rate * aux[24:40, 0:CCODE] + (1.0 - decay_rate) * moments[0:16, 0:CCODE]
    mine[...] = picture(z, section == 1, grad, code, in_mask, weights, aux, sh)
    copies = [
        pltpu.make_async_copy(source, target, sems.at[i])
        for i, (source, target) in enumerate(
            (
                (mine, pixels_out.at[0, pl.ds(section * z.mb, z.mb)]),
                (means, mean_out),
                (covs, cov_out),
            )
        )
    ]
    for copy in copies:
        copy.start()
    onehot_out[...] = tap_onehot()
    for copy in copies:
        copy.wait()


def total_kernel(z, parts, out):
    out[...] = jnp.sum(parts[...].astype(F32), axis=0)


def finish_kernel(
    z, sums, arrived, onehot, half_done, pixels_out, kernel_out, enc_out, dec_out,
    kernels, encs, decs, sems,
):
    there = z.micro - z.mb - lax.axis_index("section") * z.mb
    copies = [
        pltpu.make_async_copy(source, target, sems.at[i])
        for i, (source, target) in enumerate(
            (
                (arrived, pixels_out.at[0, pl.ds(there, z.mb)]),
                (encs, enc_out),
                (decs, dec_out),
                (kernels, kernel_out),
            )
        )
    ]
    copies[0].start()
    total = sums[...]
    chosen = dot(jnp.concatenate(split(total), axis=0), onehot[...])
    chosen = chosen[0:16] + chosen[16:32] + chosen[32:48]
    _, o = tap_target(iota((1, NK), 1))
    kernels[...] = jnp.sum(jnp.where(iota((16, NK), 0) == o, chosen, 0.0), axis=0, keepdims=True)
    copies[3].start()
    lane = iota((16, 128), 1)
    row = iota((16, 128), 0)
    for slot, out in ((120, encs), (121, decs)):
        chosen = (lane == slot) | (lane == slot + 2)
        column = jnp.sum(jnp.where(chosen, total, 0.0), axis=1, keepdims=True)
        flat = jnp.sum(jnp.where(lane == row, column, 0.0), axis=0, keepdims=True)
        out[...] = flat[:, 0 : out.shape[1]]
    copies[1].start()
    copies[2].start()
    for copy in copies:
        copy.wait()


VMEM = pl.BlockSpec(memory_space=pltpu.VMEM)
HBM = pl.BlockSpec(memory_space=pltpu.HBM)
PARAMS = pltpu.CompilerParams(vmem_limit_bytes=24 * 1024 * 1024)
DMA = pltpu.SemaphoreType.DMA


def shape(*dims, dtype=BF16):
    return jax.ShapeDtypeStruct(dims, dtype)


def shards(sections, wides):
    def run(
        fields, pixel_mask, channel_counts, kernels, enc_bias, dec_bias, cotangent, run_mean, run_cov
    ):
        z = Sizes(fields.shape, sections)
        assert 2 * z.band == HW and z.span == CIN * HW and z.mb == 4
        whole = (fields, pixel_mask, cotangent)
        (
            fields, cotangent, pixel_mask, kernels, channel_counts, enc_bias, dec_bias,
            run_mean, run_cov,
        ) = (
            pltpu.with_memory_space_constraint(x, pltpu.HBM)
            for x in (
                fields, cotangent, pixel_mask, kernels, channel_counts, enc_bias, dec_bias,
                run_mean, run_cov,
            )
        )
        swap = [(i, i ^ 1) for i in range(sections)]
        pair = [(i, i ^ 1) for i in range(wides)]
        frame = (NB, z.rows, 256)
        framed = pltpu.VMEM((NB, z.rows + 16, 256), F32)
        band_buf = pltpu.VMEM((z.mb, z.band, z.span), BF16)
        edge_buf = pltpu.VMEM((z.mb, 16, z.span), BF16)
        heavy = pl.CostEstimate(flops=4_000_000_000, bytes_accessed=4_000_000, transcendentals=0)

        def call(kernel, name, outs, ins, scratch, out_specs=None, cost=None, alias=None):
            return pl.pallas_call(
                lambda *refs: kernel(z, *refs),
                out_shape=outs,
                in_specs=ins,
                out_specs=out_specs or [VMEM] * len(outs),
                scratch_shapes=scratch,
                compiler_params=PARAMS,
                cost_estimate=cost,
                input_output_aliases=alias or {},
                name=name,
            )

        halo, kernel_own = call(
            edge_kernel,
            "edge",
            [shape(z.sent, HW), shape(COPIES, NK)],
            [HBM] * 4,
            [
                edge_buf,
                pltpu.VMEM((z.mb, 16, HW), jnp.int32),
                edge_buf,
                pltpu.VMEM((1, NK), BF16),
                DMA((4,)),
            ],
        )(fields, pixel_mask, cotangent, kernels)
        halo = lax.ppermute(halo, "wide", pair)
        kernel_other = lax.ppermute(kernel_own, "section", swap)
        pixels, in_mask, aux = call(
            prepare_kernel,
            "prepare",
            [
                shape(z.own, NB * 128),
                shape(z.own, NB * 128),
                shape(56, 128, dtype=F32),
            ],
            [VMEM] * 2 + [HBM] * 5,
            [
                pltpu.SMEM(channel_counts.shape, jnp.int32),
                pltpu.SMEM(enc_bias.shape, F32),
                pltpu.SMEM(dec_bias.shape, F32),
                pltpu.SMEM(run_mean.shape, F32),
                pltpu.VMEM(run_cov.shape, F32),
                DMA((5,)),
            ],
            cost=heavy,
        )(*whole[:2], channel_counts, enc_bias, dec_bias, run_mean, run_cov)
        (weights,) = call(taps_kernel, "taps", [shape(128, 512)], [VMEM] * 2, [])(
            kernel_own, kernel_other
        )
        coded = [shape(NB, z.rows, KS * 128), shape(*frame), shape(*frame, dtype=F32)]
        taps, code, slope, pay, banded = call(
            inner_kernel,
            "inner",
            coded + [shape(2, 128, dtype=F32), shape(KS * 128, 256)],
            [VMEM] * 4,
            [pltpu.VMEM((NB, z.own // 2 + 16, 256), F32)],
            cost=heavy,
        )(pixels, in_mask, weights, aux)
        taps, code, slope, halo_cot, pay = call(
            encode_kernel,
            "encode",
            coded + [shape(z.halo, NB * 128), shape(2, 128, dtype=F32)],
            [VMEM] * 9,
            [pltpu.VMEM((NB, 64, 256), F32)],
            alias={6: 0, 7: 1, 8: 2},
        )(pixels, in_mask, halo, banded, aux, pay, taps, code, slope)
        pay = jnp.broadcast_to(pay[None], (sections * wides, 2, 128))
        stats = lax.all_to_all(pay, ("section", "wide"), 0, 0)
        sent, decode_pay = call(
            decode_kernel,
            "decode",
            [shape(*frame), shape(CCODE, 128, dtype=F32)],
            [VMEM] * 6,
            [framed, framed],
            cost=heavy,
        )(whole[2], code, in_mask, halo_cot, weights, aux)
        grad, pay, moments = call(
            whiten_kernel,
            "whiten",
            [
                shape(*frame),
                shape(sections, CCODE, 128),
                shape(CCODE + 8, 128, dtype=F32),
            ],
            [VMEM] * 7,
            [],
            alias={3: 0},
        )(stats, code, slope, sent, taps, decode_pay, aux)
        pay = jnp.broadcast_to(pay[:, None], (sections, wides, CCODE, 128))
        pay = pay.reshape(sections * wides, CCODE, 128)
        parts = lax.all_to_all(pay, ("section", "wide"), 0, 0)
        (sending,) = call(
            send_kernel,
            "send",
            [shape(z.mb, z.band, z.span)],
            [VMEM] * 5,
            [framed],
            cost=heavy,
        )(grad, code, in_mask, weights, aux)
        arrived = lax.ppermute(sending, "section", swap)
        half_done, onehot, new_mean, new_cov = call(
            keep_kernel,
            "keep",
            [
                shape(1, z.micro, z.band, z.span),
                shape(128, NK),
                shape(1, CCODE, dtype=F32),
                shape(CCODE, CCODE, dtype=F32),
            ],
            [VMEM] * 6,
            [
                framed,
                band_buf,
                pltpu.VMEM((1, CCODE), F32),
                pltpu.VMEM((CCODE, CCODE), F32),
                DMA((3,)),
            ],
            out_specs=[HBM, VMEM, HBM, HBM],
            cost=heavy,
        )(grad, code, in_mask, weights, aux, moments)
        (sums,) = call(
            total_kernel,
            "total",
            [shape(CCODE, 128, dtype=F32)],
            [VMEM],
            [],
            cost=pl.CostEstimate(flops=100_000_000_000, bytes_accessed=0, transcendentals=0),
        )(parts)
        pixels_out, kernel_grads, enc_grad, dec_grad = call(
            finish_kernel,
            "finish",
            [
                shape(1, z.micro, z.band, z.span),
                shape(1, NK, dtype=F32),
                shape(1, CCODE, dtype=F32),
                shape(1, CIN, dtype=F32),
            ],
            [VMEM] * 3 + [HBM],
            [
                pltpu.VMEM((1, NK), F32),
                pltpu.VMEM((1, CCODE), F32),
                pltpu.VMEM((1, CIN), F32),
                DMA((4,)),
            ],
            out_specs=[HBM] * 4,
            alias={3: 0},
        )(sums, arrived, onehot, half_done)
        return (
            pixels_out,
            kernel_grads,
            enc_grad.reshape(CCODE),
            dec_grad.reshape(CIN),
            new_mean.reshape(CCODE),
            new_cov,
        )

    return run


def solution(mesh):
    in_specs = (
        P(None, "wide", None),
        P(None, "wide", None),
        P(),
        P("section", None),
        P(),
        P(),
        P(None, "wide", None),
        P(),
        P(),
    )
    out_specs = (P("section", None, "wide", None), P("section", None), P(), P(), P(), P())
    run = shards(mesh.shape["section"], mesh.shape["wide"])
    return jax.shard_map(run, mesh=mesh, in_specs=in_specs, out_specs=out_specs, check_vma=False)
```

```python
import jax
import jax.numpy as jnp
from jax import lax
from jax.experimental import pallas as pl
from jax.experimental.pallas import tpu as pltpu
from jax.sharding import PartitionSpec as P

CIN = 4
CCODE = 16
KS = 5
HW = 128

UW = 16
NB = 5
HALO = 8
NK = CCODE * CIN * KS * KS
COPIES = 32

decay_rate = 0.9
whiten_weight = 0.25

F32 = jnp.float32
BF16 = jnp.bfloat16


def iota(shape, dim):
    return lax.broadcasted_iota(jnp.int32, shape, dim)


def hot(mask):
    return jnp.where(mask, 1.0, 0.0).astype(BF16)


def dot(a, b, dims=((1,), (0,))):
    return lax.dot_general(a, b, (dims, ((), ())), preferred_element_type=F32)


def fold(x, unit):
    rolled = [x] + [pltpu.roll(x, step, 1) for step in range(unit, 128, unit)]
    while len(rolled) > 1:
        rolled = [sum(rolled[i : i + 2]) for i in range(0, len(rolled), 2)]
    return rolled[0]


def lanes_from(x, source):
    return jnp.take_along_axis(x, source, axis=1, mode="promise_in_bounds")


class Sizes:
    def __init__(self, fields, sections):
        self.micro, self.band, self.span = fields
        self.sections = sections
        self.mb = self.micro // sections
        self.jf = self.band // 2 + HALO // 2
        self.rows = self.jf * self.mb
        self.own = self.mb * self.band
        self.halo = self.mb * HALO
        self.shift = self.mb.bit_length() - 1
        self.frame = NB * self.rows
        self.near = self.halo // 2
        self.sent = CIN * (self.halo + self.near) + self.near


def tap_target(n):
    o = (n * 5243) >> 19
    t = n - 100 * o
    c = (t * 1311) >> 15
    t = t - 25 * c
    k = (t * 205) >> 10
    l = t - 5 * k
    return (3 * k + (l >> 1)) * 8 + 2 * c + (l & 1), o


def row_target(z, row):
    half = z.own // 2
    parity = (row >= half).astype(jnp.int32)
    q = row - parity * half
    return (q & (z.mb - 1)) * z.band + 2 * (q >> z.shift) + parity


def gather_rows(z):
    return hot(iota((z.own, z.own), 1) == row_target(z, iota((z.own, 1), 0)))


def scatter_rows(z):
    return hot(iota((z.own, z.own), 0) == row_target(z, iota((1, z.own), 1)))


def pixel_target(lane, inner):
    u_local = (lane >> 3) & (UW - 1)
    u = (lane >> 7) * (UW - 2) + u_local - 1
    valid = (u >= 0) & (u < HW // 2)
    if inner:
        valid = valid & (u_local >= 1) & (u_local <= UW - 2)
    return 2 * u + (lane & 1), (lane >> 1) & 3, valid


def window_columns():
    col, c, valid = pixel_target(iota((1, NB * 128), 1), False)
    target = jnp.where(valid, c * HW + col, -1)
    return hot(iota((CIN * HW, NB * 128), 0) == target)


def unwindow_columns():
    col, c, valid = pixel_target(iota((NB * 128, 1), 0), True)
    target = jnp.where(valid, c * HW + col, -1)
    return hot(iota((NB * 128, CIN * HW), 1) == target)


def window_mask_columns():
    col, _, valid = pixel_target(iota((1, NB * 128), 1), False)
    return hot(iota((HW, NB * 128), 0) == jnp.where(valid, col, -1))


def code_mask_lanes():
    lane = iota((1, 256), 1)
    u_local = lane >> 4
    inner = (u_local >= 1) & (u_local <= UW - 2)
    return hot(iota((128, 256), 0) == jnp.where(inner, u_local * 8, -1))


def own_rows(z, odd):
    j = (iota((z.rows, 1), 0) >> z.shift) - odd * (HALO // 2)
    return (j >= 0) & (j < z.band // 2)


def places(z, odd):
    own = pl.multiple_of(odd * (z.halo // 2), 16)
    halo = pl.multiple_of((1 - odd) * (z.own // 2), 16)
    return own, halo


def mend_coarse(blocks):
    last = HW // 2 - (NB - 1) * (UW - 2)
    rows = blocks[0].shape[0]
    lane = iota((rows, 128), 1)
    halves = [(x[:, :128], x[:, 128:]) for x in blocks]
    done = []
    for b, (low, high) in enumerate(halves):
        before = pltpu.roll(halves[b - 1][1], 32, 1) if b else 0.0
        new_low = jnp.where(lane < 16, before, low)
        if b + 1 < NB:
            after = pltpu.roll(halves[b + 1][0], 96, 1)
            new_high = jnp.where(lane >= 112, after, high)
        else:
            new_high = jnp.where(lane < (last + 1) * 16 - 128, high, 0.0)
        done.append((new_low, new_high))
    return done


def mend_fine(halves):
    rows = halves[0][0].shape[0]
    lane = iota((rows, 128), 1)
    done = []
    for b in range(NB):
        pair = []
        for h in range(2):
            x = halves[b][h]
            before = pltpu.roll(halves[b - 1][h], 16, 1) if b else 0.0
            after = pltpu.roll(halves[b + 1][h], 112, 1) if b + 1 < NB else 0.0
            x = jnp.where(lane < 8, before, x)
            pair.append(jnp.where(lane >= 120, after, x))
        done.append(tuple(pair))
    return done


def pad_frame(z, sh):
    zeros = jnp.zeros((NB, 8, 256), F32)
    sh[:, 0:8, :] = zeros
    sh[:, 8 + z.rows : 16 + z.rows, :] = zeros


def put_frame(z, sh, halves):
    pad_frame(z, sh)
    for b, (low, high) in enumerate(halves):
        sh[b, 8 : 8 + z.rows, 0:128] = low
        sh[b, 8 : 8 + z.rows, 128:256] = high


def put_pixels(z, sh, odd, own, halo):
    pad_frame(z, sh)
    for start, part in zip(places(z, odd), (own, halo)):
        half = part.shape[0] // 2
        rows = pl.ds(pl.multiple_of(8 + start, 8), half)
        for b in range(NB):
            for h in range(2):
                sh[b, rows, h * 128 : h * 128 + 128] = part[
                    h * half : h * half + half, b * 128 : b * 128 + 128
                ]


def fine_taps(z, sh, b):
    up = sh[b, 8 - z.mb : 8 - z.mb + z.rows, :]
    here = sh[b, 8 : 8 + z.rows, :]
    down = sh[b, 8 + z.mb : 8 + z.mb + z.rows, 0:128]
    return jnp.concatenate([up, here, down], axis=1).astype(BF16)


def coarse_taps(z, sh, b):
    down = sh[b, 8 + z.mb : 8 + z.mb + z.rows, :]
    here = sh[b, 8 : 8 + z.rows, :]
    up = sh[b, 8 - z.mb : 8 - z.mb + z.rows, :]
    return [x.astype(BF16) for x in (down, here, up)]


def spread(z, sh, weights):
    taps = [coarse_taps(z, sh, b) for b in range(NB)]
    down, here, up = (jnp.concatenate([t[i] for t in taps], axis=0) for i in range(3))
    nt = ((1,), (1,))
    out = dot(down, weights[0:256], nt) + dot(here, weights[256:512], nt)
    extra = dot(up, weights[512:640], nt)
    return out[:, :128] + extra, out[:, 128:]


def pick_taps(grads):
    lane = iota((CCODE, 128), 1)
    place = lane >> 3
    pieces = []
    for k in range(KS):
        for shift in (-1, 0, 1):
            total = jnp.zeros((CCODE, 128), F32)
            for u in range(1, UW - 1):
                part = grads[u * 16 : u * 16 + 16, k * 128 : k * 128 + 128]
                total = jnp.where(place == u + shift, part, total)
            pieces.append(total)
    pieces.append(jnp.zeros((CCODE, 128), F32))
    block = lane >> 5
    fours = []
    for first in range(4):
        group = pieces[first::4]
        parts = []
        for j in range(4):
            x = group[j]
            for t in range(1, 4):
                x = jnp.where(block == t, group[(t + j) & 3], x)
            parts.append(x)
        fours.append(
            (parts[0] + pltpu.roll(parts[1], 32, 1))
            + (pltpu.roll(parts[2], 64, 1) + pltpu.roll(parts[3], 96, 1))
        )
    inner = place & 3
    total = None
    for j in range(4):
        x = fours[j]
        for t in range(1, 4):
            x = jnp.where(inner == t, fours[(t + j) & 3], x)
        if j:
            x = jnp.where(inner >= j, pltpu.roll(x, 8 * j, 1), pltpu.roll(x, 96 + 8 * j, 1))
        total = x if total is None else total + x
    return total


def own_frame(z, odd, sh):
    start, _ = places(z, odd)
    half = z.own // 2
    rows = pl.ds(pl.multiple_of(8 + start, 8), half)
    flat = jnp.concatenate(
        [
            jnp.concatenate(
                [sh[b, rows, h * 128 : h * 128 + 128] for b in range(NB)], axis=1
            )
            for h in range(2)
        ],
        axis=0,
    )
    return flat.astype(BF16)


def kernel_rows(flat):
    taps = CIN * KS * KS
    pad = jnp.zeros((1, 256 - NK % 128), F32)
    flat = jnp.concatenate([flat, pad], axis=1)
    lane = iota((1, 128), 1)
    row = iota((CCODE, 128), 0)
    rows = jnp.zeros((CCODE, 128), F32)
    for o in range(CCODE):
        chunk, shift = divmod(o * taps, 128)
        x = flat[:, chunk * 128 : chunk * 128 + 128]
        if shift:
            after = flat[:, chunk * 128 + 128 : chunk * 128 + 256]
            x = jnp.where(
                lane < 128 - shift,
                pltpu.roll(x, 128 - shift, 1),
                pltpu.roll(after, 128 - shift, 1),
            )
        rows = jnp.where(row == o, jnp.broadcast_to(x, (CCODE, 128)), rows)
    return rows


def spread_taps(kernel_pair):
    taps = CIN * KS * KS
    rows = jnp.concatenate([kernel_rows(x) for x in kernel_pair for _ in range(8)], axis=0)
    lane = iota((1, 128), 1)
    target, _ = tap_target(jnp.minimum(lane, taps - 1))
    slots = hot(iota((128, 128), 0) == jnp.where(lane < taps, target, -1))
    wide = dot(slots, rows.T.astype(BF16)).astype(BF16)
    halves = [wide[:, 0:128], wide[:, 128:256]]
    return jnp.concatenate([x for x in halves for _ in range(2)], axis=1)


def band_weights(wide_taps):
    wide_taps = wide_taps.astype(F32)
    row_u = iota((128, 256), 0) >> 3
    lane_u = iota((128, 256), 1) >> 4
    masks = [row_u == lane_u + shift for shift in (-1, 0, 1)]
    parts = []
    for k in range(KS):
        total = jnp.zeros((128, 256), F32)
        for i, mask in enumerate(masks):
            q = 3 * k + i
            piece = wide_taps[8 * q : 8 * q + 8]
            piece = jnp.broadcast_to(piece[None], (16, 8, 256)).reshape(128, 256)
            total = jnp.where(mask, piece, total)
        parts.append(total.astype(BF16))
    return jnp.concatenate(parts, axis=0)


def edge_kernel(
    z, fields, mask, cotangent, kernel, out, kernel_out,
    field_buf, mask_buf, cot_buf, kernel_buf, sems,
):
    odd = lax.rem(lax.axis_index("wide"), 2)
    first = lax.axis_index("section") * z.mb
    start = pl.multiple_of((1 - odd) * (z.band - 16), 16)
    copies = [
        pltpu.make_async_copy(
            source.at[pl.ds(first, z.mb), pl.ds(start, 16), :], buf, sems.at[i]
        )
        for i, (source, buf) in enumerate(
            ((fields, field_buf), (mask, mask_buf), (cotangent, cot_buf))
        )
    ]
    copies.append(pltpu.make_async_copy(kernel, kernel_buf, sems.at[3]))
    for copy in copies:
        copy.start()
    for copy in copies:
        copy.wait()
    kernel_out[...] = jnp.broadcast_to(kernel_buf[...].astype(F32), (COPIES, NK)).astype(BF16)

    def beside(buf):
        rows = buf[...].astype(F32)
        return jnp.where(odd == 1, rows[:, :HALO], rows[:, HALO:])

    def ordered(rows, firsts):
        return jnp.concatenate(
            [rows[:, j + h] for h in range(2) for j in firsts], axis=0
        ).astype(BF16)

    mask_rows = beside(mask_buf)
    allowed = jnp.concatenate([mask_rows] * CIN, axis=2)
    every, half = range(0, HALO, 2), range(0, HALO // 2, 2)
    near = beside(cot_buf) * allowed
    near = jnp.where(odd == 1, near[:, : HALO // 2], near[:, HALO // 2 :])
    pieces = ordered(beside(field_buf) * allowed, every), ordered(near, half)
    start = 0
    for piece in pieces:
        count = piece.shape[0]
        for c in range(CIN):
            out[start : start + count, :] = piece[:, c * HW : c * HW + HW]
            start += count
    out[start : z.sent, :] = ordered(mask_rows, every)[0 : z.near]


def prepare_kernel(
    z, fields, mask, counts, enc_bias, dec_bias, run_mean, run_cov,
    pixels_out, inmask_out, aux_out,
    count_buf, enc_buf, dec_buf, mean_buf, cov_buf, sems,
):
    section = lax.axis_index("section")
    wide = lax.axis_index("wide")
    first = section * z.mb
    mine_rows = pl.ds(first, z.mb)
    copies = [
        pltpu.make_async_copy(source, buf, sems.at[i])
        for i, (source, buf) in enumerate(
            (
                (counts, count_buf),
                (enc_bias, enc_buf),
                (dec_bias, dec_buf),
                (run_mean, mean_buf),
                (run_cov, cov_buf),
            )
        )
    ]
    for copy in copies:
        copy.start()
    gather = gather_rows(z)
    columns = window_columns()
    mask_columns = window_mask_columns()
    pixel_mask = mask[mine_rows].astype(F32).astype(BF16).reshape(z.own, HW)
    pixels = fields[mine_rows].reshape(z.own, z.span)
    framed = dot(gather, jnp.concatenate([pixel_mask, pixels], axis=1)).astype(BF16)
    in_mask = dot(framed[:, 0:HW], mask_columns)
    windowed = dot(framed[:, HW:], columns)
    for copy in copies:
        copy.wait()
    lane = iota((8, 128), 1)
    dec_row = jnp.zeros((8, 128), F32)
    for c in range(CIN):
        dec_row = jnp.where(((lane >> 1) & 3) == c, dec_buf[c], dec_row)
    enc_row = jnp.zeros((8, 128), F32)
    mean_row = jnp.zeros((8, 128), F32)
    for o in range(CCODE):
        enc_row = jnp.where((lane & 15) == o, enc_buf[o], enc_row)
        mean_row = jnp.where((lane & 15) == o, mean_buf[o], mean_row)
    aux_out[0:8] = dec_row
    aux_out[8:16] = enc_row
    aux_out[16:24] = mean_row
    aux_out[24:40] = jnp.zeros((16, 128), F32)
    aux_out[24:40, 0:CCODE] = cov_buf[...]
    field_now = wide * z.band // HW
    micro = iota((16, 128), 0) & (z.mb - 1)
    count = jnp.zeros((16, 128), jnp.int32)
    for m in range(z.mb):
        count = jnp.where(micro == m, count_buf[first + m, field_now], count)
    channel_ok = jnp.where(((iota((16, 128), 1) >> 1) & 3) < count, 1.0, 0.0)
    aux_out[40:56] = channel_ok
    in_mask = in_mask * jnp.tile(channel_ok, (z.own // 16, NB))
    inmask_out[...] = in_mask.astype(BF16)
    pixels_out[...] = (windowed * in_mask).astype(BF16)


def taps_kernel(z, kernel_own, kernel_other, weights_out):
    mine, other = (x[0:16].astype(F32)[0:1] for x in (kernel_own, kernel_other))
    leads = lax.axis_index("section") == 0
    weights_out[...] = spread_taps((jnp.where(leads, mine, other), jnp.where(leads, other, mine)))


def local_taps(sh, b, rows, step):
    up = sh[b, 16 - step : 16 - step + rows, :]
    here = sh[b, 16 : 16 + rows, :]
    down = sh[b, 16 + step : 16 + step + rows, 0:128]
    return jnp.concatenate([up, here, down], axis=1).astype(BF16)


def encode_rows(taps, banded, bias, masks, mine):
    code_mask = dot(masks, code_mask_lanes())
    pre = dot(taps, banded) + bias
    slope = jnp.exp(jnp.minimum(pre, 0.0))
    code = jnp.where(pre > 0, pre, slope - 1.0).astype(BF16).astype(F32)
    slope = jnp.where(code_mask > 0.5, slope, -slope)
    allowed = code_mask if mine is None else jnp.where(mine, code_mask, 0.0)
    weighted = code * allowed
    halves = [
        jnp.concatenate([x[:, 0:128], x[:, 128:256]], axis=0).astype(BF16) for x in (weighted, code)
    ]
    second = dot(*halves, ((0,), (0,)))
    sums = [jnp.sum(x, axis=0, keepdims=True) for x in (weighted, allowed)]
    lane_u = iota((16, 128), 1) >> 4
    total = second[0:16]
    for u in range(1, UW // 2):
        total = jnp.where(lane_u == u, second[u * 16 : u * 16 + 16], total)
    total = fold(total, 16)
    diagonal = (iota((8, 128), 1) >> 4) == iota((8, 128), 0)
    pay = [
        jnp.sum(jnp.where(diagonal, total[h * 8 : h * 8 + 8], 0.0), axis=0, keepdims=True)
        for h in range(2)
    ]
    first, count = (
        fold(jnp.broadcast_to(x[:, :128] + x[:, 128:], (8, 128)), 16) for x in sums
    )
    lane = iota((8, 128), 1)
    inner, group = lane & 15, lane >> 4
    first = lanes_from(first, jnp.where(inner == 0, group, group + 8))
    spare = jnp.where(inner == 2, count, first)[0:1]
    pay[1] = jnp.where(inner[0:1] < 8, spare, pay[1])
    return code, slope, jnp.concatenate(pay, axis=0)


def inner_kernel(
    z, pixels, own_mask, weights, aux, taps_out, code_out, slope_out, pay_out, band_out, sh
):
    odd = lax.rem(lax.axis_index("wide"), 2)
    half = z.own // 2
    count = half - 16
    zeros = jnp.zeros((NB, 16, 256), F32)
    sh[:, 0:16, :] = zeros
    sh[:, half : half + 16, :] = zeros
    here = pl.ds(pl.multiple_of((1 - odd) * 16, 16), half)
    for b in range(NB):
        for h in range(2):
            sh[b, here, h * 128 : h * 128 + 128] = pixels[
                h * half : h * half + half, b * 128 : b * 128 + 128
            ].astype(F32)
    start = pl.multiple_of(odd * 32, 16)
    taps = [local_taps(sh, b, count, z.mb) for b in range(NB)]
    for b in range(NB):
        taps_out[b, pl.ds(start, count), :] = taps[b]
    kept = pl.ds(pl.multiple_of(odd * 16, 16), count)
    masks = jnp.concatenate([own_mask[kept, b * 128 : b * 128 + 128] for b in range(NB)], axis=0)
    bias = jnp.concatenate([aux[8:9], aux[8:9]], axis=1)
    banded = band_weights(weights[:, 0:256])
    band_out[...] = banded
    code, slope, pay = encode_rows(jnp.concatenate(taps, axis=0), banded, bias, masks, None)
    pay_out[...] = pay
    for b in range(NB):
        rs = slice(b * count, b * count + count)
        code_out[b, pl.ds(start, count), :] = code[rs].astype(BF16)
        slope_out[b, pl.ds(start, count), :] = slope[rs]


def encode_kernel(
    z, pixels, own_mask, halo, banded, aux, inner_pay, taps_in, code_in, slope_in,
    taps_out, code_out, slope_out, cot_out, pay_out,
    sh,
):
    odd = lax.rem(lax.axis_index("wide"), 2)
    half = z.own // 2
    count = 32
    channel_ok = jnp.tile(aux[40:56], (1, NB))
    middle, end = CIN * z.halo, CIN * (z.halo + z.near)
    halo_mask = dot(halo[end : z.sent, :], window_mask_columns())
    halo_rows = [
        jnp.concatenate([halo[i : i + count, :] for i in range(start, stop, count)], axis=1)
        for start, stop, count in ((0, middle, z.halo), (middle, end, z.near))
    ]
    halo_pixels = dot(jnp.concatenate(halo_rows, axis=0), window_columns())
    halo_x = halo_pixels[0 : z.halo] * jnp.tile(channel_ok, (2, 1))
    zeros = jnp.zeros((NB, 16, 256), F32)
    sh[:, 0:16, :] = zeros
    sh[:, 48:64, :] = zeros
    own_start = pl.multiple_of((1 - odd) * (half - 32), 16)
    own_there = pl.ds(pl.multiple_of(odd * 32, 16), 32)
    halo_there = pl.ds(pl.multiple_of((2 - odd) * 16, 16), 16)
    for b in range(NB):
        for h in range(2):
            cs = slice(b * 128, b * 128 + 128)
            own = pixels[pl.ds(pl.multiple_of(own_start + h * half, 16), 32), cs]
            sh[b, own_there, h * 128 : h * 128 + 128] = own.astype(F32)
            sh[b, halo_there, h * 128 : h * 128 + 128] = halo_x[h * 16 : h * 16 + 16, cs]
    start = pl.multiple_of((1 - odd) * (z.rows - count), 16)
    taps = [local_taps(sh, b, count, z.mb) for b in range(NB)]
    for b in range(NB):
        taps_out[b, pl.ds(start, count), :] = taps[b]
    edge_mask = own_mask[pl.ds(pl.multiple_of((1 - odd) * (half - 16), 16), 16), :].astype(F32)
    first = jnp.where(odd == 1, halo_mask, edge_mask)
    later = jnp.where(odd == 1, edge_mask, halo_mask)
    masks = jnp.concatenate(
        [x[:, b * 128 : b * 128 + 128] for b in range(NB) for x in (first, later)], axis=0
    ).astype(BF16)
    bias = jnp.concatenate([aux[8:9], aux[8:9]], axis=1)
    mine = ((iota((NB * count, 1), 0) >> 4) & 1) == odd
    code, slope, pay = encode_rows(jnp.concatenate(taps, axis=0), banded[...], bias, masks, mine)
    pay = pay + inner_pay[...]
    pay_out[...] = pay
    for b in range(NB):
        rs = slice(b * count, b * count + count)
        code_out[b, pl.ds(start, count), :] = code[rs].astype(BF16)
        slope_out[b, pl.ds(start, count), :] = slope[rs]
    near = halo_pixels[z.halo : z.halo + z.near] * channel_ok
    nothing = jnp.zeros((8, NB * 128), F32)
    for h in range(2):
        rows = near[h * 8 : h * 8 + 8]
        rows = [jnp.where(odd == 1, nothing, rows), jnp.where(odd == 1, rows, nothing)]
        cot_out[h * 16 : h * 16 + 16, :] = jnp.concatenate(rows, axis=0).astype(BF16)


def decode_kernel(
    z, cotangent, code, in_mask, halo_cot, weights, aux,
    sent_out, pay_out,
    sh, cot_frame,
):
    odd = lax.rem(lax.axis_index("wide"), 2)
    mine = pl.ds(lax.axis_index("section") * z.mb, z.mb)
    rows = z.rows
    put_frame(z, sh, mend_coarse([code[b].astype(F32) for b in range(NB)]))
    banded = band_weights(weights[:, 256:512])
    raws = spread(z, sh, banded)
    gather = gather_rows(z)
    columns = window_columns()
    own_cot = dot(dot(gather, cotangent[mine].reshape(z.own, z.span)).astype(BF16), columns)
    put_pixels(z, cot_frame, odd, own_cot * in_mask[...].astype(F32), halo_cot[...].astype(F32))
    mine_rows = own_rows(z, odd)
    u_local = (iota((1, 128), 1) >> 3) & (UW - 1)
    inner = mine_rows & (u_local >= 1) & (u_local <= UW - 2)
    grads = []
    bias_sum = jnp.zeros((1, 128), F32)
    for h in range(2):
        raw = raws[h] + aux[0:1]
        slope = jnp.exp(jnp.minimum(raw, 0.0))
        cs = slice(h * 128, h * 128 + 128)
        for b in range(NB):
            rs = slice(b * rows, b * rows + rows)
            grad = (cot_frame[b, 8 : 8 + rows, cs] * slope[rs]).astype(BF16).astype(F32)
            bias_sum = bias_sum + jnp.sum(jnp.where(inner, grad, 0.0), axis=0, keepdims=True)
            grads.append(grad)
    put_frame(z, sh, mend_fine([(grads[b], grads[NB + b]) for b in range(NB)]))
    taps = jnp.concatenate([fine_taps(z, sh, b) for b in range(NB)], axis=0)
    sent_out[...] = dot(taps, banded).astype(BF16).reshape(NB, rows, 256)
    last = HW // 2 - (NB - 1) * (UW - 2)
    within = mine_rows & ((iota((1, 256), 1) >> 4) <= last)
    mine = jnp.concatenate(
        [
            jnp.where(within if b == NB - 1 else mine_rows, code[b].astype(F32), 0.0).astype(BF16)
            for b in range(NB)
        ],
        axis=0,
    )
    pay = pick_taps(dot(mine, taps, ((0,), (0,))))
    bias_sum = fold(jnp.broadcast_to(bias_sum, (16, 128)), 8)
    lane = iota((16, 128), 1)
    keep = (lane < 8) & ((lane >> 1) == iota((16, 128), 0))
    column = jnp.sum(jnp.where(keep, bias_sum, 0.0), axis=1, keepdims=True)
    pay_out[...] = jnp.where(lane >= 120, column, pay)


def whiten_kernel(
    z, stats, code, slope, sent, taps, decode_pay, aux,
    grad_out, pay_out, moments_out,
):
    odd = lax.rem(lax.axis_index("wide"), 2)
    rows = z.rows
    pay = jnp.sum(stats[...], axis=0)
    lane = iota((8, 128), 1)
    inner, step = lane & 15, iota((8, 128), 0)
    low, high = (jnp.broadcast_to(pay[h : h + 1], (8, 128)) for h in range(2))
    count = lanes_from(high, jnp.full((8, 128), 2, jnp.int32))[0:1]
    first = lanes_from(high, jnp.where(inner < 8, 16 * inner, 16 * (inner - 8) + 1))[0:1]
    mean = first / count
    columns = jnp.concatenate([lanes_from(high, 16 * step + h) for h in range(2)], axis=0)
    diagonal = (lane >> 4) == step
    mirrored = lanes_from(low, jnp.where(inner < 8, 16 * inner + 8 + step, 0))
    low, high = (fold(jnp.where(diagonal, x, 0.0), 16) for x in (low, high))
    second = jnp.concatenate([low, jnp.where(inner < 8, mirrored, high)], axis=0)
    lane = iota((16, 128), 1)
    row = iota((16, 128), 0)
    wide_mean = jnp.broadcast_to(mean, (16, 128))
    total = jnp.broadcast_to(count, (16, 128))
    mean_column = columns / total
    cov = second / total - mean_column * wide_mean
    moments_out[0:CCODE] = cov
    moments_out[CCODE:] = jnp.broadcast_to(mean, (8, 128))
    offset = cov - jnp.where((lane & 15) == row, 1.0, 0.0)
    pulled = jnp.sum(offset * mean_column, axis=0, keepdims=True)
    linear = whiten_weight * mean - 2.0 * whiten_weight * pulled
    linear = jnp.concatenate([linear, linear], axis=1)
    matrix = jnp.tile(2.0 * whiten_weight * offset, (8, 1))
    matrix = jnp.where((iota((128, 128), 0) >> 4) == (iota((128, 128), 1) >> 4), matrix, 0.0)
    high = matrix.astype(BF16)
    matrix = jnp.concatenate([high, (matrix - high.astype(F32)).astype(BF16)], axis=0)
    flat = code[...].reshape(z.frame, 256)
    flat = jnp.concatenate(
        [jnp.concatenate([x, x], axis=1) for x in (flat[:, 0:128], flat[:, 128:256])], axis=0
    )
    turned = dot(flat, matrix)
    turned = jnp.concatenate([turned[0 : z.frame], turned[z.frame :]], axis=1) + linear
    mine_rows = own_rows(z, odd)
    lane_u = iota((1, 256), 1) >> 4
    inner = mine_rows & (lane_u >= 1) & (lane_u <= UW - 2)
    last = HW // 2 - (NB - 1) * (UW - 2)
    blocks, mine = [], []
    bias_sum = jnp.zeros((1, 256), F32)
    for b in range(NB):
        signed = slope[b]
        pull = jnp.where(signed > 0, turned[b * rows : b * rows + rows], 0.0)
        grad = ((sent[b].astype(F32) + pull) * jnp.abs(signed)).astype(BF16).astype(F32)
        kept = jnp.where(inner & (lane_u <= last) if b == NB - 1 else inner, grad, 0.0)
        bias_sum = bias_sum + jnp.sum(kept, axis=0, keepdims=True)
        blocks.append(grad)
        mine.append(kept.astype(BF16))
    products = dot(
        jnp.concatenate(mine, axis=0), taps[...].reshape(z.frame, KS * 128), ((0,), (0,))
    )
    encode_pay = pick_taps(products)
    bias_sum = fold(jnp.broadcast_to(bias_sum[:, :128] + bias_sum[:, 128:], (16, 128)), 16)
    column = jnp.sum(jnp.where(lane == row, bias_sum, 0.0), axis=1, keepdims=True)
    decoded = decode_pay[...]
    biases = jnp.where((lane & 1) == 0, column, decoded)
    coarse = biases.astype(BF16).astype(F32)
    biases = jnp.where((lane & 2) == 0, coarse, biases - coarse)
    encode_pay = jnp.where(lane >= 120, biases, encode_pay)
    decoded = jnp.where(lane >= 120, biases, decoded)
    pay_out[0] = encode_pay.astype(BF16)
    pay_out[1] = decoded.astype(BF16)
    for b, (low, high) in enumerate(mend_coarse(blocks)):
        grad_out[b, :, 0:128] = low.astype(BF16)
        grad_out[b, :, 128:256] = high.astype(BF16)


def picture(z, decodes, grad, code, in_mask, weights, aux, sh):
    odd = lax.rem(lax.axis_index("wide"), 2)
    rows = z.rows
    frames = [
        jnp.where(decodes, code[b].astype(F32), grad[b].astype(F32)) for b in range(NB)
    ]
    put_frame(z, sh, mend_coarse(frames))
    chosen = jnp.where(decodes, weights[:, 256:512].astype(F32), weights[:, 0:256].astype(F32))
    raws = spread(z, sh, band_weights(chosen))
    for h in range(2):
        raw = raws[h] + aux[0:1]
        raw = jnp.where(raw > 0, raw, jnp.exp(jnp.minimum(raw, 0.0)) - 1.0)
        raw = jnp.where(decodes, raw, raws[h])
        for b in range(NB):
            sh[b, 8 : 8 + rows, h * 128 : h * 128 + 128] = raw[b * rows : b * rows + rows]
    flat = own_frame(z, odd, sh) * in_mask[...]
    native = dot(flat, unwindow_columns()).astype(BF16)
    return dot(scatter_rows(z), native).astype(BF16).reshape(z.mb, z.band, z.span)


def send_kernel(z, grad, code, in_mask, weights, aux, send_out, sh):
    decodes = lax.axis_index("section") == 0
    send_out[...] = picture(z, decodes, grad, code, in_mask, weights, aux, sh)


def keep_kernel(
    z, grad, code, in_mask, weights, aux, moments,
    pixels_out, mean_out, cov_out,
    sh, mine, means, covs, sems,
):
    section = lax.axis_index("section")
    means[...] = decay_rate * aux[16:17, 0:CCODE] + (1.0 - decay_rate) * moments[16:17, 0:CCODE]
    covs[...] = decay_rate * aux[24:40, 0:CCODE] + (1.0 - decay_rate) * moments[0:16, 0:CCODE]
    mine[...] = picture(z, section == 1, grad, code, in_mask, weights, aux, sh)
    copies = [
        pltpu.make_async_copy(source, target, sems.at[i])
        for i, (source, target) in enumerate(
            (
                (mine, pixels_out.at[0, pl.ds(section * z.mb, z.mb)]),
                (means, mean_out),
                (covs, cov_out),
            )
        )
    ]
    for copy in copies:
        copy.start()
    for copy in copies:
        copy.wait()


def total_kernel(z, parts, out):
    out[...] = jnp.sum(parts[...].astype(F32), axis=0)


def finish_kernel(
    z, sums, arrived, half_done, pixels_out, kernel_out, enc_out, dec_out,
    kernels, encs, decs, sems,
):
    there = z.micro - z.mb - lax.axis_index("section") * z.mb
    copies = [
        pltpu.make_async_copy(source, target, sems.at[i])
        for i, (source, target) in enumerate(
            (
                (arrived, pixels_out.at[0, pl.ds(there, z.mb)]),
                (encs, enc_out),
                (decs, dec_out),
                (kernels, kernel_out),
            )
        )
    ]
    copies[0].start()
    total = sums[...]
    taps = CIN * KS * KS
    tap = (iota((CCODE, 128), 1) - taps * iota((CCODE, 128), 0)) & 127
    slot, _ = tap_target(jnp.minimum(tap, taps - 1))
    moved = lanes_from(total, slot)
    place = iota((1, 128), 1)
    for chunk in range((NK + 127) // 128):
        out = jnp.zeros((1, 128), F32)
        for o in range(CCODE):
            start = o * taps - chunk * 128
            if -taps < start < 128:
                out = jnp.where((place >= start) & (place < start + taps), moved[o : o + 1], out)
        width = min(128, NK - chunk * 128)
        kernels[:, chunk * 128 : chunk * 128 + width] = out[:, 0:width]
    copies[3].start()
    lane = iota((16, 128), 1)
    row = iota((16, 128), 0)
    for slot, out in ((120, encs), (121, decs)):
        chosen = (lane == slot) | (lane == slot + 2)
        column = jnp.sum(jnp.where(chosen, total, 0.0), axis=1, keepdims=True)
        flat = jnp.sum(jnp.where(lane == row, column, 0.0), axis=0, keepdims=True)
        out[...] = flat[:, 0 : out.shape[1]]
    copies[1].start()
    copies[2].start()
    for copy in copies:
        copy.wait()


VMEM = pl.BlockSpec(memory_space=pltpu.VMEM)
HBM = pl.BlockSpec(memory_space=pltpu.HBM)
PARAMS = pltpu.CompilerParams(vmem_limit_bytes=24 * 1024 * 1024)
DMA = pltpu.SemaphoreType.DMA


def shape(*dims, dtype=BF16):
    return jax.ShapeDtypeStruct(dims, dtype)


def shards(sections, wides):
    def run(
        fields, pixel_mask, channel_counts, kernels, enc_bias, dec_bias, cotangent, run_mean, run_cov
    ):
        z = Sizes(fields.shape, sections)
        assert 2 * z.band == HW and z.span == CIN * HW and z.mb == 4
        whole = (fields, pixel_mask, cotangent)
        (
            fields, cotangent, pixel_mask, kernels, channel_counts, enc_bias, dec_bias,
            run_mean, run_cov,
        ) = (
            pltpu.with_memory_space_constraint(x, pltpu.HBM)
            for x in (
                fields, cotangent, pixel_mask, kernels, channel_counts, enc_bias, dec_bias,
                run_mean, run_cov,
            )
        )
        swap = [(i, i ^ 1) for i in range(sections)]
        pair = [(i, i ^ 1) for i in range(wides)]
        frame = (NB, z.rows, 256)
        framed = pltpu.VMEM((NB, z.rows + 16, 256), F32)
        band_buf = pltpu.VMEM((z.mb, z.band, z.span), BF16)
        edge_buf = pltpu.VMEM((z.mb, 16, z.span), BF16)
        heavy = pl.CostEstimate(flops=4_000_000_000, bytes_accessed=4_000_000, transcendentals=0)

        def call(kernel, name, outs, ins, scratch, out_specs=None, cost=None, alias=None):
            return pl.pallas_call(
                lambda *refs: kernel(z, *refs),
                out_shape=outs,
                in_specs=ins,
                out_specs=out_specs or [VMEM] * len(outs),
                scratch_shapes=scratch,
                compiler_params=PARAMS,
                cost_estimate=cost,
                input_output_aliases=alias or {},
                name=name,
            )

        halo, kernel_own = call(
            edge_kernel,
            "edge",
            [shape(z.sent, HW), shape(COPIES, NK)],
            [HBM] * 4,
            [
                edge_buf,
                pltpu.VMEM((z.mb, 16, HW), jnp.int32),
                edge_buf,
                pltpu.VMEM((1, NK), BF16),
                DMA((4,)),
            ],
        )(fields, pixel_mask, cotangent, kernels)
        halo = lax.ppermute(halo, "wide", pair)
        kernel_other = lax.ppermute(kernel_own, "section", swap)
        pixels, in_mask, aux = call(
            prepare_kernel,
            "prepare",
            [
                shape(z.own, NB * 128),
                shape(z.own, NB * 128),
                shape(56, 128, dtype=F32),
            ],
            [VMEM] * 2 + [HBM] * 5,
            [
                pltpu.SMEM(channel_counts.shape, jnp.int32),
                pltpu.SMEM(enc_bias.shape, F32),
                pltpu.SMEM(dec_bias.shape, F32),
                pltpu.SMEM(run_mean.shape, F32),
                pltpu.VMEM(run_cov.shape, F32),
                DMA((5,)),
            ],
            cost=heavy,
        )(*whole[:2], channel_counts, enc_bias, dec_bias, run_mean, run_cov)
        (weights,) = call(taps_kernel, "taps", [shape(128, 512)], [VMEM] * 2, [])(
            kernel_own, kernel_other
        )
        coded = [shape(NB, z.rows, KS * 128), shape(*frame), shape(*frame, dtype=F32)]
        taps, code, slope, pay, banded = call(
            inner_kernel,
            "inner",
            coded + [shape(2, 128, dtype=F32), shape(KS * 128, 256)],
            [VMEM] * 4,
            [pltpu.VMEM((NB, z.own // 2 + 16, 256), F32)],
            cost=heavy,
        )(pixels, in_mask, weights, aux)
        taps, code, slope, halo_cot, pay = call(
            encode_kernel,
            "encode",
            coded + [shape(z.halo, NB * 128), shape(2, 128, dtype=F32)],
            [VMEM] * 9,
            [pltpu.VMEM((NB, 64, 256), F32)],
            alias={6: 0, 7: 1, 8: 2},
        )(pixels, in_mask, halo, banded, aux, pay, taps, code, slope)
        pay = jnp.broadcast_to(pay[None], (sections * wides, 2, 128))
        stats = lax.all_to_all(pay, ("section", "wide"), 0, 0)
        sent, decode_pay = call(
            decode_kernel,
            "decode",
            [shape(*frame), shape(CCODE, 128, dtype=F32)],
            [VMEM] * 6,
            [framed, framed],
            cost=heavy,
        )(whole[2], code, in_mask, halo_cot, weights, aux)
        grad, pay, moments = call(
            whiten_kernel,
            "whiten",
            [
                shape(*frame),
                shape(sections, CCODE, 128),
                shape(CCODE + 8, 128, dtype=F32),
            ],
            [VMEM] * 7,
            [],
            alias={3: 0},
        )(stats, code, slope, sent, taps, decode_pay, aux)
        pay = jnp.broadcast_to(pay[:, None], (sections, wides, CCODE, 128))
        pay = pay.reshape(sections * wides, CCODE, 128)
        parts = lax.all_to_all(pay, ("section", "wide"), 0, 0)
        (sending,) = call(
            send_kernel,
            "send",
            [shape(z.mb, z.band, z.span)],
            [VMEM] * 5,
            [framed],
            cost=heavy,
        )(grad, code, in_mask, weights, aux)
        arrived = lax.ppermute(sending, "section", swap)
        half_done, new_mean, new_cov = call(
            keep_kernel,
            "keep",
            [
                shape(1, z.micro, z.band, z.span),
                shape(1, CCODE, dtype=F32),
                shape(CCODE, CCODE, dtype=F32),
            ],
            [VMEM] * 6,
            [
                framed,
                band_buf,
                pltpu.VMEM((1, CCODE), F32),
                pltpu.VMEM((CCODE, CCODE), F32),
                DMA((3,)),
            ],
            out_specs=[HBM] * 3,
            cost=heavy,
        )(grad, code, in_mask, weights, aux, moments)
        (sums,) = call(
            total_kernel,
            "total",
            [shape(CCODE, 128, dtype=F32)],
            [VMEM],
            [],
            cost=pl.CostEstimate(flops=100_000_000_000, bytes_accessed=0, transcendentals=0),
        )(parts)
        pixels_out, kernel_grads, enc_grad, dec_grad = call(
            finish_kernel,
            "finish",
            [
                shape(1, z.micro, z.band, z.span),
                shape(1, NK, dtype=F32),
                shape(1, CCODE, dtype=F32),
                shape(1, CIN, dtype=F32),
            ],
            [VMEM] * 2 + [HBM],
            [
                pltpu.VMEM((1, NK), F32),
                pltpu.VMEM((1, CCODE), F32),
                pltpu.VMEM((1, CIN), F32),
                DMA((4,)),
            ],
            out_specs=[HBM] * 4,
            alias={2: 0},
        )(sums, arrived, half_done)
        return (
            pixels_out,
            kernel_grads,
            enc_grad.reshape(CCODE),
            dec_grad.reshape(CIN),
            new_mean.reshape(CCODE),
            new_cov,
        )

    return run


def solution(mesh):
    in_specs = (
        P(None, "wide", None),
        P(None, "wide", None),
        P(),
        P("section", None),
        P(),
        P(),
        P(None, "wide", None),
        P(),
        P(),
    )
    out_specs = (P("section", None, "wide", None), P("section", None), P(), P(), P(), P())
    run = shards(mesh.shape["section"], mesh.shape["wide"])
    return jax.shard_map(run, mesh=mesh, in_specs=in_specs, out_specs=out_specs, check_vma=False)
```

```python
import jax
import jax.numpy as jnp
from jax import lax
from jax.experimental import pallas as pl
from jax.experimental.pallas import tpu as pltpu
from jax.sharding import PartitionSpec as P

CIN = 4
CCODE = 16
KS = 5
HW = 128

UW = 16
NB = 5
HALO = 8
NK = CCODE * CIN * KS * KS
COPIES = 16
PADDED = NK + 192

decay_rate = 0.9
whiten_weight = 0.25

F32 = jnp.float32
BF16 = jnp.bfloat16


def iota(shape, dim):
    return lax.broadcasted_iota(jnp.int32, shape, dim)


def hot(mask):
    return jnp.where(mask, 1.0, 0.0).astype(BF16)


def dot(a, b, dims=((1,), (0,))):
    return lax.dot_general(a, b, (dims, ((), ())), preferred_element_type=F32)


def fold(x, unit):
    rolled = [x] + [pltpu.roll(x, step, 1) for step in range(unit, 128, unit)]
    while len(rolled) > 1:
        rolled = [sum(rolled[i : i + 2]) for i in range(0, len(rolled), 2)]
    return rolled[0]


def lanes_from(x, source):
    return jnp.take_along_axis(x, source, axis=1, mode="promise_in_bounds")


class Sizes:
    def __init__(self, fields, sections):
        self.micro, self.band, self.span = fields
        self.sections = sections
        self.mb = self.micro // sections
        self.jf = self.band // 2 + HALO // 2
        self.rows = self.jf * self.mb
        self.own = self.mb * self.band
        self.halo = self.mb * HALO
        self.shift = self.mb.bit_length() - 1
        self.frame = NB * self.rows
        self.near = self.halo // 2
        self.sent = CIN * (self.halo + self.near) + self.near


def tap_target(n):
    o = (n * 5243) >> 19
    t = n - 100 * o
    c = (t * 1311) >> 15
    t = t - 25 * c
    k = (t * 205) >> 10
    l = t - 5 * k
    return (3 * k + (l >> 1)) * 8 + 2 * c + (l & 1), o


def row_target(z, row):
    half = z.own // 2
    parity = (row >= half).astype(jnp.int32)
    q = row - parity * half
    return (q & (z.mb - 1)) * z.band + 2 * (q >> z.shift) + parity


def gather_rows(z):
    return hot(iota((z.own, z.own), 1) == row_target(z, iota((z.own, 1), 0)))


def scatter_rows(z):
    return hot(iota((z.own, z.own), 0) == row_target(z, iota((1, z.own), 1)))


def pixel_target(lane, inner):
    u_local = (lane >> 3) & (UW - 1)
    u = (lane >> 7) * (UW - 2) + u_local - 1
    valid = (u >= 0) & (u < HW // 2)
    if inner:
        valid = valid & (u_local >= 1) & (u_local <= UW - 2)
    return 2 * u + (lane & 1), (lane >> 1) & 3, valid


def window_columns():
    col, c, valid = pixel_target(iota((1, NB * 128), 1), False)
    target = jnp.where(valid, c * HW + col, -1)
    return hot(iota((CIN * HW, NB * 128), 0) == target)


def unwindow_columns():
    col, c, valid = pixel_target(iota((NB * 128, 1), 0), True)
    target = jnp.where(valid, c * HW + col, -1)
    return hot(iota((NB * 128, CIN * HW), 1) == target)


def window_mask_columns():
    col, _, valid = pixel_target(iota((1, NB * 128), 1), False)
    return hot(iota((HW, NB * 128), 0) == jnp.where(valid, col, -1))


def code_mask_lanes():
    lane = iota((1, 256), 1)
    u_local = lane >> 4
    inner = (u_local >= 1) & (u_local <= UW - 2)
    return hot(iota((128, 256), 0) == jnp.where(inner, u_local * 8, -1))


def own_rows(z, odd):
    j = (iota((z.rows, 1), 0) >> z.shift) - odd * (HALO // 2)
    return (j >= 0) & (j < z.band // 2)


def places(z, odd):
    own = pl.multiple_of(odd * (z.halo // 2), 16)
    halo = pl.multiple_of((1 - odd) * (z.own // 2), 16)
    return own, halo


def mend_coarse(blocks):
    last = HW // 2 - (NB - 1) * (UW - 2)
    rows = blocks[0].shape[0]
    lane = iota((rows, 128), 1)
    halves = [(x[:, :128], x[:, 128:]) for x in blocks]
    done = []
    for b, (low, high) in enumerate(halves):
        before = pltpu.roll(halves[b - 1][1], 32, 1) if b else 0.0
        new_low = jnp.where(lane < 16, before, low)
        if b + 1 < NB:
            after = pltpu.roll(halves[b + 1][0], 96, 1)
            new_high = jnp.where(lane >= 112, after, high)
        else:
            new_high = jnp.where(lane < (last + 1) * 16 - 128, high, 0.0)
        done.append((new_low, new_high))
    return done


def mend_fine(halves):
    rows = halves[0][0].shape[0]
    lane = iota((rows, 128), 1)
    done = []
    for b in range(NB):
        pair = []
        for h in range(2):
            x = halves[b][h]
            before = pltpu.roll(halves[b - 1][h], 16, 1) if b else 0.0
            after = pltpu.roll(halves[b + 1][h], 112, 1) if b + 1 < NB else 0.0
            x = jnp.where(lane < 8, before, x)
            pair.append(jnp.where(lane >= 120, after, x))
        done.append(tuple(pair))
    return done


def pad_frame(z, sh):
    zeros = jnp.zeros((NB, 8, 256), F32)
    sh[:, 0:8, :] = zeros
    sh[:, 8 + z.rows : 16 + z.rows, :] = zeros


def put_frame(z, sh, halves):
    pad_frame(z, sh)
    for b, (low, high) in enumerate(halves):
        sh[b, 8 : 8 + z.rows, 0:128] = low
        sh[b, 8 : 8 + z.rows, 128:256] = high


def put_pixels(z, sh, odd, own, halo):
    pad_frame(z, sh)
    for start, part in zip(places(z, odd), (own, halo)):
        half = part.shape[0] // 2
        rows = pl.ds(pl.multiple_of(8 + start, 8), half)
        for b in range(NB):
            for h in range(2):
                sh[b, rows, h * 128 : h * 128 + 128] = part[
                    h * half : h * half + half, b * 128 : b * 128 + 128
                ]


def fine_taps(z, sh, b):
    up = sh[b, 8 - z.mb : 8 - z.mb + z.rows, :]
    here = sh[b, 8 : 8 + z.rows, :]
    down = sh[b, 8 + z.mb : 8 + z.mb + z.rows, 0:128]
    return jnp.concatenate([up, here, down], axis=1).astype(BF16)


def coarse_taps(z, sh, b):
    down = sh[b, 8 + z.mb : 8 + z.mb + z.rows, :]
    here = sh[b, 8 : 8 + z.rows, :]
    up = sh[b, 8 - z.mb : 8 - z.mb + z.rows, :]
    return [x.astype(BF16) for x in (down, here, up)]


def spread(z, sh, weights):
    taps = [coarse_taps(z, sh, b) for b in range(NB)]
    down, here, up = (jnp.concatenate([t[i] for t in taps], axis=0) for i in range(3))
    nt = ((1,), (1,))
    out = dot(down, weights[0:256], nt) + dot(here, weights[256:512], nt)
    extra = dot(up, weights[512:640], nt)
    return out[:, :128] + extra, out[:, 128:]


def pick_taps(grads):
    lane = iota((CCODE, 128), 1)
    place = lane >> 3
    pieces = []
    for k in range(KS):
        for shift in (-1, 0, 1):
            total = jnp.zeros((CCODE, 128), F32)
            for u in range(1, UW - 1):
                part = grads[u * 16 : u * 16 + 16, k * 128 : k * 128 + 128]
                total = jnp.where(place == u + shift, part, total)
            pieces.append(total)
    pieces.append(jnp.zeros((CCODE, 128), F32))
    block = lane >> 5
    fours = []
    for first in range(4):
        group = pieces[first::4]
        parts = []
        for j in range(4):
            x = group[j]
            for t in range(1, 4):
                x = jnp.where(block == t, group[(t + j) & 3], x)
            parts.append(x)
        fours.append(
            (parts[0] + pltpu.roll(parts[1], 32, 1))
            + (pltpu.roll(parts[2], 64, 1) + pltpu.roll(parts[3], 96, 1))
        )
    inner = place & 3
    total = None
    for j in range(4):
        x = fours[j]
        for t in range(1, 4):
            x = jnp.where(inner == t, fours[(t + j) & 3], x)
        if j:
            x = jnp.where(inner >= j, pltpu.roll(x, 8 * j, 1), pltpu.roll(x, 96 + 8 * j, 1))
        total = x if total is None else total + x
    return total


def own_frame(z, odd, sh):
    start, _ = places(z, odd)
    half = z.own // 2
    rows = pl.ds(pl.multiple_of(8 + start, 8), half)
    flat = jnp.concatenate(
        [
            jnp.concatenate(
                [sh[b, rows, h * 128 : h * 128 + 128] for b in range(NB)], axis=1
            )
            for h in range(2)
        ],
        axis=0,
    )
    return flat.astype(BF16)


def kernel_rows(flat):
    taps = CIN * KS * KS
    pad = jnp.zeros((1, 256 - NK % 128), F32)
    flat = jnp.concatenate([flat, pad], axis=1)
    lane = iota((1, 128), 1)
    row = iota((CCODE, 128), 0)
    rows = jnp.zeros((CCODE, 128), F32)
    for o in range(CCODE):
        chunk, shift = divmod(o * taps, 128)
        x = flat[:, chunk * 128 : chunk * 128 + 128]
        if shift:
            after = flat[:, chunk * 128 + 128 : chunk * 128 + 256]
            x = jnp.where(
                lane < 128 - shift,
                pltpu.roll(x, 128 - shift, 1),
                pltpu.roll(after, 128 - shift, 1),
            )
        rows = jnp.where(row == o, jnp.broadcast_to(x, (CCODE, 128)), rows)
    return rows


def spread_taps(kernel_pair):
    taps = CIN * KS * KS
    rows = jnp.concatenate([kernel_rows(x) for x in kernel_pair for _ in range(8)], axis=0)
    lane = iota((1, 128), 1)
    target, _ = tap_target(jnp.minimum(lane, taps - 1))
    slots = hot(iota((128, 128), 0) == jnp.where(lane < taps, target, -1))
    wide = dot(slots, rows.T.astype(BF16)).astype(BF16)
    halves = [wide[:, 0:128], wide[:, 128:256]]
    return jnp.concatenate([x for x in halves for _ in range(2)], axis=1)


def band_weights(wide_taps):
    wide_taps = wide_taps.astype(F32)
    row_u = iota((128, 256), 0) >> 3
    lane_u = iota((128, 256), 1) >> 4
    masks = [row_u == lane_u + shift for shift in (-1, 0, 1)]
    parts = []
    for k in range(KS):
        total = jnp.zeros((128, 256), F32)
        for i, mask in enumerate(masks):
            q = 3 * k + i
            piece = wide_taps[8 * q : 8 * q + 8]
            piece = jnp.broadcast_to(piece[None], (16, 8, 256)).reshape(128, 256)
            total = jnp.where(mask, piece, total)
        parts.append(total.astype(BF16))
    return jnp.concatenate(parts, axis=0)


def edge_kernel(
    z, fields, mask, cotangent, kernel, out, kernel_out,
    field_buf, mask_buf, cot_buf, kernel_buf, sems,
):
    odd = lax.rem(lax.axis_index("wide"), 2)
    first = lax.axis_index("section") * z.mb
    start = pl.multiple_of((1 - odd) * (z.band - 16), 16)
    copies = [
        pltpu.make_async_copy(
            source.at[pl.ds(first, z.mb), pl.ds(start, 16), :], buf, sems.at[i]
        )
        for i, (source, buf) in enumerate(
            ((fields, field_buf), (mask, mask_buf), (cotangent, cot_buf))
        )
    ]
    copies.append(pltpu.make_async_copy(kernel, kernel_buf, sems.at[3]))
    for copy in copies:
        copy.start()
    for copy in copies:
        copy.wait()
    kernel_row = kernel_buf[...].astype(F32)
    kernel_out[:, 0:NK] = jnp.broadcast_to(kernel_row, (COPIES, NK)).astype(BF16)
    kernel_out[:, NK:] = jnp.zeros((COPIES, PADDED - NK), BF16)

    def beside(buf):
        rows = buf[...].astype(F32)
        return jnp.where(odd == 1, rows[:, :HALO], rows[:, HALO:])

    def ordered(rows, firsts):
        return jnp.concatenate(
            [rows[:, j + h] for h in range(2) for j in firsts], axis=0
        ).astype(BF16)

    mask_rows = beside(mask_buf)
    allowed = jnp.concatenate([mask_rows] * CIN, axis=2)
    every, half = range(0, HALO, 2), range(0, HALO // 2, 2)
    near = beside(cot_buf) * allowed
    near = jnp.where(odd == 1, near[:, : HALO // 2], near[:, HALO // 2 :])
    pieces = ordered(beside(field_buf) * allowed, every), ordered(near, half)
    start = 0
    for piece in pieces:
        count = piece.shape[0]
        for c in range(CIN):
            out[start : start + count, :] = piece[:, c * HW : c * HW + HW]
            start += count
    out[start : z.sent, :] = ordered(mask_rows, every)[0 : z.near]


def prepare_kernel(
    z, fields, mask, counts, enc_bias, dec_bias, run_mean, run_cov,
    pixels_out, inmask_out, aux_out,
    count_buf, enc_buf, dec_buf, mean_buf, cov_buf, sems,
):
    section = lax.axis_index("section")
    wide = lax.axis_index("wide")
    first = section * z.mb
    mine_rows = pl.ds(first, z.mb)
    copies = [
        pltpu.make_async_copy(source, buf, sems.at[i])
        for i, (source, buf) in enumerate(
            (
                (counts, count_buf),
                (enc_bias, enc_buf),
                (dec_bias, dec_buf),
                (run_mean, mean_buf),
                (run_cov, cov_buf),
            )
        )
    ]
    for copy in copies:
        copy.start()
    gather = gather_rows(z)
    columns = window_columns()
    mask_columns = window_mask_columns()
    pixel_mask = mask[mine_rows].astype(F32).astype(BF16).reshape(z.own, HW)
    pixels = fields[mine_rows].reshape(z.own, z.span)
    framed = dot(gather, jnp.concatenate([pixel_mask, pixels], axis=1)).astype(BF16)
    in_mask = dot(framed[:, 0:HW], mask_columns)
    windowed = dot(framed[:, HW:], columns)
    for copy in copies:
        copy.wait()
    lane = iota((8, 128), 1)
    dec_row = jnp.zeros((8, 128), F32)
    for c in range(CIN):
        dec_row = jnp.where(((lane >> 1) & 3) == c, dec_buf[c], dec_row)
    enc_row = jnp.zeros((8, 128), F32)
    mean_row = jnp.zeros((8, 128), F32)
    for o in range(CCODE):
        enc_row = jnp.where((lane & 15) == o, enc_buf[o], enc_row)
        mean_row = jnp.where((lane & 15) == o, mean_buf[o], mean_row)
    aux_out[0:8] = dec_row
    aux_out[8:16] = enc_row
    aux_out[16:24] = mean_row
    aux_out[24:40] = jnp.zeros((16, 128), F32)
    aux_out[24:40, 0:CCODE] = cov_buf[...]
    field_now = wide * z.band // HW
    micro = iota((16, 128), 0) & (z.mb - 1)
    count = jnp.zeros((16, 128), jnp.int32)
    for m in range(z.mb):
        count = jnp.where(micro == m, count_buf[first + m, field_now], count)
    channel_ok = jnp.where(((iota((16, 128), 1) >> 1) & 3) < count, 1.0, 0.0)
    aux_out[40:56] = channel_ok
    in_mask = in_mask * jnp.tile(channel_ok, (z.own // 16, NB))
    inmask_out[...] = in_mask.astype(BF16)
    pixels_out[...] = (windowed * in_mask).astype(BF16)


def taps_kernel(z, kernel_own, kernel_other, weights_out):
    mine, other = (x[:, 0:NK].astype(F32)[0:1] for x in (kernel_own, kernel_other))
    leads = lax.axis_index("section") == 0
    weights_out[...] = spread_taps((jnp.where(leads, mine, other), jnp.where(leads, other, mine)))


def local_taps(sh, b, rows, step):
    up = sh[b, 16 - step : 16 - step + rows, :]
    here = sh[b, 16 : 16 + rows, :]
    down = sh[b, 16 + step : 16 + step + rows, 0:128]
    return jnp.concatenate([up, here, down], axis=1).astype(BF16)


def encode_rows(taps, banded, bias, masks, mine):
    code_mask = dot(masks, code_mask_lanes())
    pre = dot(taps, banded) + bias
    slope = jnp.exp(jnp.minimum(pre, 0.0))
    code = jnp.where(pre > 0, pre, slope - 1.0).astype(BF16).astype(F32)
    slope = jnp.where(code_mask > 0.5, slope, -slope)
    allowed = code_mask if mine is None else jnp.where(mine, code_mask, 0.0)
    weighted = code * allowed
    halves = [
        jnp.concatenate([x[:, 0:128], x[:, 128:256]], axis=0).astype(BF16) for x in (weighted, code)
    ]
    second = dot(*halves, ((0,), (0,)))
    sums = [jnp.sum(x, axis=0, keepdims=True) for x in (weighted, allowed)]
    lane_u = iota((16, 128), 1) >> 4
    total = second[0:16]
    for u in range(1, UW // 2):
        total = jnp.where(lane_u == u, second[u * 16 : u * 16 + 16], total)
    total = fold(total, 16)
    diagonal = (iota((8, 128), 1) >> 4) == iota((8, 128), 0)
    pay = [
        jnp.sum(jnp.where(diagonal, total[h * 8 : h * 8 + 8], 0.0), axis=0, keepdims=True)
        for h in range(2)
    ]
    first, count = (
        fold(jnp.broadcast_to(x[:, :128] + x[:, 128:], (8, 128)), 16) for x in sums
    )
    lane = iota((8, 128), 1)
    inner, group = lane & 15, lane >> 4
    first = lanes_from(first, jnp.where(inner == 0, group, group + 8))
    spare = jnp.where(inner == 2, count, first)[0:1]
    pay[1] = jnp.where(inner[0:1] < 8, spare, pay[1])
    return code, slope, jnp.concatenate(pay, axis=0)


def inner_kernel(
    z, pixels, own_mask, weights, aux, taps_out, code_out, slope_out, pay_out, band_out, sh
):
    odd = lax.rem(lax.axis_index("wide"), 2)
    half = z.own // 2
    count = half - 16
    zeros = jnp.zeros((NB, 16, 256), F32)
    sh[:, 0:16, :] = zeros
    sh[:, half : half + 16, :] = zeros
    here = pl.ds(pl.multiple_of((1 - odd) * 16, 16), half)
    for b in range(NB):
        for h in range(2):
            sh[b, here, h * 128 : h * 128 + 128] = pixels[
                h * half : h * half + half, b * 128 : b * 128 + 128
            ].astype(F32)
    start = pl.multiple_of(odd * 32, 16)
    taps = [local_taps(sh, b, count, z.mb) for b in range(NB)]
    for b in range(NB):
        taps_out[b, pl.ds(start, count), :] = taps[b]
    kept = pl.ds(pl.multiple_of(odd * 16, 16), count)
    masks = jnp.concatenate([own_mask[kept, b * 128 : b * 128 + 128] for b in range(NB)], axis=0)
    bias = jnp.concatenate([aux[8:9], aux[8:9]], axis=1)
    banded = band_weights(weights[:, 0:256])
    band_out[...] = banded
    code, slope, pay = encode_rows(jnp.concatenate(taps, axis=0), banded, bias, masks, None)
    pay_out[...] = pay
    for b in range(NB):
        rs = slice(b * count, b * count + count)
        code_out[b, pl.ds(start, count), :] = code[rs].astype(BF16)
        slope_out[b, pl.ds(start, count), :] = slope[rs]


def encode_kernel(
    z, pixels, own_mask, halo, banded, aux, inner_pay, taps_in, code_in, slope_in,
    taps_out, code_out, slope_out, pay_out,
    sh,
):
    odd = lax.rem(lax.axis_index("wide"), 2)
    half = z.own // 2
    count = 32
    channel_ok = jnp.tile(aux[40:56], (1, NB))
    middle, end = CIN * z.halo, CIN * (z.halo + z.near)
    halo_mask = dot(halo[end : z.sent, :], window_mask_columns())
    halo_rows = [halo[i : i + z.halo, :] for i in range(0, middle, z.halo)]
    halo_pixels = dot(jnp.concatenate(halo_rows, axis=1), window_columns())
    halo_x = halo_pixels * jnp.tile(channel_ok, (2, 1))
    zeros = jnp.zeros((NB, 16, 256), F32)
    sh[:, 0:16, :] = zeros
    sh[:, 48:64, :] = zeros
    own_start = pl.multiple_of((1 - odd) * (half - 32), 16)
    own_there = pl.ds(pl.multiple_of(odd * 32, 16), 32)
    halo_there = pl.ds(pl.multiple_of((2 - odd) * 16, 16), 16)
    for b in range(NB):
        for h in range(2):
            cs = slice(b * 128, b * 128 + 128)
            own = pixels[pl.ds(pl.multiple_of(own_start + h * half, 16), 32), cs]
            sh[b, own_there, h * 128 : h * 128 + 128] = own.astype(F32)
            sh[b, halo_there, h * 128 : h * 128 + 128] = halo_x[h * 16 : h * 16 + 16, cs]
    start = pl.multiple_of((1 - odd) * (z.rows - count), 16)
    taps = [local_taps(sh, b, count, z.mb) for b in range(NB)]
    for b in range(NB):
        taps_out[b, pl.ds(start, count), :] = taps[b]
    edge_mask = own_mask[pl.ds(pl.multiple_of((1 - odd) * (half - 16), 16), 16), :].astype(F32)
    first = jnp.where(odd == 1, halo_mask, edge_mask)
    later = jnp.where(odd == 1, edge_mask, halo_mask)
    masks = jnp.concatenate(
        [x[:, b * 128 : b * 128 + 128] for b in range(NB) for x in (first, later)], axis=0
    ).astype(BF16)
    bias = jnp.concatenate([aux[8:9], aux[8:9]], axis=1)
    mine = ((iota((NB * count, 1), 0) >> 4) & 1) == odd
    code, slope, pay = encode_rows(jnp.concatenate(taps, axis=0), banded[...], bias, masks, mine)
    pay = pay + inner_pay[...]
    pay_out[...] = pay
    for b in range(NB):
        rs = slice(b * count, b * count + count)
        code_out[b, pl.ds(start, count), :] = code[rs].astype(BF16)
        slope_out[b, pl.ds(start, count), :] = slope[rs]


def decode_kernel(
    z, cotangent, code, in_mask, halo, weights, aux,
    sent_out, pay_out,
    sh, cot_frame,
):
    odd = lax.rem(lax.axis_index("wide"), 2)
    mine = pl.ds(lax.axis_index("section") * z.mb, z.mb)
    rows = z.rows
    put_frame(z, sh, mend_coarse([code[b].astype(F32) for b in range(NB)]))
    banded = band_weights(weights[:, 256:512])
    raws = spread(z, sh, banded)
    gather = gather_rows(z)
    columns = window_columns()
    own_cot = dot(gather, cotangent[mine].reshape(z.own, z.span)).astype(BF16)
    near = [
        halo[i : i + z.near, :] for i in range(CIN * z.halo, CIN * (z.halo + z.near), z.near)
    ]
    cots = dot(jnp.concatenate([own_cot, jnp.concatenate(near, axis=1)], axis=0), columns)
    near = cots[z.own : z.own + z.near] * jnp.tile(aux[40:56], (1, NB))
    nothing = jnp.zeros((8, NB * 128), F32)
    beside = []
    for h in range(2):
        part = near[h * 8 : h * 8 + 8]
        beside += [jnp.where(odd == 1, nothing, part), jnp.where(odd == 1, part, nothing)]
    own_cot = cots[0 : z.own] * in_mask[...].astype(F32)
    put_pixels(z, cot_frame, odd, own_cot, jnp.concatenate(beside, axis=0))
    mine_rows = own_rows(z, odd)
    u_local = (iota((1, 128), 1) >> 3) & (UW - 1)
    inner = mine_rows & (u_local >= 1) & (u_local <= UW - 2)
    grads = []
    bias_sum = jnp.zeros((1, 128), F32)
    for h in range(2):
        raw = raws[h] + aux[0:1]
        slope = jnp.exp(jnp.minimum(raw, 0.0))
        cs = slice(h * 128, h * 128 + 128)
        for b in range(NB):
            rs = slice(b * rows, b * rows + rows)
            grad = (cot_frame[b, 8 : 8 + rows, cs] * slope[rs]).astype(BF16).astype(F32)
            bias_sum = bias_sum + jnp.sum(jnp.where(inner, grad, 0.0), axis=0, keepdims=True)
            grads.append(grad)
    put_frame(z, sh, mend_fine([(grads[b], grads[NB + b]) for b in range(NB)]))
    taps = jnp.concatenate([fine_taps(z, sh, b) for b in range(NB)], axis=0)
    sent_out[...] = dot(taps, banded).astype(BF16).reshape(NB, rows, 256)
    last = HW // 2 - (NB - 1) * (UW - 2)
    within = mine_rows & ((iota((1, 256), 1) >> 4) <= last)
    mine = jnp.concatenate(
        [
            jnp.where(within if b == NB - 1 else mine_rows, code[b].astype(F32), 0.0).astype(BF16)
            for b in range(NB)
        ],
        axis=0,
    )
    pay = pick_taps(dot(mine, taps, ((0,), (0,))))
    bias_sum = fold(jnp.broadcast_to(bias_sum, (16, 128)), 8)
    lane = iota((16, 128), 1)
    keep = (lane < 8) & ((lane >> 1) == iota((16, 128), 0))
    column = jnp.sum(jnp.where(keep, bias_sum, 0.0), axis=1, keepdims=True)
    pay_out[...] = jnp.where(lane >= 120, column, pay)


def whiten_kernel(
    z, stats, code, slope, sent, taps, decode_pay, aux,
    grad_out, pay_out, moments_out,
):
    odd = lax.rem(lax.axis_index("wide"), 2)
    rows = z.rows
    pay = jnp.sum(stats[...], axis=0)
    lane = iota((8, 128), 1)
    inner, step = lane & 15, iota((8, 128), 0)
    low, high = (jnp.broadcast_to(pay[h : h + 1], (8, 128)) for h in range(2))
    count = lanes_from(high, jnp.full((8, 128), 2, jnp.int32))[0:1]
    first = lanes_from(high, jnp.where(inner < 8, 16 * inner, 16 * (inner - 8) + 1))[0:1]
    mean = first / count
    columns = jnp.concatenate([lanes_from(high, 16 * step + h) for h in range(2)], axis=0)
    diagonal = (lane >> 4) == step
    mirrored = lanes_from(low, jnp.where(inner < 8, 16 * inner + 8 + step, 0))
    low, high = (fold(jnp.where(diagonal, x, 0.0), 16) for x in (low, high))
    second = jnp.concatenate([low, jnp.where(inner < 8, mirrored, high)], axis=0)
    lane = iota((16, 128), 1)
    row = iota((16, 128), 0)
    wide_mean = jnp.broadcast_to(mean, (16, 128))
    total = jnp.broadcast_to(count, (16, 128))
    mean_column = columns / total
    cov = second / total - mean_column * wide_mean
    moments_out[0:CCODE] = cov
    moments_out[CCODE:] = jnp.broadcast_to(mean, (8, 128))
    offset = cov - jnp.where((lane & 15) == row, 1.0, 0.0)
    pulled = jnp.sum(offset * mean_column, axis=0, keepdims=True)
    linear = whiten_weight * mean - 2.0 * whiten_weight * pulled
    linear = jnp.concatenate([linear, linear], axis=1)
    matrix = jnp.tile(2.0 * whiten_weight * offset, (8, 1))
    matrix = jnp.where((iota((128, 128), 0) >> 4) == (iota((128, 128), 1) >> 4), matrix, 0.0)
    high = matrix.astype(BF16)
    matrix = jnp.concatenate([high, (matrix - high.astype(F32)).astype(BF16)], axis=0)
    flat = code[...].reshape(z.frame, 256)
    flat = jnp.concatenate(
        [jnp.concatenate([x, x], axis=1) for x in (flat[:, 0:128], flat[:, 128:256])], axis=0
    )
    turned = dot(flat, matrix)
    turned = jnp.concatenate([turned[0 : z.frame], turned[z.frame :]], axis=1) + linear
    mine_rows = own_rows(z, odd)
    lane_u = iota((1, 256), 1) >> 4
    inner = mine_rows & (lane_u >= 1) & (lane_u <= UW - 2)
    last = HW // 2 - (NB - 1) * (UW - 2)
    blocks, mine = [], []
    bias_sum = jnp.zeros((1, 256), F32)
    for b in range(NB):
        signed = slope[b]
        pull = jnp.where(signed > 0, turned[b * rows : b * rows + rows], 0.0)
        grad = ((sent[b].astype(F32) + pull) * jnp.abs(signed)).astype(BF16).astype(F32)
        kept = jnp.where(inner & (lane_u <= last) if b == NB - 1 else inner, grad, 0.0)
        bias_sum = bias_sum + jnp.sum(kept, axis=0, keepdims=True)
        blocks.append(grad)
        mine.append(kept.astype(BF16))
    products = dot(
        jnp.concatenate(mine, axis=0), taps[...].reshape(z.frame, KS * 128), ((0,), (0,))
    )
    encode_pay = pick_taps(products)
    bias_sum = fold(jnp.broadcast_to(bias_sum[:, :128] + bias_sum[:, 128:], (16, 128)), 16)
    column = jnp.sum(jnp.where(lane == row, bias_sum, 0.0), axis=1, keepdims=True)
    decoded = decode_pay[...]
    biases = jnp.where((lane & 1) == 0, column, decoded)
    coarse = biases.astype(BF16).astype(F32)
    biases = jnp.where((lane & 2) == 0, coarse, biases - coarse)
    encode_pay = jnp.where(lane >= 120, biases, encode_pay)
    decoded = jnp.where(lane >= 120, biases, decoded)
    pay_out[0] = encode_pay.astype(BF16)
    pay_out[1] = decoded.astype(BF16)
    for b, (low, high) in enumerate(mend_coarse(blocks)):
        grad_out[b, :, 0:128] = low.astype(BF16)
        grad_out[b, :, 128:256] = high.astype(BF16)


def picture(z, decodes, grad, code, in_mask, weights, aux, sh):
    odd = lax.rem(lax.axis_index("wide"), 2)
    rows = z.rows
    frames = [
        jnp.where(decodes, code[b].astype(F32), grad[b].astype(F32)) for b in range(NB)
    ]
    put_frame(z, sh, mend_coarse(frames))
    chosen = jnp.where(decodes, weights[:, 256:512].astype(F32), weights[:, 0:256].astype(F32))
    raws = spread(z, sh, band_weights(chosen))
    for h in range(2):
        raw = raws[h] + aux[0:1]
        raw = jnp.where(raw > 0, raw, jnp.exp(jnp.minimum(raw, 0.0)) - 1.0)
        raw = jnp.where(decodes, raw, raws[h])
        for b in range(NB):
            sh[b, 8 : 8 + rows, h * 128 : h * 128 + 128] = raw[b * rows : b * rows + rows]
    flat = own_frame(z, odd, sh) * in_mask[...]
    native = dot(flat, unwindow_columns()).astype(BF16)
    return dot(scatter_rows(z), native).astype(BF16).reshape(z.mb, z.band, z.span)


def send_kernel(z, grad, code, in_mask, weights, aux, send_out, sh):
    decodes = lax.axis_index("section") == 0
    send_out[...] = picture(z, decodes, grad, code, in_mask, weights, aux, sh)


def keep_kernel(
    z, grad, code, in_mask, weights, aux, moments,
    pixels_out, mean_out, cov_out,
    sh, mine, means, covs, sems,
):
    section = lax.axis_index("section")
    means[...] = decay_rate * aux[16:17, 0:CCODE] + (1.0 - decay_rate) * moments[16:17, 0:CCODE]
    covs[...] = decay_rate * aux[24:40, 0:CCODE] + (1.0 - decay_rate) * moments[0:16, 0:CCODE]
    mine[...] = picture(z, section == 1, grad, code, in_mask, weights, aux, sh)
    copies = [
        pltpu.make_async_copy(source, target, sems.at[i])
        for i, (source, target) in enumerate(
            (
                (mine, pixels_out.at[0, pl.ds(section * z.mb, z.mb)]),
                (means, mean_out),
                (covs, cov_out),
            )
        )
    ]
    for copy in copies:
        copy.start()
    for copy in copies:
        copy.wait()


def total_kernel(z, parts, out):
    out[...] = jnp.sum(parts[...].astype(F32), axis=0)


def finish_kernel(
    z, sums, arrived, half_done, pixels_out, kernel_out, enc_out, dec_out,
    kernels, encs, decs, sems,
):
    there = z.micro - z.mb - lax.axis_index("section") * z.mb
    copies = [
        pltpu.make_async_copy(source, target, sems.at[i])
        for i, (source, target) in enumerate(
            (
                (arrived, pixels_out.at[0, pl.ds(there, z.mb)]),
                (encs, enc_out),
                (decs, dec_out),
                (kernels, kernel_out),
            )
        )
    ]
    copies[0].start()
    total = sums[...]
    taps = CIN * KS * KS
    tap = (iota((CCODE, 128), 1) - taps * iota((CCODE, 128), 0)) & 127
    slot, _ = tap_target(jnp.minimum(tap, taps - 1))
    moved = lanes_from(total, slot)
    place = iota((1, 128), 1)
    for chunk in range((NK + 127) // 128):
        out = jnp.zeros((1, 128), F32)
        for o in range(CCODE):
            start = o * taps - chunk * 128
            if -taps < start < 128:
                out = jnp.where((place >= start) & (place < start + taps), moved[o : o + 1], out)
        width = min(128, NK - chunk * 128)
        kernels[:, chunk * 128 : chunk * 128 + width] = out[:, 0:width]
    copies[3].start()
    lane = iota((16, 128), 1)
    row = iota((16, 128), 0)
    for slot, out in ((120, encs), (121, decs)):
        chosen = (lane == slot) | (lane == slot + 2)
        column = jnp.sum(jnp.where(chosen, total, 0.0), axis=1, keepdims=True)
        flat = jnp.sum(jnp.where(lane == row, column, 0.0), axis=0, keepdims=True)
        out[...] = flat[:, 0 : out.shape[1]]
    copies[1].start()
    copies[2].start()
    for copy in copies:
        copy.wait()


VMEM = pl.BlockSpec(memory_space=pltpu.VMEM)
HBM = pl.BlockSpec(memory_space=pltpu.HBM)
PARAMS = pltpu.CompilerParams(vmem_limit_bytes=24 * 1024 * 1024)
DMA = pltpu.SemaphoreType.DMA


def shape(*dims, dtype=BF16):
    return jax.ShapeDtypeStruct(dims, dtype)


def shards(sections, wides):
    def run(
        fields, pixel_mask, channel_counts, kernels, enc_bias, dec_bias, cotangent, run_mean, run_cov
    ):
        z = Sizes(fields.shape, sections)
        assert 2 * z.band == HW and z.span == CIN * HW and z.mb == 4
        whole = (fields, pixel_mask, cotangent)
        (
            fields, cotangent, pixel_mask, kernels, channel_counts, enc_bias, dec_bias,
            run_mean, run_cov,
        ) = (
            pltpu.with_memory_space_constraint(x, pltpu.HBM)
            for x in (
                fields, cotangent, pixel_mask, kernels, channel_counts, enc_bias, dec_bias,
                run_mean, run_cov,
            )
        )
        swap = [(i, i ^ 1) for i in range(sections)]
        pair = [(i, i ^ 1) for i in range(wides)]
        frame = (NB, z.rows, 256)
        framed = pltpu.VMEM((NB, z.rows + 16, 256), F32)
        band_buf = pltpu.VMEM((z.mb, z.band, z.span), BF16)
        edge_buf = pltpu.VMEM((z.mb, 16, z.span), BF16)
        heavy = pl.CostEstimate(flops=4_000_000_000, bytes_accessed=4_000_000, transcendentals=0)

        def call(kernel, name, outs, ins, scratch, out_specs=None, cost=None, alias=None):
            return pl.pallas_call(
                lambda *refs: kernel(z, *refs),
                out_shape=outs,
                in_specs=ins,
                out_specs=out_specs or [VMEM] * len(outs),
                scratch_shapes=scratch,
                compiler_params=PARAMS,
                cost_estimate=cost,
                input_output_aliases=alias or {},
                name=name,
            )

        halo, kernel_own = call(
            edge_kernel,
            "edge",
            [shape(z.sent, HW), shape(COPIES, PADDED)],
            [HBM] * 4,
            [
                edge_buf,
                pltpu.VMEM((z.mb, 16, HW), jnp.int32),
                edge_buf,
                pltpu.VMEM((1, NK), BF16),
                DMA((4,)),
            ],
        )(fields, pixel_mask, cotangent, kernels)
        halo = lax.ppermute(halo, "wide", pair)
        kernel_other = lax.ppermute(kernel_own, "section", swap)
        pixels, in_mask, aux = call(
            prepare_kernel,
            "prepare",
            [
                shape(z.own, NB * 128),
                shape(z.own, NB * 128),
                shape(56, 128, dtype=F32),
            ],
            [VMEM] * 2 + [HBM] * 5,
            [
                pltpu.SMEM(channel_counts.shape, jnp.int32),
                pltpu.SMEM(enc_bias.shape, F32),
                pltpu.SMEM(dec_bias.shape, F32),
                pltpu.SMEM(run_mean.shape, F32),
                pltpu.VMEM(run_cov.shape, F32),
                DMA((5,)),
            ],
            cost=heavy,
        )(*whole[:2], channel_counts, enc_bias, dec_bias, run_mean, run_cov)
        (weights,) = call(taps_kernel, "taps", [shape(128, 512)], [VMEM] * 2, [])(
            kernel_own, kernel_other
        )
        coded = [shape(NB, z.rows, KS * 128), shape(*frame), shape(*frame, dtype=F32)]
        taps, code, slope, pay, banded = call(
            inner_kernel,
            "inner",
            coded + [shape(2, 128, dtype=F32), shape(KS * 128, 256)],
            [VMEM] * 4,
            [pltpu.VMEM((NB, z.own // 2 + 16, 256), F32)],
            cost=heavy,
        )(pixels, in_mask, weights, aux)
        taps, code, slope, pay = call(
            encode_kernel,
            "encode",
            coded + [shape(2, 128, dtype=F32)],
            [VMEM] * 9,
            [pltpu.VMEM((NB, 64, 256), F32)],
            alias={6: 0, 7: 1, 8: 2},
        )(pixels, in_mask, halo, banded, aux, pay, taps, code, slope)
        pay = jnp.broadcast_to(pay[None], (sections * wides, 2, 128))
        stats = lax.all_to_all(pay, ("section", "wide"), 0, 0)
        sent, decode_pay = call(
            decode_kernel,
            "decode",
            [shape(*frame), shape(CCODE, 128, dtype=F32)],
            [VMEM] * 6,
            [framed, framed],
            cost=heavy,
        )(whole[2], code, in_mask, halo, weights, aux)
        grad, pay, moments = call(
            whiten_kernel,
            "whiten",
            [
                shape(*frame),
                shape(sections, CCODE, 128),
                shape(CCODE + 8, 128, dtype=F32),
            ],
            [VMEM] * 7,
            [],
            alias={3: 0},
        )(stats, code, slope, sent, taps, decode_pay, aux)
        pay = jnp.broadcast_to(pay[:, None], (sections, wides, CCODE, 128))
        pay = pay.reshape(sections * wides, CCODE, 128)
        parts = lax.all_to_all(pay, ("section", "wide"), 0, 0)
        (sending,) = call(
            send_kernel,
            "send",
            [shape(z.mb, z.band, z.span)],
            [VMEM] * 5,
            [framed],
            cost=heavy,
        )(grad, code, in_mask, weights, aux)
        arrived = lax.ppermute(sending, "section", swap)
        half_done, new_mean, new_cov = call(
            keep_kernel,
            "keep",
            [
                shape(1, z.micro, z.band, z.span),
                shape(1, CCODE, dtype=F32),
                shape(CCODE, CCODE, dtype=F32),
            ],
            [VMEM] * 6,
            [
                framed,
                band_buf,
                pltpu.VMEM((1, CCODE), F32),
                pltpu.VMEM((CCODE, CCODE), F32),
                DMA((3,)),
            ],
            out_specs=[HBM] * 3,
            cost=heavy,
        )(grad, code, in_mask, weights, aux, moments)
        (sums,) = call(
            total_kernel,
            "total",
            [shape(CCODE, 128, dtype=F32)],
            [VMEM],
            [],
            cost=pl.CostEstimate(flops=100_000_000_000, bytes_accessed=0, transcendentals=0),
        )(parts)
        pixels_out, kernel_grads, enc_grad, dec_grad = call(
            finish_kernel,
            "finish",
            [
                shape(1, z.micro, z.band, z.span),
                shape(1, NK, dtype=F32),
                shape(1, CCODE, dtype=F32),
                shape(1, CIN, dtype=F32),
            ],
            [VMEM] * 2 + [HBM],
            [
                pltpu.VMEM((1, NK), F32),
                pltpu.VMEM((1, CCODE), F32),
                pltpu.VMEM((1, CIN), F32),
                DMA((4,)),
            ],
            out_specs=[HBM] * 4,
            alias={2: 0},
        )(sums, arrived, half_done)
        return (
            pixels_out,
            kernel_grads,
            enc_grad.reshape(CCODE),
            dec_grad.reshape(CIN),
            new_mean.reshape(CCODE),
            new_cov,
        )

    return run


def solution(mesh):
    in_specs = (
        P(None, "wide", None),
        P(None, "wide", None),
        P(),
        P("section", None),
        P(),
        P(),
        P(None, "wide", None),
        P(),
        P(),
    )
    out_specs = (P("section", None, "wide", None), P("section", None), P(), P(), P(), P())
    run = shards(mesh.shape["section"], mesh.shape["wide"])
    return jax.shard_map(run, mesh=mesh, in_specs=in_specs, out_specs=out_specs, check_vma=False)
```

```python
import jax
import jax.numpy as jnp
from jax import lax
from jax.experimental import pallas as pl
from jax.experimental.pallas import tpu as pltpu
from jax.sharding import PartitionSpec as P

CIN = 4
CCODE = 16
KS = 5
HW = 128

UW = 16
NB = 5
HALO = 8
NK = CCODE * CIN * KS * KS
COPIES = 16
PADDED = NK + 192

decay_rate = 0.9
whiten_weight = 0.25

F32 = jnp.float32
BF16 = jnp.bfloat16


def iota(shape, dim):
    return lax.broadcasted_iota(jnp.int32, shape, dim)


def hot(mask):
    return jnp.where(mask, 1.0, 0.0).astype(BF16)


def dot(a, b, dims=((1,), (0,))):
    return lax.dot_general(a, b, (dims, ((), ())), preferred_element_type=F32)


def fold(x, unit):
    rolled = [x] + [pltpu.roll(x, step, 1) for step in range(unit, 128, unit)]
    while len(rolled) > 1:
        rolled = [sum(rolled[i : i + 2]) for i in range(0, len(rolled), 2)]
    return rolled[0]


def lanes_from(x, source):
    return jnp.take_along_axis(x, source, axis=1, mode="promise_in_bounds")


class Sizes:
    def __init__(self, fields, sections):
        self.micro, self.band, self.span = fields
        self.sections = sections
        self.mb = self.micro // sections
        self.jf = self.band // 2 + HALO // 2
        self.rows = self.jf * self.mb
        self.own = self.mb * self.band
        self.halo = self.mb * HALO
        self.shift = self.mb.bit_length() - 1
        self.frame = NB * self.rows
        self.near = self.halo // 2
        self.sent = CIN * (self.halo + self.near) + self.near


def tap_target(n):
    o = (n * 5243) >> 19
    t = n - 100 * o
    c = (t * 1311) >> 15
    t = t - 25 * c
    k = (t * 205) >> 10
    l = t - 5 * k
    return (3 * k + (l >> 1)) * 8 + 2 * c + (l & 1), o


def row_target(z, row):
    half = z.own // 2
    parity = (row >= half).astype(jnp.int32)
    q = row - parity * half
    return (q & (z.mb - 1)) * z.band + 2 * (q >> z.shift) + parity


def gather_rows(z):
    return hot(iota((z.own, z.own), 1) == row_target(z, iota((z.own, 1), 0)))


def scatter_rows(z):
    return hot(iota((z.own, z.own), 0) == row_target(z, iota((1, z.own), 1)))


def pixel_target(lane, inner):
    u_local = (lane >> 3) & (UW - 1)
    u = (lane >> 7) * (UW - 2) + u_local - 1
    valid = (u >= 0) & (u < HW // 2)
    if inner:
        valid = valid & (u_local >= 1) & (u_local <= UW - 2)
    return 2 * u + (lane & 1), (lane >> 1) & 3, valid


def window_columns():
    col, c, valid = pixel_target(iota((1, NB * 128), 1), False)
    target = jnp.where(valid, c * HW + col, -1)
    return hot(iota((CIN * HW, NB * 128), 0) == target)


def unwindow_columns():
    col, c, valid = pixel_target(iota((NB * 128, 1), 0), True)
    target = jnp.where(valid, c * HW + col, -1)
    return hot(iota((NB * 128, CIN * HW), 1) == target)


def window_mask_columns():
    col, _, valid = pixel_target(iota((1, NB * 128), 1), False)
    return hot(iota((HW, NB * 128), 0) == jnp.where(valid, col, -1))


def code_mask_lanes():
    lane = iota((1, 256), 1)
    u_local = lane >> 4
    inner = (u_local >= 1) & (u_local <= UW - 2)
    return hot(iota((128, 256), 0) == jnp.where(inner, u_local * 8, -1))


def own_rows(z, odd):
    j = (iota((z.rows, 1), 0) >> z.shift) - odd * (HALO // 2)
    return (j >= 0) & (j < z.band // 2)


def places(z, odd):
    own = pl.multiple_of(odd * (z.halo // 2), 16)
    halo = pl.multiple_of((1 - odd) * (z.own // 2), 16)
    return own, halo


def mend_coarse(blocks):
    last = HW // 2 - (NB - 1) * (UW - 2)
    rows = blocks[0].shape[0]
    lane = iota((rows, 128), 1)
    halves = [(x[:, :128], x[:, 128:]) for x in blocks]
    done = []
    for b, (low, high) in enumerate(halves):
        before = pltpu.roll(halves[b - 1][1], 32, 1) if b else 0.0
        new_low = jnp.where(lane < 16, before, low)
        if b + 1 < NB:
            after = pltpu.roll(halves[b + 1][0], 96, 1)
            new_high = jnp.where(lane >= 112, after, high)
        else:
            new_high = jnp.where(lane < (last + 1) * 16 - 128, high, 0.0)
        done.append((new_low, new_high))
    return done


def mend_fine(halves):
    rows = halves[0][0].shape[0]
    lane = iota((rows, 128), 1)
    done = []
    for b in range(NB):
        pair = []
        for h in range(2):
            x = halves[b][h]
            before = pltpu.roll(halves[b - 1][h], 16, 1) if b else 0.0
            after = pltpu.roll(halves[b + 1][h], 112, 1) if b + 1 < NB else 0.0
            x = jnp.where(lane < 8, before, x)
            pair.append(jnp.where(lane >= 120, after, x))
        done.append(tuple(pair))
    return done


def pad_frame(z, sh):
    zeros = jnp.zeros((NB, 8, 256), F32)
    sh[:, 0:8, :] = zeros
    sh[:, 8 + z.rows : 16 + z.rows, :] = zeros


def put_frame(z, sh, halves):
    pad_frame(z, sh)
    for b, (low, high) in enumerate(halves):
        sh[b, 8 : 8 + z.rows, 0:128] = low
        sh[b, 8 : 8 + z.rows, 128:256] = high


def put_pixels(z, sh, odd, own, halo):
    pad_frame(z, sh)
    for start, part in zip(places(z, odd), (own, halo)):
        half = part.shape[0] // 2
        rows = pl.ds(pl.multiple_of(8 + start, 8), half)
        for b in range(NB):
            for h in range(2):
                sh[b, rows, h * 128 : h * 128 + 128] = part[
                    h * half : h * half + half, b * 128 : b * 128 + 128
                ]


def fine_taps(z, sh, b):
    up = sh[b, 8 - z.mb : 8 - z.mb + z.rows, :]
    here = sh[b, 8 : 8 + z.rows, :]
    down = sh[b, 8 + z.mb : 8 + z.mb + z.rows, 0:128]
    return jnp.concatenate([up, here, down], axis=1).astype(BF16)


def coarse_taps(z, sh, b):
    down = sh[b, 8 + z.mb : 8 + z.mb + z.rows, :]
    here = sh[b, 8 : 8 + z.rows, :]
    up = sh[b, 8 - z.mb : 8 - z.mb + z.rows, :]
    return [x.astype(BF16) for x in (down, here, up)]


def spread(z, sh, weights):
    taps = [coarse_taps(z, sh, b) for b in range(NB)]
    down, here, up = (jnp.concatenate([t[i] for t in taps], axis=0) for i in range(3))
    nt = ((1,), (1,))
    out = dot(down, weights[0:256], nt) + dot(here, weights[256:512], nt)
    extra = dot(up, weights[512:640], nt)
    return out[:, :128] + extra, out[:, 128:]


def pick_taps(grads):
    lane = iota((CCODE, 128), 1)
    place = lane >> 3
    pieces = []
    for k in range(KS):
        for shift in (-1, 0, 1):
            total = jnp.zeros((CCODE, 128), F32)
            for u in range(1, UW - 1):
                part = grads[u * 16 : u * 16 + 16, k * 128 : k * 128 + 128]
                total = jnp.where(place == u + shift, part, total)
            pieces.append(total)
    pieces.append(jnp.zeros((CCODE, 128), F32))
    block = lane >> 5
    fours = []
    for first in range(4):
        group = pieces[first::4]
        parts = []
        for j in range(4):
            x = group[j]
            for t in range(1, 4):
                x = jnp.where(block == t, group[(t + j) & 3], x)
            parts.append(x)
        fours.append(
            (parts[0] + pltpu.roll(parts[1], 32, 1))
            + (pltpu.roll(parts[2], 64, 1) + pltpu.roll(parts[3], 96, 1))
        )
    inner = place & 3
    total = None
    for j in range(4):
        x = fours[j]
        for t in range(1, 4):
            x = jnp.where(inner == t, fours[(t + j) & 3], x)
        if j:
            x = jnp.where(inner >= j, pltpu.roll(x, 8 * j, 1), pltpu.roll(x, 96 + 8 * j, 1))
        total = x if total is None else total + x
    return total


def own_frame(z, odd, sh):
    start, _ = places(z, odd)
    half = z.own // 2
    rows = pl.ds(pl.multiple_of(8 + start, 8), half)
    flat = jnp.concatenate(
        [
            jnp.concatenate(
                [sh[b, rows, h * 128 : h * 128 + 128] for b in range(NB)], axis=1
            )
            for h in range(2)
        ],
        axis=0,
    )
    return flat.astype(BF16)


def kernel_rows(flat):
    taps = CIN * KS * KS
    pad = jnp.zeros((1, 256 - NK % 128), F32)
    flat = jnp.concatenate([flat, pad], axis=1)
    lane = iota((1, 128), 1)
    row = iota((CCODE, 128), 0)
    rows = jnp.zeros((CCODE, 128), F32)
    for o in range(CCODE):
        chunk, shift = divmod(o * taps, 128)
        x = flat[:, chunk * 128 : chunk * 128 + 128]
        if shift:
            after = flat[:, chunk * 128 + 128 : chunk * 128 + 256]
            x = jnp.where(
                lane < 128 - shift,
                pltpu.roll(x, 128 - shift, 1),
                pltpu.roll(after, 128 - shift, 1),
            )
        rows = jnp.where(row == o, jnp.broadcast_to(x, (CCODE, 128)), rows)
    return rows


def spread_taps(kernel_pair):
    taps = CIN * KS * KS
    rows = jnp.concatenate([kernel_rows(x) for x in kernel_pair for _ in range(8)], axis=0)
    lane = iota((1, 128), 1)
    target, _ = tap_target(jnp.minimum(lane, taps - 1))
    slots = hot(iota((128, 128), 0) == jnp.where(lane < taps, target, -1))
    wide = dot(slots, rows.T.astype(BF16)).astype(BF16)
    halves = [wide[:, 0:128], wide[:, 128:256]]
    return jnp.concatenate([x for x in halves for _ in range(2)], axis=1)


def band_weights(wide_taps):
    wide_taps = wide_taps.astype(F32)
    row_u = iota((128, 256), 0) >> 3
    lane_u = iota((128, 256), 1) >> 4
    masks = [row_u == lane_u + shift for shift in (-1, 0, 1)]
    parts = []
    for k in range(KS):
        total = jnp.zeros((128, 256), F32)
        for i, mask in enumerate(masks):
            q = 3 * k + i
            piece = wide_taps[8 * q : 8 * q + 8]
            piece = jnp.broadcast_to(piece[None], (16, 8, 256)).reshape(128, 256)
            total = jnp.where(mask, piece, total)
        parts.append(total.astype(BF16))
    return jnp.concatenate(parts, axis=0)


def edge_kernel(
    z, fields, mask, cotangent, kernel, out, kernel_out,
    field_buf, mask_buf, cot_buf, kernel_buf, sems,
):
    odd = lax.rem(lax.axis_index("wide"), 2)
    first = lax.axis_index("section") * z.mb
    start = pl.multiple_of((1 - odd) * (z.band - 16), 16)
    copies = [
        pltpu.make_async_copy(
            source.at[pl.ds(first, z.mb), pl.ds(start, 16), :], buf, sems.at[i]
        )
        for i, (source, buf) in enumerate(
            ((fields, field_buf), (mask, mask_buf), (cotangent, cot_buf))
        )
    ]
    copies.append(pltpu.make_async_copy(kernel, kernel_buf, sems.at[3]))
    for copy in copies:
        copy.start()
    for copy in copies:
        copy.wait()
    kernel_row = kernel_buf[...].astype(F32)
    kernel_out[:, 0:NK] = jnp.broadcast_to(kernel_row, (COPIES, NK)).astype(BF16)
    kernel_out[:, NK:] = jnp.zeros((COPIES, PADDED - NK), BF16)

    def beside(buf):
        rows = buf[...].astype(F32)
        return jnp.where(odd == 1, rows[:, :HALO], rows[:, HALO:])

    def ordered(rows, firsts):
        return jnp.concatenate(
            [rows[:, j + h] for h in range(2) for j in firsts], axis=0
        ).astype(BF16)

    mask_rows = beside(mask_buf)
    allowed = jnp.concatenate([mask_rows] * CIN, axis=2)
    every, half = range(0, HALO, 2), range(0, HALO // 2, 2)
    near = beside(cot_buf) * allowed
    near = jnp.where(odd == 1, near[:, : HALO // 2], near[:, HALO // 2 :])
    pieces = ordered(beside(field_buf) * allowed, every), ordered(near, half)
    start = 0
    for piece in pieces:
        count = piece.shape[0]
        for c in range(CIN):
            out[start : start + count, :] = piece[:, c * HW : c * HW + HW]
            start += count
    out[start : z.sent, :] = ordered(mask_rows, every)[0 : z.near]


def prepare_kernel(
    z, fields, mask, counts, enc_bias, dec_bias, run_mean, run_cov,
    pixels_out, inmask_out, aux_out,
    count_buf, enc_buf, dec_buf, mean_buf, cov_buf, sems,
):
    section = lax.axis_index("section")
    wide = lax.axis_index("wide")
    first = section * z.mb
    mine_rows = pl.ds(first, z.mb)
    copies = [
        pltpu.make_async_copy(source, buf, sems.at[i])
        for i, (source, buf) in enumerate(
            (
                (counts, count_buf),
                (enc_bias, enc_buf),
                (dec_bias, dec_buf),
                (run_mean, mean_buf),
                (run_cov, cov_buf),
            )
        )
    ]
    for copy in copies:
        copy.start()
    gather = gather_rows(z)
    columns = window_columns()
    mask_columns = window_mask_columns()
    pixel_mask = mask[mine_rows].astype(F32).astype(BF16).reshape(z.own, HW)
    pixels = fields[mine_rows].reshape(z.own, z.span)
    framed = dot(gather, jnp.concatenate([pixel_mask, pixels], axis=1)).astype(BF16)
    in_mask = dot(framed[:, 0:HW], mask_columns)
    windowed = dot(framed[:, HW:], columns)
    for copy in copies:
        copy.wait()
    lane = iota((8, 128), 1)
    dec_row = jnp.zeros((8, 128), F32)
    for c in range(CIN):
        dec_row = jnp.where(((lane >> 1) & 3) == c, dec_buf[c], dec_row)
    enc_row = jnp.zeros((8, 128), F32)
    mean_row = jnp.zeros((8, 128), F32)
    for o in range(CCODE):
        enc_row = jnp.where((lane & 15) == o, enc_buf[o], enc_row)
        mean_row = jnp.where((lane & 15) == o, mean_buf[o], mean_row)
    aux_out[0:8] = dec_row
    aux_out[8:16] = enc_row
    aux_out[16:24] = mean_row
    aux_out[24:40] = jnp.zeros((16, 128), F32)
    aux_out[24:40, 0:CCODE] = cov_buf[...]
    field_now = wide * z.band // HW
    micro = iota((16, 128), 0) & (z.mb - 1)
    count = jnp.zeros((16, 128), jnp.int32)
    for m in range(z.mb):
        count = jnp.where(micro == m, count_buf[first + m, field_now], count)
    channel_ok = jnp.where(((iota((16, 128), 1) >> 1) & 3) < count, 1.0, 0.0)
    aux_out[40:56] = channel_ok
    in_mask = in_mask * jnp.tile(channel_ok, (z.own // 16, NB))
    inmask_out[...] = in_mask.astype(BF16)
    pixels_out[...] = (windowed * in_mask).astype(BF16)


def taps_kernel(z, kernel_own, kernel_other, weights_out):
    mine, other = (x[:, 0:NK].astype(F32)[0:1] for x in (kernel_own, kernel_other))
    leads = lax.axis_index("section") == 0
    weights_out[...] = spread_taps((jnp.where(leads, mine, other), jnp.where(leads, other, mine)))


def local_taps(sh, b, rows, step):
    up = sh[b, 16 - step : 16 - step + rows, :]
    here = sh[b, 16 : 16 + rows, :]
    down = sh[b, 16 + step : 16 + step + rows, 0:128]
    return jnp.concatenate([up, here, down], axis=1).astype(BF16)


def encode_rows(taps, banded, bias, masks, counted):
    code_mask = dot(masks, code_mask_lanes())
    pre = dot(taps, banded) + bias
    slope = jnp.exp(jnp.minimum(pre, 0.0))
    code = jnp.where(pre > 0, pre, slope - 1.0).astype(BF16).astype(F32)
    slope = jnp.where(code_mask > 0.5, slope, -slope)
    allowed, seen = counted(code_mask), counted(code)
    weighted = seen * allowed
    halves = [
        jnp.concatenate([x[:, 0:128], x[:, 128:256]], axis=0).astype(BF16) for x in (weighted, seen)
    ]
    second = dot(*halves, ((0,), (0,)))
    sums = [jnp.sum(x, axis=0, keepdims=True) for x in (weighted, allowed)]
    lane_u = iota((16, 128), 1) >> 4
    total = second[0:16]
    for u in range(1, UW // 2):
        total = jnp.where(lane_u == u, second[u * 16 : u * 16 + 16], total)
    total = fold(total, 16)
    diagonal = (iota((8, 128), 1) >> 4) == iota((8, 128), 0)
    pay = [
        jnp.sum(jnp.where(diagonal, total[h * 8 : h * 8 + 8], 0.0), axis=0, keepdims=True)
        for h in range(2)
    ]
    first, count = (
        fold(jnp.broadcast_to(x[:, :128] + x[:, 128:], (8, 128)), 16) for x in sums
    )
    lane = iota((8, 128), 1)
    inner, group = lane & 15, lane >> 4
    first = lanes_from(first, jnp.where(inner == 0, group, group + 8))
    spare = jnp.where(inner == 2, count, first)[0:1]
    pay[1] = jnp.where(inner[0:1] < 8, spare, pay[1])
    return code, slope, jnp.concatenate(pay, axis=0)


def inner_kernel(
    z, pixels, own_mask, weights, aux, taps_out, code_out, slope_out, pay_out, band_out, sh
):
    odd = lax.rem(lax.axis_index("wide"), 2)
    half = z.own // 2
    count = half - 16
    zeros = jnp.zeros((NB, 16, 256), F32)
    sh[:, 0:16, :] = zeros
    sh[:, half : half + 16, :] = zeros
    here = pl.ds(pl.multiple_of((1 - odd) * 16, 16), half)
    for b in range(NB):
        for h in range(2):
            sh[b, here, h * 128 : h * 128 + 128] = pixels[
                h * half : h * half + half, b * 128 : b * 128 + 128
            ].astype(F32)
    start = pl.multiple_of(odd * 32, 16)
    taps = [local_taps(sh, b, count, z.mb) for b in range(NB)]
    for b in range(NB):
        taps_out[b, pl.ds(start, count), :] = taps[b]
    kept = pl.ds(pl.multiple_of(odd * 16, 16), count)
    masks = jnp.concatenate([own_mask[kept, b * 128 : b * 128 + 128] for b in range(NB)], axis=0)
    bias = jnp.concatenate([aux[8:9], aux[8:9]], axis=1)
    banded = band_weights(weights[:, 0:256])
    band_out[...] = banded
    code, slope, pay = encode_rows(
        jnp.concatenate(taps, axis=0), banded, bias, masks, lambda x: x
    )
    pay_out[...] = pay
    for b in range(NB):
        rs = slice(b * count, b * count + count)
        code_out[b, pl.ds(start, count), :] = code[rs].astype(BF16)
        slope_out[b, pl.ds(start, count), :] = slope[rs]


def encode_kernel(
    z, pixels, own_mask, halo, banded, aux, inner_pay, taps_in, code_in, slope_in,
    taps_out, code_out, slope_out, pay_out,
    sh,
):
    odd = lax.rem(lax.axis_index("wide"), 2)
    half = z.own // 2
    count = 32
    channel_ok = jnp.tile(aux[40:56], (1, NB))
    middle, end = CIN * z.halo, CIN * (z.halo + z.near)
    halo_mask = dot(halo[end : z.sent, :], window_mask_columns())
    halo_rows = [halo[i : i + z.halo, :] for i in range(0, middle, z.halo)]
    halo_pixels = dot(jnp.concatenate(halo_rows, axis=1), window_columns())
    halo_x = halo_pixels * jnp.tile(channel_ok, (2, 1))
    zeros = jnp.zeros((NB, 16, 256), F32)
    sh[:, 0:16, :] = zeros
    sh[:, 48:64, :] = zeros
    own_start = pl.multiple_of((1 - odd) * (half - 32), 16)
    own_there = pl.ds(pl.multiple_of(odd * 32, 16), 32)
    halo_there = pl.ds(pl.multiple_of((2 - odd) * 16, 16), 16)
    for b in range(NB):
        for h in range(2):
            cs = slice(b * 128, b * 128 + 128)
            own = pixels[pl.ds(pl.multiple_of(own_start + h * half, 16), 32), cs]
            sh[b, own_there, h * 128 : h * 128 + 128] = own.astype(F32)
            sh[b, halo_there, h * 128 : h * 128 + 128] = halo_x[h * 16 : h * 16 + 16, cs]
    start = pl.multiple_of((1 - odd) * (z.rows - count), 16)
    taps = [local_taps(sh, b, count, z.mb) for b in range(NB)]
    for b in range(NB):
        taps_out[b, pl.ds(start, count), :] = taps[b]
    edge_mask = own_mask[pl.ds(pl.multiple_of((1 - odd) * (half - 16), 16), 16), :].astype(F32)
    first = jnp.where(odd == 1, halo_mask, edge_mask)
    later = jnp.where(odd == 1, edge_mask, halo_mask)
    masks = jnp.concatenate(
        [x[:, b * 128 : b * 128 + 128] for b in range(NB) for x in (first, later)], axis=0
    ).astype(BF16)
    bias = jnp.concatenate([aux[8:9], aux[8:9]], axis=1)

    def own_part(x):
        parts = [x[i * 16 : i * 16 + 16] for i in range(2 * NB)]
        return jnp.concatenate(
            [jnp.where(odd == 1, y, x) for x, y in zip(parts[::2], parts[1::2])], axis=0
        )

    code, slope, pay = encode_rows(
        jnp.concatenate(taps, axis=0), banded[...], bias, masks, own_part
    )
    pay = pay + inner_pay[...]
    pay_out[...] = pay
    for b in range(NB):
        rs = slice(b * count, b * count + count)
        code_out[b, pl.ds(start, count), :] = code[rs].astype(BF16)
        slope_out[b, pl.ds(start, count), :] = slope[rs]


def decode_kernel(
    z, cotangent, code, in_mask, halo, weights, aux,
    sent_out, pay_out,
    sh, cot_frame,
):
    odd = lax.rem(lax.axis_index("wide"), 2)
    mine = pl.ds(lax.axis_index("section") * z.mb, z.mb)
    rows = z.rows
    put_frame(z, sh, mend_coarse([code[b].astype(F32) for b in range(NB)]))
    banded = band_weights(weights[:, 256:512])
    raws = spread(z, sh, banded)
    gather = gather_rows(z)
    columns = window_columns()
    own_cot = dot(gather, cotangent[mine].reshape(z.own, z.span)).astype(BF16)
    near = [
        halo[i : i + z.near, :] for i in range(CIN * z.halo, CIN * (z.halo + z.near), z.near)
    ]
    cots = dot(jnp.concatenate([own_cot, jnp.concatenate(near, axis=1)], axis=0), columns)
    near = cots[z.own : z.own + z.near] * jnp.tile(aux[40:56], (1, NB))
    nothing = jnp.zeros((8, NB * 128), F32)
    beside = []
    for h in range(2):
        part = near[h * 8 : h * 8 + 8]
        beside += [jnp.where(odd == 1, nothing, part), jnp.where(odd == 1, part, nothing)]
    own_cot = cots[0 : z.own] * in_mask[...].astype(F32)
    put_pixels(z, cot_frame, odd, own_cot, jnp.concatenate(beside, axis=0))
    mine_rows = own_rows(z, odd)
    u_local = (iota((1, 128), 1) >> 3) & (UW - 1)
    inner = mine_rows & (u_local >= 1) & (u_local <= UW - 2)
    grads = []
    bias_sum = jnp.zeros((1, 128), F32)
    for h in range(2):
        raw = raws[h] + aux[0:1]
        slope = jnp.exp(jnp.minimum(raw, 0.0))
        cs = slice(h * 128, h * 128 + 128)
        for b in range(NB):
            rs = slice(b * rows, b * rows + rows)
            grad = (cot_frame[b, 8 : 8 + rows, cs] * slope[rs]).astype(BF16).astype(F32)
            bias_sum = bias_sum + jnp.sum(jnp.where(inner, grad, 0.0), axis=0, keepdims=True)
            grads.append(grad)
    put_frame(z, sh, mend_fine([(grads[b], grads[NB + b]) for b in range(NB)]))
    taps = jnp.concatenate([fine_taps(z, sh, b) for b in range(NB)], axis=0)
    sent_out[...] = dot(taps, banded).astype(BF16).reshape(NB, rows, 256)
    last = HW // 2 - (NB - 1) * (UW - 2)
    within = mine_rows & ((iota((1, 256), 1) >> 4) <= last)
    mine = jnp.concatenate(
        [
            jnp.where(within if b == NB - 1 else mine_rows, code[b].astype(F32), 0.0).astype(BF16)
            for b in range(NB)
        ],
        axis=0,
    )
    pay = pick_taps(dot(mine, taps, ((0,), (0,))))
    bias_sum = fold(jnp.broadcast_to(bias_sum, (16, 128)), 8)
    lane = iota((16, 128), 1)
    keep = (lane < 8) & ((lane >> 1) == iota((16, 128), 0))
    column = jnp.sum(jnp.where(keep, bias_sum, 0.0), axis=1, keepdims=True)
    pay_out[...] = jnp.where(lane >= 120, column, pay)


def whiten_kernel(
    z, stats, code, slope, sent, taps, decode_pay, aux,
    grad_out, pay_out, moments_out,
):
    odd = lax.rem(lax.axis_index("wide"), 2)
    rows = z.rows
    pay = jnp.sum(stats[...], axis=0)
    lane = iota((8, 128), 1)
    inner, step = lane & 15, iota((8, 128), 0)
    low, high = (jnp.broadcast_to(pay[h : h + 1], (8, 128)) for h in range(2))
    count = lanes_from(high, jnp.full((8, 128), 2, jnp.int32))[0:1]
    first = lanes_from(high, jnp.where(inner < 8, 16 * inner, 16 * (inner - 8) + 1))[0:1]
    mean = first / count
    columns = jnp.concatenate([lanes_from(high, 16 * step + h) for h in range(2)], axis=0)
    diagonal = (lane >> 4) == step
    mirrored = lanes_from(low, jnp.where(inner < 8, 16 * inner + 8 + step, 0))
    low, high = (fold(jnp.where(diagonal, x, 0.0), 16) for x in (low, high))
    second = jnp.concatenate([low, jnp.where(inner < 8, mirrored, high)], axis=0)
    lane = iota((16, 128), 1)
    row = iota((16, 128), 0)
    wide_mean = jnp.broadcast_to(mean, (16, 128))
    total = jnp.broadcast_to(count, (16, 128))
    mean_column = columns / total
    cov = second / total - mean_column * wide_mean
    moments_out[0:CCODE] = cov
    moments_out[CCODE:] = jnp.broadcast_to(mean, (8, 128))
    offset = cov - jnp.where((lane & 15) == row, 1.0, 0.0)
    pulled = jnp.sum(offset * mean_column, axis=0, keepdims=True)
    linear = whiten_weight * mean - 2.0 * whiten_weight * pulled
    linear = jnp.concatenate([linear, linear], axis=1)
    matrix = jnp.tile(2.0 * whiten_weight * offset, (8, 1))
    matrix = jnp.where((iota((128, 128), 0) >> 4) == (iota((128, 128), 1) >> 4), matrix, 0.0)
    high = matrix.astype(BF16)
    matrix = jnp.concatenate([high, (matrix - high.astype(F32)).astype(BF16)], axis=0)
    flat = code[...].reshape(z.frame, 256)
    flat = jnp.concatenate(
        [jnp.concatenate([x, x], axis=1) for x in (flat[:, 0:128], flat[:, 128:256])], axis=0
    )
    turned = dot(flat, matrix)
    turned = jnp.concatenate([turned[0 : z.frame], turned[z.frame :]], axis=1) + linear
    mine_rows = own_rows(z, odd)
    lane_u = iota((1, 256), 1) >> 4
    inner = mine_rows & (lane_u >= 1) & (lane_u <= UW - 2)
    last = HW // 2 - (NB - 1) * (UW - 2)
    blocks, mine = [], []
    bias_sum = jnp.zeros((1, 256), F32)
    for b in range(NB):
        signed = slope[b]
        pull = jnp.where(signed > 0, turned[b * rows : b * rows + rows], 0.0)
        grad = ((sent[b].astype(F32) + pull) * jnp.abs(signed)).astype(BF16).astype(F32)
        kept = jnp.where(inner & (lane_u <= last) if b == NB - 1 else inner, grad, 0.0)
        bias_sum = bias_sum + jnp.sum(kept, axis=0, keepdims=True)
        blocks.append(grad)
        mine.append(kept.astype(BF16))
    products = dot(
        jnp.concatenate(mine, axis=0), taps[...].reshape(z.frame, KS * 128), ((0,), (0,))
    )
    encode_pay = pick_taps(products)
    bias_sum = fold(jnp.broadcast_to(bias_sum[:, :128] + bias_sum[:, 128:], (16, 128)), 16)
    column = jnp.sum(jnp.where(lane == row, bias_sum, 0.0), axis=1, keepdims=True)
    decoded = decode_pay[...]
    biases = jnp.where((lane & 1) == 0, column, decoded)
    coarse = biases.astype(BF16).astype(F32)
    biases = jnp.where((lane & 2) == 0, coarse, biases - coarse)
    encode_pay = jnp.where(lane >= 120, biases, encode_pay)
    decoded = jnp.where(lane >= 120, biases, decoded)
    pay_out[0] = encode_pay.astype(BF16)
    pay_out[1] = decoded.astype(BF16)
    for b, (low, high) in enumerate(mend_coarse(blocks)):
        grad_out[b, :, 0:128] = low.astype(BF16)
        grad_out[b, :, 128:256] = high.astype(BF16)


def picture(z, decodes, grad, code, in_mask, weights, aux, sh):
    odd = lax.rem(lax.axis_index("wide"), 2)
    rows = z.rows
    frames = [
        jnp.where(decodes, code[b].astype(F32), grad[b].astype(F32)) for b in range(NB)
    ]
    put_frame(z, sh, mend_coarse(frames))
    chosen = jnp.where(decodes, weights[:, 256:512].astype(F32), weights[:, 0:256].astype(F32))
    raws = spread(z, sh, band_weights(chosen))
    for h in range(2):
        raw = raws[h] + aux[0:1]
        raw = jnp.where(raw > 0, raw, jnp.exp(jnp.minimum(raw, 0.0)) - 1.0)
        raw = jnp.where(decodes, raw, raws[h])
        for b in range(NB):
            sh[b, 8 : 8 + rows, h * 128 : h * 128 + 128] = raw[b * rows : b * rows + rows]
    flat = own_frame(z, odd, sh) * in_mask[...]
    native = dot(flat, unwindow_columns()).astype(BF16)
    return dot(scatter_rows(z), native).astype(BF16).reshape(z.mb, z.band, z.span)


def send_kernel(z, grad, code, in_mask, weights, aux, send_out, sh):
    decodes = lax.axis_index("section") == 0
    send_out[...] = picture(z, decodes, grad, code, in_mask, weights, aux, sh)


def keep_kernel(
    z, grad, code, in_mask, weights, aux, moments,
    pixels_out, mean_out, cov_out,
    sh, mine, means, covs, sems,
):
    section = lax.axis_index("section")
    means[...] = decay_rate * aux[16:17, 0:CCODE] + (1.0 - decay_rate) * moments[16:17, 0:CCODE]
    covs[...] = decay_rate * aux[24:40, 0:CCODE] + (1.0 - decay_rate) * moments[0:16, 0:CCODE]
    mine[...] = picture(z, section == 1, grad, code, in_mask, weights, aux, sh)
    copies = [
        pltpu.make_async_copy(source, target, sems.at[i])
        for i, (source, target) in enumerate(
            (
                (mine, pixels_out.at[0, pl.ds(section * z.mb, z.mb)]),
                (means, mean_out),
                (covs, cov_out),
            )
        )
    ]
    for copy in copies:
        copy.start()
    for copy in copies:
        copy.wait()


def total_kernel(z, parts, out):
    out[...] = jnp.sum(parts[...].astype(F32), axis=0)


def finish_kernel(
    z, sums, arrived, half_done, pixels_out, kernel_out, enc_out, dec_out,
    kernels, encs, decs, sems,
):
    there = z.micro - z.mb - lax.axis_index("section") * z.mb
    copies = [
        pltpu.make_async_copy(source, target, sems.at[i])
        for i, (source, target) in enumerate(
            (
                (arrived, pixels_out.at[0, pl.ds(there, z.mb)]),
                (encs, enc_out),
                (decs, dec_out),
                (kernels, kernel_out),
            )
        )
    ]
    copies[0].start()
    total = sums[...]
    taps = CIN * KS * KS
    tap = (iota((CCODE, 128), 1) - taps * iota((CCODE, 128), 0)) & 127
    slot, _ = tap_target(jnp.minimum(tap, taps - 1))
    moved = lanes_from(total, slot)
    place = iota((1, 128), 1)
    for chunk in range((NK + 127) // 128):
        out = jnp.zeros((1, 128), F32)
        for o in range(CCODE):
            start = o * taps - chunk * 128
            if -taps < start < 128:
                out = jnp.where((place >= start) & (place < start + taps), moved[o : o + 1], out)
        width = min(128, NK - chunk * 128)
        kernels[:, chunk * 128 : chunk * 128 + width] = out[:, 0:width]
    copies[3].start()
    lane = iota((16, 128), 1)
    row = iota((16, 128), 0)
    for slot, out in ((120, encs), (121, decs)):
        chosen = (lane == slot) | (lane == slot + 2)
        column = jnp.sum(jnp.where(chosen, total, 0.0), axis=1, keepdims=True)
        flat = jnp.sum(jnp.where(lane == row, column, 0.0), axis=0, keepdims=True)
        out[...] = flat[:, 0 : out.shape[1]]
    copies[1].start()
    copies[2].start()
    for copy in copies:
        copy.wait()


VMEM = pl.BlockSpec(memory_space=pltpu.VMEM)
HBM = pl.BlockSpec(memory_space=pltpu.HBM)
PARAMS = pltpu.CompilerParams(vmem_limit_bytes=24 * 1024 * 1024)
DMA = pltpu.SemaphoreType.DMA


def shape(*dims, dtype=BF16):
    return jax.ShapeDtypeStruct(dims, dtype)


def shards(sections, wides):
    def run(
        fields, pixel_mask, channel_counts, kernels, enc_bias, dec_bias, cotangent, run_mean, run_cov
    ):
        z = Sizes(fields.shape, sections)
        assert 2 * z.band == HW and z.span == CIN * HW and z.mb == 4
        whole = (fields, pixel_mask, cotangent)
        (
            fields, cotangent, pixel_mask, kernels, channel_counts, enc_bias, dec_bias,
            run_mean, run_cov,
        ) = (
            pltpu.with_memory_space_constraint(x, pltpu.HBM)
            for x in (
                fields, cotangent, pixel_mask, kernels, channel_counts, enc_bias, dec_bias,
                run_mean, run_cov,
            )
        )
        swap = [(i, i ^ 1) for i in range(sections)]
        pair = [(i, i ^ 1) for i in range(wides)]
        frame = (NB, z.rows, 256)
        framed = pltpu.VMEM((NB, z.rows + 16, 256), F32)
        band_buf = pltpu.VMEM((z.mb, z.band, z.span), BF16)
        edge_buf = pltpu.VMEM((z.mb, 16, z.span), BF16)
        heavy = pl.CostEstimate(flops=4_000_000_000, bytes_accessed=4_000_000, transcendentals=0)

        def call(kernel, name, outs, ins, scratch, out_specs=None, cost=None, alias=None):
            return pl.pallas_call(
                lambda *refs: kernel(z, *refs),
                out_shape=outs,
                in_specs=ins,
                out_specs=out_specs or [VMEM] * len(outs),
                scratch_shapes=scratch,
                compiler_params=PARAMS,
                cost_estimate=cost,
                input_output_aliases=alias or {},
                name=name,
            )

        halo, kernel_own = call(
            edge_kernel,
            "edge",
            [shape(z.sent, HW), shape(COPIES, PADDED)],
            [HBM] * 4,
            [
                edge_buf,
                pltpu.VMEM((z.mb, 16, HW), jnp.int32),
                edge_buf,
                pltpu.VMEM((1, NK), BF16),
                DMA((4,)),
            ],
        )(fields, pixel_mask, cotangent, kernels)
        halo = lax.ppermute(halo, "wide", pair)
        kernel_other = lax.ppermute(kernel_own, "section", swap)
        pixels, in_mask, aux = call(
            prepare_kernel,
            "prepare",
            [
                shape(z.own, NB * 128),
                shape(z.own, NB * 128),
                shape(56, 128, dtype=F32),
            ],
            [VMEM] * 2 + [HBM] * 5,
            [
                pltpu.SMEM(channel_counts.shape, jnp.int32),
                pltpu.SMEM(enc_bias.shape, F32),
                pltpu.SMEM(dec_bias.shape, F32),
                pltpu.SMEM(run_mean.shape, F32),
                pltpu.VMEM(run_cov.shape, F32),
                DMA((5,)),
            ],
            cost=heavy,
        )(*whole[:2], channel_counts, enc_bias, dec_bias, run_mean, run_cov)
        (weights,) = call(taps_kernel, "taps", [shape(128, 512)], [VMEM] * 2, [])(
            kernel_own, kernel_other
        )
        coded = [shape(NB, z.rows, KS * 128), shape(*frame), shape(*frame, dtype=F32)]
        taps, code, slope, pay, banded = call(
            inner_kernel,
            "inner",
            coded + [shape(2, 128, dtype=F32), shape(KS * 128, 256)],
            [VMEM] * 4,
            [pltpu.VMEM((NB, z.own // 2 + 16, 256), F32)],
            cost=heavy,
        )(pixels, in_mask, weights, aux)
        taps, code, slope, pay = call(
            encode_kernel,
            "encode",
            coded + [shape(2, 128, dtype=F32)],
            [VMEM] * 9,
            [pltpu.VMEM((NB, 64, 256), F32)],
            alias={6: 0, 7: 1, 8: 2},
        )(pixels, in_mask, halo, banded, aux, pay, taps, code, slope)
        pay = jnp.broadcast_to(pay[None], (sections * wides, 2, 128))
        stats = lax.all_to_all(pay, ("section", "wide"), 0, 0)
        sent, decode_pay = call(
            decode_kernel,
            "decode",
            [shape(*frame), shape(CCODE, 128, dtype=F32)],
            [VMEM] * 6,
            [framed, framed],
            cost=heavy,
        )(whole[2], code, in_mask, halo, weights, aux)
        grad, pay, moments = call(
            whiten_kernel,
            "whiten",
            [
                shape(*frame),
                shape(sections, CCODE, 128),
                shape(CCODE + 8, 128, dtype=F32),
            ],
            [VMEM] * 7,
            [],
            alias={3: 0},
        )(stats, code, slope, sent, taps, decode_pay, aux)
        pay = jnp.broadcast_to(pay[:, None], (sections, wides, CCODE, 128))
        pay = pay.reshape(sections * wides, CCODE, 128)
        parts = lax.all_to_all(pay, ("section", "wide"), 0, 0)
        (sending,) = call(
            send_kernel,
            "send",
            [shape(z.mb, z.band, z.span)],
            [VMEM] * 5,
            [framed],
            cost=heavy,
        )(grad, code, in_mask, weights, aux)
        arrived = lax.ppermute(sending, "section", swap)
        half_done, new_mean, new_cov = call(
            keep_kernel,
            "keep",
            [
                shape(1, z.micro, z.band, z.span),
                shape(1, CCODE, dtype=F32),
                shape(CCODE, CCODE, dtype=F32),
            ],
            [VMEM] * 6,
            [
                framed,
                band_buf,
                pltpu.VMEM((1, CCODE), F32),
                pltpu.VMEM((CCODE, CCODE), F32),
                DMA((3,)),
            ],
            out_specs=[HBM] * 3,
            cost=heavy,
        )(grad, code, in_mask, weights, aux, moments)
        (sums,) = call(
            total_kernel,
            "total",
            [shape(CCODE, 128, dtype=F32)],
            [VMEM],
            [],
            cost=pl.CostEstimate(flops=100_000_000_000, bytes_accessed=0, transcendentals=0),
        )(parts)
        pixels_out, kernel_grads, enc_grad, dec_grad = call(
            finish_kernel,
            "finish",
            [
                shape(1, z.micro, z.band, z.span),
                shape(1, NK, dtype=F32),
                shape(1, CCODE, dtype=F32),
                shape(1, CIN, dtype=F32),
            ],
            [VMEM] * 2 + [HBM],
            [
                pltpu.VMEM((1, NK), F32),
                pltpu.VMEM((1, CCODE), F32),
                pltpu.VMEM((1, CIN), F32),
                DMA((4,)),
            ],
            out_specs=[HBM] * 4,
            alias={2: 0},
        )(sums, arrived, half_done)
        return (
            pixels_out,
            kernel_grads,
            enc_grad.reshape(CCODE),
            dec_grad.reshape(CIN),
            new_mean.reshape(CCODE),
            new_cov,
        )

    return run


def solution(mesh):
    in_specs = (
        P(None, "wide", None),
        P(None, "wide", None),
        P(),
        P("section", None),
        P(),
        P(),
        P(None, "wide", None),
        P(),
        P(),
    )
    out_specs = (P("section", None, "wide", None), P("section", None), P(), P(), P(), P())
    run = shards(mesh.shape["section"], mesh.shape["wide"])
    return jax.shard_map(run, mesh=mesh, in_specs=in_specs, out_specs=out_specs, check_vma=False)
```
